128 devices in a mesh: ctx: 16 (over z, y_lo, core), ch: 8 (over x, y_hi).
Axes of the slice: x: 4, y: 4 (y_hi: 2, y_lo: 2; y = y_hi * 2 + y_lo), z: 4, core: 2. Of those that a mesh axis runs over, the one named last changes fastest.
Arguments:
- gate_in: bfloat16 [4096, 8192], P('ctx', 'ch'), may hold values from -6 to 6
- key_in: bfloat16 [4096, 8192], P('ctx', 'ch'), may hold values from -6 to 6
- value_in: bfloat16 [4096, 8192], P('ctx', 'ch'), may hold values from -6 to 6
- cotangent: bfloat16 [4096, 8192], P('ctx', 'ch'), may hold values from -6 to 6
- skip: float32 [8192], P('ch'), may hold values from 0.5 to 1.5
- residue: float32 [1024, 16], P('ch'), may hold values from -2 to 2
- decay: float32 [1024, 16], P('ch'), may hold values from 0.00024414062 to 0.05
Outputs:
- mixed: bfloat16 [4096, 8192], P('ctx', 'ch')
- grad_gate: bfloat16 [4096, 8192], P('ctx', 'ch')
- grad_key: bfloat16 [4096, 8192], P('ctx', 'ch')
- grad_value: bfloat16 [4096, 8192], P('ctx', 'ch')
- grad_skip: float32 [8192], P('ch')
- grad_residue: float32 [1024, 16], P('ch')
- grad_log_decay: float32 [1024, 16], P('ch')
The draws below stay inside these ranges and needn't reach their ends.
All inputs are finite; a program needn't handle non-finite values.
Results may differ from the reference program's by a relative error of at most 0.0012.
Values sent between devices are 32-bit elements; how exact they have to be, the bound alone decides.
No kernel may reach another device: no remote copies, remote signals or barrier semaphores. Data moves between devices by JAX's collectives and lax.ppermute only.
A program may use at most 128 MiB of HBM per device.

```python
import math
import jax
import jax.numpy as jnp
from jax import lax

D = 8192
FILTERS = 1024
MODES = 16
TOKENS = 4096


def levels(key, extent, cuts, least, largest):
    def one(position, parts):
        draws = jax.random.uniform(jax.random.fold_in(jax.random.fold_in(key, 6), position), (parts,), jnp.float32, least / len(cuts), largest / len(cuts))
        return jnp.repeat(jnp.exp(draws), extent[position] // parts).reshape((-1,) + (1,) * (len(extent) - position - 1))

    level = one(*cuts[0])
    for cut in cuts[1:]:
        level = level * one(*cut)
    return level


def bell_draw(key, extent, deviation, bound, split=(), held_as=jnp.bfloat16):
    level = levels(key, extent, split, -0.22, 0.18) if split else 1.0
    values = jax.random.normal(key, extent, jnp.float32) * deviation * level
    return jnp.minimum(jnp.maximum(values, -bound), bound).astype(held_as)


def setup_inputs(seed: int = 0) -> dict:
    key_of = jax.random.split(jax.random.key(seed), 8)
    return {
        "gate_in": bell_draw(key_of[0], (TOKENS, D), 1.0, 6.0, ((0, 16), (1, 8))),
        "key_in": bell_draw(key_of[1], (TOKENS, D), 1.0, 6.0, ((0, 16), (1, 8))),
        "value_in": bell_draw(key_of[2], (TOKENS, D), 1.0, 6.0, ((0, 16), (1, 8))),
        "cotangent": bell_draw(key_of[3], (TOKENS, D), 1.0, 6.0, ((0, 16), (1, 8))),
        "skip": jnp.clip(0.5 + 1.0 * jax.random.uniform(key_of[4], (D,), jnp.float32) ** levels(key_of[4], (D,), ((0, 8),), -0.2, 0.2), 0.5, 1.5),
        "residue": bell_draw(key_of[5], (FILTERS, MODES), 0.35, 2.0, ((0, 8),), jnp.float32),
        "decay": jnp.clip(jnp.exp(math.log(0.05) - 5.322034 * jax.random.uniform(key_of[6], (FILTERS, MODES), jnp.float32) ** levels(key_of[6], (FILTERS, MODES), ((0, 8),), -0.2, 0.2)), 0.00024414062, 0.05),
    }


def impulse(residue, decay):
    times = jnp.arange(TOKENS).astype(jnp.float32)[:, None]
    total = jnp.zeros((TOKENS, residue.shape[0]), jnp.float32)
    for mode in range(residue.shape[1]):
        rate = decay[:, mode][None, :]
        total = total + residue[:, mode][None, :] * jnp.sqrt(rate) * jnp.exp(-rate * times)
    return total

def reference(gate_in, key_in, value_in, cotangent, skip, residue, decay):
    length = 2 * TOKENS
    kernel = impulse(residue, decay)
    kernel_spec = jnp.fft.rfft(kernel, n=length, axis=0)
    blocks = D // FILTERS

    def split_blocks(array):
        return jnp.moveaxis(array.reshape(TOKENS, blocks, FILTERS), 1, 0)
    inputs = (split_blocks(gate_in), split_blocks(key_in), split_blocks(value_in), split_blocks(cotangent), skip.reshape(blocks, FILTERS))

    def one_block(carry, item):
        gate_value, key_value, value_value, cot_value, skip_block = item
        gate_value = gate_value.astype(jnp.float32)
        key_value = key_value.astype(jnp.float32)
        value_value = value_value.astype(jnp.float32)
        cot_value = cot_value.astype(jnp.float32)
        product = key_value * value_value
        product_spec = jnp.fft.rfft(product, n=length, axis=0)
        conv = jnp.fft.irfft(product_spec * kernel_spec, n=length, axis=0)[:TOKENS]
        pre_gate = conv + skip_block[None, :] * product
        mixed = (gate_value * pre_gate).astype(jnp.bfloat16)
        grad_gate = (cot_value * pre_gate).astype(jnp.bfloat16)
        back = cot_value * gate_value
        back_spec = jnp.fft.rfft(back, n=length, axis=0)
        grad_product = jnp.fft.irfft(jnp.conj(kernel_spec) * back_spec, n=length, axis=0)[:TOKENS]
        grad_product = grad_product + skip_block[None, :] * back
        grad_key = (grad_product * value_value).astype(jnp.bfloat16)
        grad_value = (grad_product * key_value).astype(jnp.bfloat16)
        grad_skip = lax.optimization_barrier(jnp.sum(back * product, axis=0))
        carry = carry + jnp.conj(product_spec) * back_spec
        return (carry, (mixed, grad_gate, grad_key, grad_value, grad_skip))
    total_spec, results = lax.scan(one_block, jnp.zeros_like(kernel_spec), inputs)

    def merge_blocks(array):
        return jnp.moveaxis(array, 0, 1).reshape(TOKENS, D)
    grad_kernel = jnp.fft.irfft(total_spec, n=length, axis=0)[:TOKENS]
    _, pullback = jax.vjp(impulse, residue, decay)
    grad_residue, grad_decay = pullback(grad_kernel)
    return (merge_blocks(results[0]), merge_blocks(results[1]), merge_blocks(results[2]), merge_blocks(results[3]), results[4].reshape(D), grad_residue, decay * grad_decay)
```

```python
import functools

import jax
import jax.numpy as jnp
import numpy as np
from jax import lax
from jax.experimental import pallas as pl
from jax.experimental.pallas import tpu as pltpu
from jax.sharding import PartitionSpec as P

LANES = 128
ROWS = 8
VMEM = pl.BlockSpec(memory_space=pltpu.VMEM)
SMEM = pl.BlockSpec(memory_space=pltpu.SMEM)


def call(body, outs, limit_mib, cost, scratch=()):
    flops, moved = cost
    return lambda specs, *args: pl.pallas_call(
        body,
        out_shape=[jax.ShapeDtypeStruct(s, t) for s, t in outs],
        in_specs=list(specs),
        out_specs=[VMEM] * len(outs),
        scratch_shapes=list(scratch),
        compiler_params=pltpu.CompilerParams(vmem_limit_bytes=limit_mib * 2**20),
        cost_estimate=pl.CostEstimate(flops=flops, bytes_accessed=moved, transcendentals=0),
    )(*args)


def halves(table):
    high = table.astype(jnp.bfloat16)
    low = (table - high.astype(np.float64)).astype(jnp.bfloat16)
    return np.concatenate([high, high, low], axis=1)


def transform_tables(length):
    full = 2 * length
    wave = np.arange(length)[:, None]
    time = np.arange(length)[None, :]
    angle = 2.0 * np.pi * ((wave * time) % full) / full
    real, imag = np.cos(angle), -np.sin(angle)
    imag[0] = np.where(np.arange(length) % 2 == 0, 1.0, -1.0)
    weight = np.where(wave == 0, 1.0, 2.0) / full
    forward = np.concatenate([real, imag], axis=0)
    inverse = np.concatenate([weight * real, weight * imag], axis=0).T
    return halves(forward), halves(inverse)


def split_dot(table, signal):
    high = signal.astype(jnp.bfloat16)
    low = (signal - high.astype(jnp.float32)).astype(jnp.bfloat16)
    return jnp.dot(table, jnp.concatenate([high, low, high], axis=0), preferred_element_type=jnp.float32)


def row_iota(shape):
    return lax.broadcasted_iota(jnp.int32, shape, 0)


def spectral_product(left, right, conjugate):
    count = left.shape[0] // 2
    lre, lim, rre, rim = left[:count], left[count:], right[:count], right[count:]
    first = row_iota(lre.shape) == 0
    both = lim * rim
    cross = jnp.where(first, 0.0, both)
    if conjugate:
        real, imag = lre * rre + cross, lre * rim - lim * rre
    else:
        real, imag = lre * rre - cross, lre * rim + lim * rre
    return jnp.concatenate([real, jnp.where(first, both, imag)], axis=0)


def spread_body(decay_ref, residue_ref, out_ref):
    modes = decay_ref.shape[0]
    for block in range(out_ref.shape[0]):
        out_ref[block, :modes] = decay_ref[...]
        out_ref[block, modes:] = residue_ref[...]


def product_body(gate_ref, key_ref, value_ref, cot_ref, fwd_ref, inv_ref, x_ref, b_ref, xs_ref, bs_ref, gk_ref, sk_ref):
    width = 2 * LANES

    def step(block, carry):
        lanes = pl.ds(pl.multiple_of(block * width, width), width)
        x = key_ref[:, lanes].astype(jnp.float32) * value_ref[:, lanes].astype(jnp.float32)
        b = cot_ref[:, lanes].astype(jnp.float32) * gate_ref[:, lanes].astype(jnp.float32)
        x_ref[:, lanes] = x
        b_ref[:, lanes] = b
        total = jnp.sum(x * b, axis=0, keepdims=True)
        sk_ref[pl.ds(2 * block, 1), :] = total[:, :LANES]
        sk_ref[pl.ds(2 * block + 1, 1), :] = total[:, LANES:]
        xs = split_dot(fwd_ref[...], x)
        bs = split_dot(fwd_ref[...], b)
        xs_ref[:, lanes] = xs
        bs_ref[:, lanes] = bs
        gk_ref[:, lanes] = split_dot(inv_ref[...], spectral_product(xs, bs, True))
        return carry

    lax.fori_loop(0, x_ref.shape[1] // width, step, 0)


def moments(decay, upward, downward):
    modes = decay.shape[0]
    rates = [jnp.broadcast_to(decay[m : m + 1], (ROWS, LANES)) for m in range(modes)]
    step8 = [jnp.exp(-float(ROWS) * rate) for rate in rates]
    tiles = upward[0][1] if upward else downward[0][1]
    ups = [[None] * modes for _ in upward]
    downs = [[None] * modes for _ in downward]
    for tile in range(tiles):
        for sums, (fetch, _), place in [(s, f, tile) for s, f in zip(ups, upward)] + [
            (s, f, tiles - 1 - tile) for s, f in zip(downs, downward)
        ]:
            value = fetch(place)
            for m in range(modes):
                sums[m] = value if sums[m] is None else step8[m] * sums[m] + value
    phase = row_iota((ROWS, LANES)).astype(jnp.float32)
    up_weight = [jnp.exp(-rate * (ROWS - 1.0 - phase)) for rate in rates] if upward else []
    down_weight = [jnp.exp(-rate * phase) for rate in rates] if downward else []

    def gather(sums, weights):
        rows = [jnp.sum(s * w, axis=0, keepdims=True) for s, w in zip(sums, weights)]
        return jnp.concatenate(rows, axis=0)

    return [gather(s, up_weight) for s in ups], [gather(s, down_weight) for s in downs]


def turn_out(scratch_ref, out_ref, slot):
    owners = out_ref.shape[0]
    for group in range(scratch_ref.shape[0] // LANES):
        turned = scratch_ref[pl.ds(group * LANES, LANES), :].T
        out_ref[:, slot + group] = turned.reshape(owners, LANES // owners, LANES)


def state_body(par_ref, x_ref, b_ref, sk_ref, out_ref, rate_ref, sums_ref, rates_ref):
    blocks, modes = par_ref.shape[0], par_ref.shape[1] // 2
    tiles = x_ref.shape[0] // ROWS

    def step(block, carry):
        lanes = pl.ds(pl.multiple_of(block * LANES, LANES), LANES)
        decay = par_ref[block, :modes, :]
        (up,), (down,) = moments(
            decay,
            [(lambda tile: x_ref[pl.ds(tile * ROWS, ROWS), lanes], tiles)],
            [(lambda tile: b_ref[pl.ds(tile * ROWS, ROWS), lanes], tiles)],
        )
        start = pl.multiple_of(block * 2 * modes, 2 * modes)
        sums_ref[pl.ds(start, 2 * modes), :] = jnp.concatenate([up, down], axis=0)
        rates_ref[pl.ds(start, 2 * modes), :] = jnp.concatenate([decay, decay], axis=0)
        return carry

    lax.fori_loop(0, blocks, step, 0)
    turn_out(sums_ref, out_ref, 0)
    groups = sums_ref.shape[0] // LANES
    for owner in range(out_ref.shape[0]):
        out_ref[owner, groups, :blocks] = sk_ref[...]
    for group in range(groups):
        rate_ref[group] = rates_ref[pl.ds(group * LANES, LANES), :].T


def slope_body(par_ref, x_ref, b_ref, gk_ref, qa_ref, qb_ref, suma_ref, sumb_ref):
    blocks, modes = par_ref.shape[0], par_ref.shape[1] // 2
    positions = x_ref.shape[0]
    tiles = positions // ROWS
    half = modes // 2

    def step(block, carry):
        lanes = pl.ds(pl.multiple_of(block * LANES, LANES), LANES)
        phase = row_iota((ROWS, LANES)).astype(jnp.float32)

        def late(tile):
            return (positions - 1.0 - tile * ROWS - phase) * x_ref[pl.ds(tile * ROWS, ROWS), lanes]

        def early(ref):
            return lambda tile: (tile * float(ROWS) + phase) * ref[pl.ds(tile * ROWS, ROWS), lanes]

        for part in range(2):
            decay = par_ref[block, part * half : (part + 1) * half, :]
            (up,), (down, plain, slope) = moments(
                decay,
                [(late, tiles)],
                [
                    (early(b_ref), tiles),
                    (lambda tile: gk_ref[pl.ds(tile * ROWS, ROWS), lanes], tiles),
                    (early(gk_ref), tiles),
                ],
            )
            start = pl.multiple_of(block * 2 * modes, 2 * modes) + part * half
            suma_ref[pl.ds(start, half), :] = down
            suma_ref[pl.ds(start + modes, half), :] = up
            sumb_ref[pl.ds(start, half), :] = plain
            sumb_ref[pl.ds(start + modes, half), :] = slope
        return carry

    lax.fori_loop(0, blocks, step, 0)
    turn_out(suma_ref, qa_ref, 0)
    turn_out(sumb_ref, qb_ref, 0)


def tree(values):
    while len(values) > 1:
        values = [a + b for a, b in zip(values[::2], values[1::2])]
    return values[0]


def local_body(par_ref, skip_ref, x_ref, b_ref, xs_ref, bs_ref, fwd_ref, inv_ref, pre_ref, gp_ref, k_ref):
    modes = par_ref.shape[1] // 2
    width = 2 * LANES
    tiles = x_ref.shape[0] // ROWS

    def step(pair, carry):
        phase = row_iota((ROWS, LANES)).astype(jnp.float32)
        for side in range(2):
            block = 2 * pair + side
            decay, residue = par_ref[block, :modes, :], par_ref[block, modes:, :]
            weight = residue * jnp.sqrt(decay)
            rates = [jnp.broadcast_to(decay[m : m + 1], (ROWS, LANES)) for m in range(modes)]
            step8 = [jnp.exp(-float(ROWS) * rate) for rate in rates]
            terms = [weight[m : m + 1] * jnp.exp(-rates[m] * phase) for m in range(modes)]
            for tile in range(tiles):
                k_ref[pl.ds(tile * ROWS, ROWS), side * LANES : (side + 1) * LANES] = tree(terms)
                if tile < tiles - 1:
                    terms = [t * s for t, s in zip(terms, step8)]
        lanes = pl.ds(pl.multiple_of(pair * width, width), width)
        skip = jnp.concatenate([skip_ref[pl.ds(2 * pair, 1), :], skip_ref[pl.ds(2 * pair + 1, 1), :]], axis=1)
        ks = split_dot(fwd_ref[...], k_ref[...])
        conv = split_dot(inv_ref[...], spectral_product(ks, xs_ref[:, lanes], False))
        pre_ref[:, lanes] = conv + skip * x_ref[:, lanes]
        corr = split_dot(inv_ref[...], spectral_product(ks, bs_ref[:, lanes], True))
        gp_ref[:, lanes] = corr + skip * b_ref[:, lanes]
        return carry

    lax.fori_loop(0, x_ref.shape[1] // width, step, 0)


def lane_is_first(shape, modes):
    return lax.broadcasted_iota(jnp.int32, shape, 1) % (2 * modes) < modes


def scan_body(index_ref, s_ref, rate_ref, qa_ref, qb_ref, out_ref, acc_ref, skip_ref, *, modes, length):
    chunks = s_ref.shape[0]
    groups = rate_ref.shape[0]
    rows = s_ref.shape[2]
    start = pl.multiple_of(index_ref[0] * rows, rows)
    first = lane_is_first((rows, LANES), modes)
    zero = jnp.zeros((rows, LANES), jnp.float32)
    for group in range(groups):
        alpha = jnp.exp(-float(length) * rate_ref[group, pl.ds(start, rows), :])
        before, lead, total0, total1 = zero, zero, zero, zero
        heads = []
        for k in range(chunks):
            value = s_ref[k, group]
            later = pltpu.roll(value, LANES - modes, 1)
            heads.append(before)
            total0 += before * later
            total1 += (lead + before) * later
            lead = alpha * (lead + float(length) * before)
            before = alpha * before + value
        after = zero
        for k in reversed(range(chunks)):
            out_ref[k, group] = jnp.where(first, heads[k], after)
            after = alpha * after + s_ref[k, group]
        acc_ref[group] = jnp.where(first, total0, pltpu.roll(total1, modes, 1))
    for k in range(chunks):
        out_ref[k, groups : 2 * groups] = qa_ref[k]
        out_ref[k, 2 * groups : 3 * groups] = qb_ref[k]
    skip_ref[...] = tree([s_ref[k, groups, : skip_ref.shape[0]] for k in range(chunks)])


def slope_sum_body(index_ref, r_ref, own_ref, acc_ref, rate_ref, out_ref, *, modes):
    chunks, groups, rows = r_ref.shape[0], rate_ref.shape[0], r_ref.shape[2]
    start = pl.multiple_of(index_ref[0] * rows, rows)
    first = lane_is_first((rows, LANES), modes)
    blocks = out_ref.shape[1]
    for group in range(groups):
        cross = tree([own_ref[k, group] * r_ref[k, groups + group] for k in range(chunks)])
        inner = tree([r_ref[k, 2 * groups + group] for k in range(chunks)])
        cross = jnp.where(first, 0.0, cross + pltpu.roll(cross, modes, 1))
        total = inner + jnp.exp(-rate_ref[group, pl.ds(start, rows), :]) * (acc_ref[group] + cross)
        for block in range(group * (blocks // groups), (group + 1) * (blocks // groups)):
            for owner in range(out_ref.shape[0]):
                out_ref[owner, block] = total


def final_body(index_ref, g_ref, residue_ref, decay_ref, gres_ref, gdec_ref, turned_ref):
    modes = residue_ref.shape[0]
    blocks = g_ref.shape[1]
    turned_ref[...] = tree([g_ref[:, block] for block in range(blocks)]).reshape(LANES, LANES).T
    place = pl.multiple_of(lax.rem(index_ref[0], LANES // (2 * modes)) * (2 * modes), 2 * modes)
    plain, slope = turned_ref[pl.ds(place, modes), :], turned_ref[pl.ds(place + modes, modes), :]
    decay = decay_ref[...]
    root = jnp.sqrt(decay)
    gres_ref[...] = root * plain
    gdec_ref[...] = residue_ref[...] * root * (0.5 * plain - decay * slope)


def out_body(par_ref, r_ref, pre_ref, gp_ref, gate_ref, key_ref, value_ref, cot_ref, mixed_ref, ggate_ref, gkey_ref, gvalue_ref, hb_ref):
    blocks, modes = par_ref.shape[0], par_ref.shape[1] // 2
    groups = hb_ref.shape[0] // LANES
    pack = 2 * ROWS
    for group in range(groups):
        hb_ref[pl.ds(group * LANES, LANES), :] = r_ref[:, group].reshape(LANES, LANES).T

    def step(block, carry):
        lanes = pl.ds(pl.multiple_of(block * LANES, LANES), LANES)
        phase = row_iota((ROWS, LANES)).astype(jnp.float32)
        decay, residue = par_ref[block, :modes, :], par_ref[block, modes:, :]
        start = pl.multiple_of(block * 2 * modes, 2 * modes)
        weight = residue * jnp.sqrt(decay)
        first = weight * hb_ref[pl.ds(start, modes), :]
        last = weight * hb_ref[pl.ds(start + modes, modes), :]
        rates = [jnp.broadcast_to(decay[m : m + 1], (ROWS, LANES)) for m in range(modes)]
        step8 = [jnp.exp(-float(ROWS) * rate) for rate in rates]
        terms = [first[m : m + 1] * jnp.exp(-rates[m] * (phase + 1.0)) for m in range(modes)]
        count = pre_ref.shape[0] // pack
        for place in range(count):
            lower = tree(terms)
            terms = [t * s for t, s in zip(terms, step8)]
            upper = tree(terms)
            terms = [t * s for t, s in zip(terms, step8)]
            rows = pl.ds(place * pack, pack)
            pre = pre_ref[rows, lanes] + jnp.concatenate([lower, upper], axis=0)
            mixed_ref[rows, lanes] = (gate_ref[rows, lanes].astype(jnp.float32) * pre).astype(jnp.bfloat16)
            ggate_ref[rows, lanes] = (cot_ref[rows, lanes].astype(jnp.float32) * pre).astype(jnp.bfloat16)
        terms = [last[m : m + 1] * jnp.exp(-rates[m] * (ROWS - phase)) for m in range(modes)]
        for place in reversed(range(count)):
            upper = tree(terms)
            terms = [t * s for t, s in zip(terms, step8)]
            lower = tree(terms)
            terms = [t * s for t, s in zip(terms, step8)]
            rows = pl.ds(place * pack, pack)
            grad = gp_ref[rows, lanes] + jnp.concatenate([lower, upper], axis=0)
            gkey_ref[rows, lanes] = (grad * value_ref[rows, lanes].astype(jnp.float32)).astype(jnp.bfloat16)
            gvalue_ref[rows, lanes] = (grad * key_ref[rows, lanes].astype(jnp.float32)).astype(jnp.bfloat16)
        return carry

    lax.fori_loop(0, blocks, step, 0)


def on_device(gate_in, key_in, value_in, cotangent, skip, residue, decay):
    f32, bf16 = jnp.float32, jnp.bfloat16
    owners = lax.axis_size("ctx")
    blocks = lax.axis_size("ch")
    length, channels = gate_in.shape
    filters, modes = residue.shape
    share = filters // owners
    groups = blocks * 2 * modes // LANES
    place = lax.axis_index("ctx").astype(jnp.int32).reshape(1)
    column = lax.axis_index("ch").astype(jnp.int32).reshape(1)
    forward, inverse = (jnp.asarray(t) for t in transform_tables(length))
    whole = (length, channels)
    size = length * channels

    (sent,) = call(spread_body, [((blocks, 2 * modes, LANES), f32)], 8, (0, 10**5))([VMEM] * 2, decay.T, residue.T)
    params = lax.all_to_all(sent, "ch", 0, 0, tiled=True)

    x, b, xs, bs, gk, sk = call(
        product_body,
        [(whole, f32), (whole, f32), ((2 * length, channels), f32), ((2 * length, channels), f32), (whole, f32), ((blocks, LANES), f32)],
        32,
        (18 * length * size, 36 * size),
    )([VMEM] * 6, gate_in, key_in, value_in, cotangent, forward, inverse)

    states, rates = call(
        state_body,
        [((owners, groups + 1, share, LANES), f32), ((groups, LANES, LANES), f32)],
        16,
        (64 * size, 8 * size),
        [pltpu.VMEM((groups * LANES, LANES), f32)] * 2,
    )([VMEM] * 4, params, x, b, sk)
    states = lax.all_to_all(states, "ctx", 0, 0, tiled=True)

    slopes, inner = call(
        slope_body,
        [((owners, groups, share, LANES), f32)] * 2,
        16,
        (128 * size, 12 * size),
        [pltpu.VMEM((groups * LANES, LANES), f32)] * 2,
    )([VMEM] * 4, params, x, b, gk)

    bundle, acc, grad_skip = call(
        functools.partial(scan_body, modes=modes, length=length),
        [((owners, 3 * groups, share, LANES), f32), ((groups, share, LANES), f32), ((blocks, LANES), f32)],
        8,
        (10**5, 10**6),
    )([SMEM] + [VMEM] * 4, place, states, rates, slopes, inner)
    arrived = lax.all_to_all(bundle, "ctx", 0, 0, tiled=True)

    pre, gp = call(
        local_body,
        [(whole, f32)] * 2,
        32,
        (18 * length * size, 36 * size),
        [pltpu.VMEM((length, 2 * LANES), f32)],
    )([VMEM] * 8, params, skip.reshape(blocks, LANES), x, b, xs, bs, forward, inverse)

    (grads,) = call(
        functools.partial(slope_sum_body, modes=modes),
        [((owners, blocks, share, LANES), f32)],
        8,
        (10**5, 10**6),
    )([SMEM] + [VMEM] * 4, place, arrived, bundle, acc, rates)
    grads = lax.all_to_all(grads.reshape(owners * blocks, share, LANES), ("ctx", "ch"), 0, 0, tiled=True)

    mixed, grad_gate, grad_key, grad_value = call(
        out_body,
        [(whole, bf16)] * 4,
        24,
        (64 * size, 20 * size),
        [pltpu.VMEM((groups * LANES, LANES), f32)],
    )([VMEM] * 8, params, arrived, pre, gp, gate_in, key_in, value_in, cotangent)

    grad_residue, grad_log_decay = call(
        final_body, [((modes, filters), f32)] * 2, 8, (10**5, 10**6), [pltpu.VMEM((LANES, LANES), f32)]
    )([SMEM] + [VMEM] * 3, column, grads.reshape(owners, blocks, share, LANES), residue.T, decay.T)
    return (mixed, grad_gate, grad_key, grad_value, grad_skip.reshape(channels), grad_residue.T, grad_log_decay.T)


def solution(mesh):
    rows = P("ctx", "ch")
    return jax.shard_map(
        on_device,
        mesh=mesh,
        in_specs=(rows, rows, rows, rows, P("ch"), P("ch", None), P("ch", None)),
        out_specs=(rows, rows, rows, rows, P("ch"), P("ch", None), P("ch", None)),
        check_vma=False,
    )
```

```python
import functools

import jax
import jax.numpy as jnp
import numpy as np
from jax import lax
from jax.experimental import pallas as pl
from jax.experimental.pallas import tpu as pltpu
from jax.sharding import PartitionSpec as P

LANES = 128
ROWS = 8
VMEM = pl.BlockSpec(memory_space=pltpu.VMEM)
SMEM = pl.BlockSpec(memory_space=pltpu.SMEM)
HBM = pl.BlockSpec(memory_space=pltpu.HBM)
ANY = pl.BlockSpec(memory_space=pl.ANY)
DMA = pltpu.SemaphoreType.DMA


def call(body, outs, limit_mib, cost, scratch=(), aliases=None):
    flops, moved = cost
    return lambda specs, *args: pl.pallas_call(
        body,
        out_shape=[jax.ShapeDtypeStruct(s, t) for s, t, _ in outs],
        in_specs=list(specs),
        out_specs=[w for _, _, w in outs],
        scratch_shapes=list(scratch),
        input_output_aliases=aliases or {},
        compiler_params=pltpu.CompilerParams(vmem_limit_bytes=limit_mib * 2**20),
        cost_estimate=pl.CostEstimate(flops=flops, bytes_accessed=moved, transcendentals=0),
    )(*args)


def start_all(copies):
    for copy in copies:
        copy.start()
    return copies


def wait_all(copies):
    for copy in copies:
        copy.wait()


def halves(table):
    high = table.astype(jnp.bfloat16)
    low = (table - high.astype(np.float64)).astype(jnp.bfloat16)
    return np.concatenate([high, high, low], axis=1)


def transform_tables(length):
    full = 2 * length
    wave = np.arange(length)[:, None]
    time = np.arange(length)[None, :]
    angle = 2.0 * np.pi * ((wave * time) % full) / full
    real, imag = np.cos(angle), -np.sin(angle)
    imag[0] = np.where(np.arange(length) % 2 == 0, 1.0, -1.0)
    weight = np.where(wave == 0, 1.0, 2.0) / full
    forward = np.concatenate([real, imag], axis=0)
    inverse = np.concatenate([weight * real, weight * imag], axis=0).T
    return halves(forward), halves(inverse)


def split_dot(table, signal):
    high = signal.astype(jnp.bfloat16)
    low = (signal - high.astype(jnp.float32)).astype(jnp.bfloat16)
    return jnp.dot(table, jnp.concatenate([high, low, high], axis=0), preferred_element_type=jnp.float32)


def row_iota(shape):
    return lax.broadcasted_iota(jnp.int32, shape, 0)


def spectral_product(left, right, conjugate):
    count = left.shape[0] // 2
    lre, lim, rre, rim = left[:count], left[count:], right[:count], right[count:]
    first = row_iota(lre.shape) == 0
    both = lim * rim
    cross = jnp.where(first, 0.0, both)
    if conjugate:
        real, imag = lre * rre + cross, lre * rim - lim * rre
    else:
        real, imag = lre * rre - cross, lre * rim + lim * rre
    return jnp.concatenate([real, jnp.where(first, both, imag)], axis=0)


def spread_body(decay_ref, residue_ref, out_ref, sem):
    modes, blocks = decay_ref.shape[0], out_ref.shape[0]
    copies = [pltpu.make_async_copy(decay_ref, out_ref.at[k, pl.ds(0, modes)], sem.at[0, k]) for k in range(blocks)]
    copies += [pltpu.make_async_copy(residue_ref, out_ref.at[k, pl.ds(modes, modes)], sem.at[1, k]) for k in range(blocks)]
    wait_all(start_all(copies))


def product_body(
    gate_ref, key_ref, value_ref, cot_ref, fwd_ref, inv_ref,
    x_ref, b_ref, xs_ref, bs_ref, gk_ref, sk_ref,
    in_ref, fwd_v, inv_v, spec_ref, in_sem, table_sem, out_sem,
):
    width = 2 * LANES
    count = x_ref.shape[1] // width
    fetch = []
    for block in range(count):
        lanes = pl.ds(block * width, width)
        fetch.append(
            start_all([
                pltpu.make_async_copy(ref.at[:, lanes], in_ref.at[k, :, lanes], in_sem.at[block, k])
                for k, ref in enumerate((gate_ref, key_ref, value_ref, cot_ref))
            ])
        )
        if block == 0:
            tables = start_all([
                pltpu.make_async_copy(fwd_ref, fwd_v, table_sem.at[0]),
                pltpu.make_async_copy(inv_ref, inv_v, table_sem.at[1]),
            ])
    stores = []
    for block in range(count):
        lanes = pl.ds(block * width, width)
        wait_all(fetch[block])
        gate, key, value, cot = (in_ref[k, :, lanes].astype(jnp.float32) for k in range(4))
        x, b = key * value, cot * gate
        x_ref[:, lanes] = x
        b_ref[:, lanes] = b
        total = jnp.sum(x * b, axis=0, keepdims=True)
        sk_ref[pl.ds(2 * block, 1), :] = total[:, :LANES]
        sk_ref[pl.ds(2 * block + 1, 1), :] = total[:, LANES:]
        if block == 0:
            tables[0].wait()
        xs = split_dot(fwd_v[...], x)
        bs = split_dot(fwd_v[...], b)
        spec_ref[0, :, lanes] = xs
        spec_ref[1, :, lanes] = bs
        stores += start_all([
            pltpu.make_async_copy(spec_ref.at[k, :, lanes], ref.at[:, lanes], out_sem.at[block, k])
            for k, ref in enumerate((xs_ref, bs_ref))
        ])
        if block == 0:
            tables[1].wait()
        gk_ref[:, lanes] = split_dot(inv_v[...], spectral_product(xs, bs, True))
    wait_all(stores)


def moments(decay, upward, downward):
    modes = decay.shape[0]
    rates = [jnp.broadcast_to(decay[m : m + 1], (ROWS, LANES)) for m in range(modes)]
    step8 = [jnp.exp(-float(ROWS) * rate) for rate in rates]
    tiles = upward[0][1] if upward else downward[0][1]
    ups = [[None] * modes for _ in upward]
    downs = [[None] * modes for _ in downward]
    for tile in range(tiles):
        for sums, (fetch, _), place in [(s, f, tile) for s, f in zip(ups, upward)] + [
            (s, f, tiles - 1 - tile) for s, f in zip(downs, downward)
        ]:
            value = fetch(place)
            for m in range(modes):
                sums[m] = value if sums[m] is None else step8[m] * sums[m] + value
    phase = row_iota((ROWS, LANES)).astype(jnp.float32)
    up_weight = [jnp.exp(-rate * (ROWS - 1.0 - phase)) for rate in rates] if upward else []
    down_weight = [jnp.exp(-rate * phase) for rate in rates] if downward else []

    def gather(sums, weights):
        rows = [jnp.sum(s * w, axis=0, keepdims=True) for s, w in zip(sums, weights)]
        return jnp.concatenate(rows, axis=0)

    return [gather(s, up_weight) for s in ups], [gather(s, down_weight) for s in downs]


def turned(scratch_ref, group, owners):
    return scratch_ref[pl.ds(group * LANES, LANES), :].T.reshape(owners, LANES // owners, LANES)


def state_body(index_ref, par_ref, x_ref, b_ref, sk_ref, out_ref, rate_ref, sums_ref, rates_ref, turn_ref, sem):
    blocks, modes = par_ref.shape[0], par_ref.shape[1] // 2
    tiles = x_ref.shape[0] // ROWS
    owners, share = out_ref.shape[0], out_ref.shape[2]
    groups = sums_ref.shape[0] // LANES
    for owner in range(owners):
        turn_ref[groups, owner, :blocks] = sk_ref[...]
    copies = start_all([pltpu.make_async_copy(turn_ref.at[groups], out_ref.at[:, groups], sem.at[groups])])

    def step(block, carry):
        lanes = pl.ds(pl.multiple_of(block * LANES, LANES), LANES)
        decay = par_ref[block, :modes, :]
        (up,), (down,) = moments(
            decay,
            [(lambda tile: x_ref[pl.ds(tile * ROWS, ROWS), lanes], tiles)],
            [(lambda tile: b_ref[pl.ds(tile * ROWS, ROWS), lanes], tiles)],
        )
        start = pl.multiple_of(block * 2 * modes, 2 * modes)
        sums_ref[pl.ds(start, 2 * modes), :] = jnp.concatenate([up, down], axis=0)
        rates_ref[pl.ds(start, 2 * modes), :] = jnp.concatenate([decay, decay], axis=0)
        return carry

    for group in range(groups):
        lax.fori_loop(group * blocks // groups, (group + 1) * blocks // groups, step, 0)
        turn_ref[group] = turned(sums_ref, group, owners)
        copies += start_all([pltpu.make_async_copy(turn_ref.at[group], out_ref.at[:, group], sem.at[group])])
    for group in range(groups):
        rates_ref[pl.ds(group * LANES, LANES), :] = rates_ref[pl.ds(group * LANES, LANES), :].T
        rate_ref[group] = rates_ref[pl.ds(pl.multiple_of(group * LANES + index_ref[0] * share, share), share), :]
    wait_all(copies)


def slope_body(par_ref, x_ref, b_ref, gk_ref, out_ref, suma_ref, sumb_ref, turn_ref, sem):
    blocks, modes = par_ref.shape[0], par_ref.shape[1] // 2
    positions = x_ref.shape[0]
    tiles = positions // ROWS
    half = modes // 2
    groups = suma_ref.shape[0] // LANES
    owners = out_ref.shape[0]

    def step(block, carry):
        lanes = pl.ds(pl.multiple_of(block * LANES, LANES), LANES)
        phase = row_iota((ROWS, LANES)).astype(jnp.float32)

        def late(tile):
            return (positions - 1.0 - tile * ROWS - phase) * x_ref[pl.ds(tile * ROWS, ROWS), lanes]

        def early(ref):
            return lambda tile: (tile * float(ROWS) + phase) * ref[pl.ds(tile * ROWS, ROWS), lanes]

        for part in range(2):
            decay = par_ref[block, part * half : (part + 1) * half, :]
            (up,), (down, plain, slope) = moments(
                decay,
                [(late, tiles)],
                [
                    (early(b_ref), tiles),
                    (lambda tile: gk_ref[pl.ds(tile * ROWS, ROWS), lanes], tiles),
                    (early(gk_ref), tiles),
                ],
            )
            start = pl.multiple_of(block * 2 * modes, 2 * modes) + part * half
            suma_ref[pl.ds(start, half), :] = down
            suma_ref[pl.ds(start + modes, half), :] = up
            sumb_ref[pl.ds(start, half), :] = plain
            sumb_ref[pl.ds(start + modes, half), :] = slope
        return carry

    copies = []
    for group in range(groups):
        lax.fori_loop(group * blocks // groups, (group + 1) * blocks // groups, step, 0)
        for kind, ref in enumerate((suma_ref, sumb_ref)):
            slot = kind * groups + group
            turn_ref[slot] = turned(ref, group, owners)
            copies += start_all([pltpu.make_async_copy(turn_ref.at[slot], out_ref.at[:, groups + slot], sem.at[slot])])
    wait_all(copies)


def tree(values):
    while len(values) > 1:
        values = [a + b for a, b in zip(values[::2], values[1::2])]
    return values[0]


def local_body(
    par_ref, skip_ref, x_ref, b_ref, xs_ref, bs_ref, fwd_ref, inv_ref,
    pre_ref, gp_ref, token_ref,
    k_ref, fwd_v, inv_v, spec_ref, table_sem, in_sem,
):
    modes = par_ref.shape[1] // 2
    width = 2 * LANES
    tiles = x_ref.shape[0] // ROWS
    count = x_ref.shape[1] // width
    tables = start_all([
        pltpu.make_async_copy(fwd_ref, fwd_v, table_sem.at[0]),
        pltpu.make_async_copy(inv_ref, inv_v, table_sem.at[1]),
    ])
    fetch = []
    for pair in range(count):
        lanes = pl.ds(pair * width, width)
        fetch.append(
            start_all([
                pltpu.make_async_copy(ref.at[:, lanes], spec_ref.at[k, :, lanes], in_sem.at[pair, k])
                for k, ref in enumerate((xs_ref, bs_ref))
            ])
        )
    token_ref[...] = jnp.zeros(token_ref.shape, jnp.float32)
    for pair in range(count):
        phase = row_iota((ROWS, LANES)).astype(jnp.float32)
        for side in range(2):
            block = 2 * pair + side
            decay, residue = par_ref[block, :modes, :], par_ref[block, modes:, :]
            weight = residue * jnp.sqrt(decay)
            rates = [jnp.broadcast_to(decay[m : m + 1], (ROWS, LANES)) for m in range(modes)]
            step8 = [jnp.exp(-float(ROWS) * rate) for rate in rates]
            terms = [weight[m : m + 1] * jnp.exp(-rates[m] * phase) for m in range(modes)]
            for tile in range(tiles):
                k_ref[pair % 2, pl.ds(tile * ROWS, ROWS), side * LANES : (side + 1) * LANES] = tree(terms)
                if tile < tiles - 1:
                    terms = [t * s for t, s in zip(terms, step8)]
        lanes = pl.ds(pair * width, width)
        skip = jnp.concatenate([skip_ref[pl.ds(2 * pair, 1), :], skip_ref[pl.ds(2 * pair + 1, 1), :]], axis=1)
        if pair == 0:
            wait_all(tables)
        ks = split_dot(fwd_v[...], k_ref[pair % 2])
        wait_all(fetch[pair])
        conv = split_dot(inv_v[...], spectral_product(ks, spec_ref[0, :, lanes], False))
        pre_ref[:, lanes] = conv + skip * x_ref[:, lanes]
        corr = split_dot(inv_v[...], spectral_product(ks, spec_ref[1, :, lanes], True))
        gp_ref[:, lanes] = corr + skip * b_ref[:, lanes]


def lane_is_first(shape, modes):
    return lax.broadcasted_iota(jnp.int32, shape, 1) % (2 * modes) < modes


def scan_body(s_ref, rate_ref, slopes_ref, out_ref, heads_ref, acc_ref, skip_ref, sem, *, modes, length):
    chunks, groups, rows = s_ref.shape[0], rate_ref.shape[0], s_ref.shape[2]
    first = lane_is_first((rows, LANES), modes)
    zero = jnp.zeros((rows, LANES), jnp.float32)
    copies = []
    for group in range(groups):
        alpha = jnp.exp(-float(length) * rate_ref[group])
        before, lead, total0, total1 = zero, zero, zero, zero
        heads = []
        for k in range(chunks):
            value = s_ref[k, group]
            later = pltpu.roll(value, LANES - modes, 1)
            heads.append(before)
            total0 += before * later
            total1 += (lead + before) * later
            lead = alpha * (lead + float(length) * before)
            before = alpha * before + value
        after = zero
        for k in reversed(range(chunks)):
            heads_ref[group, k] = jnp.where(first, heads[k], after)
            after = alpha * after + s_ref[k, group]
        copies += start_all([pltpu.make_async_copy(heads_ref.at[group], out_ref.at[:, group], sem.at[group])])
        acc_ref[group] = jnp.where(first, total0, pltpu.roll(total1, modes, 1))
    skip_ref[...] = tree([s_ref[k, groups, : skip_ref.shape[0]] for k in range(chunks)])
    wait_all(copies)


def slope_sum_body(r_ref, own_ref, acc_ref, rate_ref, token_ref, out_ref, pack_ref, sem, *, modes):
    chunks, groups, rows = r_ref.shape[0], rate_ref.shape[0], r_ref.shape[2]
    first = lane_is_first((rows, LANES), modes)
    span = 2 * modes
    fold = LANES // span
    row = row_iota((rows, LANES)) % fold
    column = lax.broadcasted_iota(jnp.int32, (rows, LANES), 1) // span
    for group in range(groups):
        cross = tree([own_ref[group, k] * r_ref[k, groups + group] for k in range(chunks)])
        inner = tree([r_ref[k, 2 * groups + group] for k in range(chunks)])
        cross = jnp.where(first, 0.0, cross + pltpu.roll(cross, modes, 1))
        total = inner + jnp.exp(-rate_ref[group]) * (acc_ref[group] + cross)
        packed = total
        for shift in range(1, fold):
            moved = pltpu.roll(total, LANES - shift * span, 1)
            moved = jnp.where(row >= shift, pltpu.roll(moved, shift, 0), pltpu.roll(moved, rows - fold + shift, 0))
            packed = jnp.where((row - column + fold) % fold == shift, moved, packed)
        for block in range(fold):
            for r in range(rows // fold):
                pack_ref[group * fold + block, pl.ds(r, 1), :] = packed[r * fold + block : r * fold + block + 1]
    wait_all(start_all([pltpu.make_async_copy(pack_ref, out_ref.at[k], sem.at[k]) for k in range(out_ref.shape[0])]))


def final_body(g_ref, residue_ref, decay_ref, gres_ref, gdec_ref, spread_ref):
    modes = residue_ref.shape[0]
    owners, blocks, rows = g_ref.shape[0], g_ref.shape[1], g_ref.shape[2]
    span = 2 * modes
    fold = LANES // span
    total = tree([g_ref[:, block] for block in range(blocks)]).reshape(owners * rows, LANES)
    for k in range(fold):
        moved = total if k == 0 else pltpu.roll(total, LANES - k * span, 1)
        spread_ref[pl.ds(k, owners * rows, stride=fold), :] = moved
    sums = spread_ref[...].T
    plain, slope = sums[:modes], sums[modes:span]
    decay = decay_ref[...]
    root = jnp.sqrt(decay)
    gres_ref[...] = root * plain
    gdec_ref[...] = residue_ref[...] * root * (0.5 * plain - decay * slope)


def out_body(
    par_ref, r_ref, pre_ref, gp_ref, gate_hbm, key_hbm, value_hbm, cot_hbm,
    mixed_ref, ggate_ref, gkey_ref, gvalue_ref,
    hb_ref, gate_ref, key_ref, value_ref, cot_ref, sem,
):
    blocks, modes = par_ref.shape[0], par_ref.shape[1] // 2
    groups = hb_ref.shape[0] // LANES
    pack = 2 * ROWS
    copies = start_all([
        pltpu.make_async_copy(source, target, sem.at[k])
        for k, (source, target) in enumerate(
            zip((gate_hbm, key_hbm, value_hbm, cot_hbm), (gate_ref, key_ref, value_ref, cot_ref))
        )
    ])
    for group in range(groups):
        hb_ref[pl.ds(group * LANES, LANES), :] = r_ref[:, group].reshape(LANES, LANES).T
    wait_all(copies)

    def step(block, carry):
        lanes = pl.ds(pl.multiple_of(block * LANES, LANES), LANES)
        phase = row_iota((ROWS, LANES)).astype(jnp.float32)
        decay, residue = par_ref[block, :modes, :], par_ref[block, modes:, :]
        start = pl.multiple_of(block * 2 * modes, 2 * modes)
        weight = residue * jnp.sqrt(decay)
        first = weight * hb_ref[pl.ds(start, modes), :]
        last = weight * hb_ref[pl.ds(start + modes, modes), :]
        rates = [jnp.broadcast_to(decay[m : m + 1], (ROWS, LANES)) for m in range(modes)]
        step8 = [jnp.exp(-float(ROWS) * rate) for rate in rates]
        terms = [first[m : m + 1] * jnp.exp(-rates[m] * (phase + 1.0)) for m in range(modes)]
        count = pre_ref.shape[0] // pack
        for place in range(count):
            lower = tree(terms)
            terms = [t * s for t, s in zip(terms, step8)]
            upper = tree(terms)
            terms = [t * s for t, s in zip(terms, step8)]
            rows = pl.ds(place * pack, pack)
            pre = pre_ref[rows, lanes] + jnp.concatenate([lower, upper], axis=0)
            mixed_ref[rows, lanes] = (gate_ref[rows, lanes].astype(jnp.float32) * pre).astype(jnp.bfloat16)
            ggate_ref[rows, lanes] = (cot_ref[rows, lanes].astype(jnp.float32) * pre).astype(jnp.bfloat16)
        terms = [last[m : m + 1] * jnp.exp(-rates[m] * (ROWS - phase)) for m in range(modes)]
        for place in reversed(range(count)):
            upper = tree(terms)
            terms = [t * s for t, s in zip(terms, step8)]
            lower = tree(terms)
            terms = [t * s for t, s in zip(terms, step8)]
            rows = pl.ds(place * pack, pack)
            grad = gp_ref[rows, lanes] + jnp.concatenate([lower, upper], axis=0)
            gkey_ref[rows, lanes] = (grad * value_ref[rows, lanes].astype(jnp.float32)).astype(jnp.bfloat16)
            gvalue_ref[rows, lanes] = (grad * key_ref[rows, lanes].astype(jnp.float32)).astype(jnp.bfloat16)
        return carry

    lax.fori_loop(0, blocks, step, 0)


def on_device(gate_in, key_in, value_in, cotangent, skip, residue, decay):
    f32, bf16 = jnp.float32, jnp.bfloat16
    owners = lax.axis_size("ctx")
    blocks = lax.axis_size("ch")
    length, channels = gate_in.shape
    filters, modes = residue.shape
    share = filters // owners
    groups = blocks * 2 * modes // LANES
    place = lax.axis_index("ctx").astype(jnp.int32).reshape(1)
    forward, inverse = (jnp.asarray(t) for t in transform_tables(length))
    whole = (length, channels)
    size = length * channels
    dense = pltpu.VMEM(whole, bf16)
    tables = [pltpu.VMEM(forward.shape, bf16), pltpu.VMEM(inverse.shape, bf16)]
    spectra = pltpu.VMEM((2, 2 * length, channels), f32)
    pairs = channels // (2 * LANES)
    sums = pltpu.VMEM((groups * LANES, LANES), f32)
    tile = (share, LANES)

    (sent,) = call(spread_body, [((blocks, 2 * modes, LANES), f32, HBM)], 4, (0, 10**5), [DMA((2, blocks))])(
        [ANY] * 2, decay.T, residue.T
    )
    params = lax.all_to_all(sent, "ch", 0, 0, tiled=True)

    x, b, xs, bs, gk, sk = call(
        product_body,
        [(whole, f32, VMEM)] * 2
        + [((2 * length, channels), f32, HBM)] * 2
        + [(whole, f32, VMEM), ((blocks, LANES), f32, VMEM)],
        24,
        (18 * length * size, 36 * size),
        [pltpu.VMEM((4, *whole), bf16), *tables, spectra, DMA((pairs, 4)), DMA((2,)), DMA((pairs, 2))],
    )([ANY] * 6, gate_in, key_in, value_in, cotangent, forward, inverse)

    states, rates = call(
        state_body,
        [((owners, groups + 1, *tile), f32, HBM), ((groups, *tile), f32, VMEM)],
        8,
        (64 * size, 8 * size),
        [sums, sums, pltpu.VMEM((groups + 1, owners, *tile), f32), DMA((groups + 1,))],
    )([SMEM] + [VMEM] * 4, place, params, x, b, sk)
    states = lax.all_to_all(states, "ctx", 0, 0, tiled=True)

    (slopes,) = call(
        slope_body,
        [((owners, 3 * groups, *tile), f32, HBM)],
        8,
        (128 * size, 12 * size),
        [sums, sums, pltpu.VMEM((2 * groups, owners, *tile), f32), DMA((2 * groups,))],
    )([VMEM] * 4, params, x, b, gk)

    bundle, heads, acc, grad_skip = call(
        functools.partial(scan_body, modes=modes, length=length),
        [
            ((owners, 3 * groups, *tile), f32, HBM),
            ((groups, owners, *tile), f32, VMEM),
            ((groups, *tile), f32, VMEM),
            ((blocks, LANES), f32, VMEM),
        ],
        8,
        (10**5, 10**6),
        [DMA((groups,))],
        {2: 0},
    )([VMEM, VMEM, HBM], states, rates, slopes)
    arrived = lax.all_to_all(bundle, "ctx", 0, 0, tiled=True)

    pre, gp, token = call(
        local_body,
        [(whole, f32, VMEM)] * 2 + [((ROWS, LANES), f32, VMEM)],
        24,
        (18 * length * size, 36 * size),
        [pltpu.VMEM((2, length, 2 * LANES), f32), *tables, spectra, DMA((2,)), DMA((pairs, 2))],
    )([VMEM] * 4 + [ANY] * 4, params, skip.reshape(blocks, LANES), x, b, xs, bs, forward, inverse)

    packed = (owners, blocks, share * 2 * modes // LANES, LANES)
    (grads,) = call(
        functools.partial(slope_sum_body, modes=modes),
        [(packed, f32, HBM)],
        8,
        (10**5, 10**6),
        [pltpu.VMEM(packed[1:], f32), DMA((owners,))],
    )([VMEM] * 4 + [ANY], arrived, heads, acc, rates, token)
    grads = lax.all_to_all(grads.reshape(owners * blocks, *packed[2:]), ("ctx", "ch"), 0, 0, tiled=True)

    mixed, grad_gate, grad_key, grad_value = call(
        out_body,
        [(whole, bf16, VMEM)] * 4,
        16,
        (64 * size, 20 * size),
        [sums, dense, dense, dense, dense, DMA((4,))],
    )([VMEM] * 4 + [ANY] * 4, params, arrived, pre, gp, gate_in, key_in, value_in, cotangent)

    grad_residue, grad_log_decay = call(
        final_body, [((modes, filters), f32, VMEM)] * 2, 8, (10**5, 10**6), [pltpu.VMEM((LANES, LANES), f32)]
    )([VMEM] * 3, grads.reshape(packed), residue.T, decay.T)
    return (mixed, grad_gate, grad_key, grad_value, grad_skip.reshape(channels), grad_residue.T, grad_log_decay.T)


def solution(mesh):
    rows = P("ctx", "ch")
    return jax.shard_map(
        on_device,
        mesh=mesh,
        in_specs=(rows, rows, rows, rows, P("ch"), P("ch", None), P("ch", None)),
        out_specs=(rows, rows, rows, rows, P("ch"), P("ch", None), P("ch", None)),
        check_vma=False,
    )
```

```python
import functools

import jax
import jax.numpy as jnp
import numpy as np
from jax import lax
from jax.experimental import pallas as pl
from jax.experimental.pallas import tpu as pltpu
from jax.sharding import PartitionSpec as P

LANES = 128
ROWS = 8
VMEM = pl.BlockSpec(memory_space=pltpu.VMEM)
SMEM = pl.BlockSpec(memory_space=pltpu.SMEM)
HBM = pl.BlockSpec(memory_space=pltpu.HBM)
DMA = pltpu.SemaphoreType.DMA


def call(body, outs, limit_mib, cost, scratch=(), aliases=None):
    flops, moved = cost
    return lambda specs, *args: pl.pallas_call(
        body,
        out_shape=[pltpu.HBM(s, t) if w is HBM else jax.ShapeDtypeStruct(s, t) for s, t, w in outs],
        in_specs=list(specs),
        out_specs=[w for _, _, w in outs],
        scratch_shapes=list(scratch),
        input_output_aliases=aliases or {},
        compiler_params=pltpu.CompilerParams(vmem_limit_bytes=limit_mib * 2**20),
        cost_estimate=pl.CostEstimate(flops=flops, bytes_accessed=moved, transcendentals=0),
    )(*(pltpu.with_memory_space_constraint(a, pltpu.HBM) if w is HBM else a for w, a in zip(specs, args)))


def start_all(copies):
    for copy in copies:
        copy.start()
    return copies


def wait_all(copies):
    for copy in copies:
        copy.wait()


def halves(table):
    high = table.astype(jnp.bfloat16)
    low = (table - high.astype(np.float64)).astype(jnp.bfloat16)
    return np.concatenate([high, low], axis=1)


def transform_tables(length):
    full = 2 * length
    wave = np.arange(length)[:, None]
    time = np.arange(length)[None, :]
    angle = 2.0 * np.pi * ((wave * time) % full) / full
    real, imag = np.cos(angle), -np.sin(angle)
    imag[0] = np.where(np.arange(length) % 2 == 0, 1.0, -1.0)
    weight = np.where(wave == 0, 1.0, 2.0) / full
    forward = np.concatenate([real, imag], axis=0)
    inverse = np.concatenate([weight * real, weight * imag], axis=0).T
    return halves(forward), halves(inverse)


def split_dot(table, signal):
    high = signal.astype(jnp.bfloat16)
    low = (signal - high.astype(jnp.float32)).astype(jnp.bfloat16)
    depth = signal.shape[0]
    table = jnp.concatenate([table[:, :depth], table], axis=1)
    return jnp.dot(table, jnp.concatenate([low, high, high], axis=0), preferred_element_type=jnp.float32)


def row_iota(shape):
    return lax.broadcasted_iota(jnp.int32, shape, 0)


def spectral_product(left, right, conjugate):
    count = left.shape[0] // 2
    lre, lim, rre, rim = left[:count], left[count:], right[:count], right[count:]
    first = row_iota(lre.shape) == 0
    both = lim * rim
    cross = jnp.where(first, 0.0, both)
    if conjugate:
        real, imag = lre * rre + cross, lre * rim - lim * rre
    else:
        real, imag = lre * rre - cross, lre * rim + lim * rre
    return jnp.concatenate([real, jnp.where(first, both, imag)], axis=0)


def spread_body(decay_ref, residue_ref, out_ref, held_ref, in_sem, out_sem):
    modes, blocks = decay_ref.shape[0], out_ref.shape[0]
    wait_all(
        start_all([
            pltpu.make_async_copy(ref, held_ref.at[pl.ds(k * modes, modes)], in_sem.at[k])
            for k, ref in enumerate((decay_ref, residue_ref))
        ])
    )
    wait_all(start_all([pltpu.make_async_copy(held_ref, out_ref.at[k], out_sem.at[k]) for k in range(blocks)]))


def product_body(
    gate_ref, key_ref, value_ref, cot_ref, fwd_ref, inv_ref,
    x_ref, b_ref, xs_ref, bs_ref, gk_ref, sk_ref,
    in_ref, fwd_v, inv_v, spec_ref, turn_ref, in_sem, table_sem, out_sem,
):
    width = 2 * LANES
    count = x_ref.shape[1] // width
    fetch = []
    for block in range(count):
        lanes = pl.ds(block * width, width)
        fetch.append(
            start_all([
                pltpu.make_async_copy(ref.at[:, lanes], in_ref.at[k, :, lanes], in_sem.at[block, k])
                for k, ref in enumerate((gate_ref, key_ref, value_ref, cot_ref))
            ])
        )
        if block == 0:
            tables = start_all([
                pltpu.make_async_copy(fwd_ref, fwd_v, table_sem.at[0]),
                pltpu.make_async_copy(inv_ref, inv_v, table_sem.at[1]),
            ])
    stores = []
    for block in range(count):
        lanes = pl.ds(block * width, width)
        wait_all(fetch[block])
        gate, key, value, cot = (in_ref[k, :, lanes].astype(jnp.float32) for k in range(4))
        x, b = key * value, cot * gate
        x_ref[:, lanes] = x
        b_ref[:, lanes] = b
        total = jnp.sum(x * b, axis=0, keepdims=True)
        sk_ref[pl.ds(2 * block, 1), :] = total[:, :LANES]
        sk_ref[pl.ds(2 * block + 1, 1), :] = total[:, LANES:]
        if block == 0:
            tables[0].wait()
        xs = split_dot(fwd_v[...], x)
        bs = split_dot(fwd_v[...], b)
        spec_ref[0, :, lanes] = xs
        spec_ref[1, :, lanes] = bs
        stores += start_all([
            pltpu.make_async_copy(spec_ref.at[k, :, lanes], ref.at[:, lanes], out_sem.at[block, k])
            for k, ref in enumerate((xs_ref, bs_ref))
        ])
        if block == 0:
            tables[1].wait()
        turn_ref[:, lanes] = split_dot(inv_v[...], spectral_product(xs, bs, True))
        stores += start_all([pltpu.make_async_copy(turn_ref.at[:, lanes], gk_ref.at[:, lanes], out_sem.at[block, 2])])
    wait_all(stores)


def moments(decay, upward, downward):
    modes = decay.shape[0]
    rates = [jnp.broadcast_to(decay[m : m + 1], (ROWS, LANES)) for m in range(modes)]
    step8 = [jnp.exp(-float(ROWS) * rate) for rate in rates]
    tiles = upward[0][1] if upward else downward[0][1]
    ups = [[None] * modes for _ in upward]
    downs = [[None] * modes for _ in downward]
    for tile in range(tiles):
        for sums, (fetch, _), place in [(s, f, tile) for s, f in zip(ups, upward)] + [
            (s, f, tiles - 1 - tile) for s, f in zip(downs, downward)
        ]:
            value = fetch(place)
            for m in range(modes):
                sums[m] = value if sums[m] is None else step8[m] * sums[m] + value
    phase = row_iota((ROWS, LANES)).astype(jnp.float32)
    up_weight = [jnp.exp(-rate * (ROWS - 1.0 - phase)) for rate in rates] if upward else []
    down_weight = [jnp.exp(-rate * phase) for rate in rates] if downward else []

    def gather(sums, weights):
        rows = [jnp.sum(s * w, axis=0, keepdims=True) for s, w in zip(sums, weights)]
        return jnp.concatenate(rows, axis=0)

    return [gather(s, up_weight) for s in ups], [gather(s, down_weight) for s in downs]


def turned(scratch_ref, group, owners):
    return scratch_ref[pl.ds(group * LANES, LANES), :].T.reshape(owners, LANES // owners, LANES)


def state_body(index_ref, par_ref, x_ref, b_ref, sk_ref, out_ref, rate_ref, sums_ref, rates_ref, turn_ref, sem):
    blocks, modes = par_ref.shape[0], par_ref.shape[1] // 2
    tiles = x_ref.shape[0] // ROWS
    owners, share = out_ref.shape[0], out_ref.shape[2]
    groups = sums_ref.shape[0] // LANES
    for owner in range(owners):
        turn_ref[groups, owner, :blocks] = sk_ref[...]
    copies = start_all([pltpu.make_async_copy(turn_ref.at[groups], out_ref.at[:, groups], sem.at[groups])])

    def step(block, carry):
        lanes = pl.ds(pl.multiple_of(block * LANES, LANES), LANES)
        decay = par_ref[block, :modes, :]
        (up,), (down,) = moments(
            decay,
            [(lambda tile: x_ref[pl.ds(tile * ROWS, ROWS), lanes], tiles)],
            [(lambda tile: b_ref[pl.ds(tile * ROWS, ROWS), lanes], tiles)],
        )
        start = pl.multiple_of(block * 2 * modes, 2 * modes)
        sums_ref[pl.ds(start, 2 * modes), :] = jnp.concatenate([up, down], axis=0)
        rates_ref[pl.ds(start, 2 * modes), :] = jnp.concatenate([decay, decay], axis=0)
        return carry

    for group in range(groups):
        lax.fori_loop(group * blocks // groups, (group + 1) * blocks // groups, step, 0)
        turn_ref[group] = turned(sums_ref, group, owners)
        copies += start_all([pltpu.make_async_copy(turn_ref.at[group], out_ref.at[:, group], sem.at[group])])
    for group in range(groups):
        rates_ref[pl.ds(group * LANES, LANES), :] = rates_ref[pl.ds(group * LANES, LANES), :].T
        rate_ref[group] = rates_ref[pl.ds(pl.multiple_of(group * LANES + index_ref[0] * share, share), share), :]
    wait_all(copies)


def slope_body(par_ref, x_ref, b_ref, gk_hbm, out_ref, gk_ref, suma_ref, sumb_ref, turn_ref, sem, gk_sem):
    blocks, modes = par_ref.shape[0], par_ref.shape[1] // 2
    positions = x_ref.shape[0]
    tiles = positions // ROWS
    groups = suma_ref.shape[0] // LANES
    owners = out_ref.shape[0]
    fetch = pltpu.make_async_copy(gk_hbm, gk_ref, gk_sem)
    fetch.start()

    def reader(ref, block, weight=None):
        lanes = pl.ds(pl.multiple_of(block * LANES, LANES), LANES)
        phase = row_iota((ROWS, LANES)).astype(jnp.float32)

        def read(tile):
            value = ref[pl.ds(tile * ROWS, ROWS), lanes]
            return value if weight is None else weight(tile * float(ROWS) + phase) * value

        return read, tiles

    def keep(ref, block, first, second):
        start = pl.multiple_of(block * 2 * modes, 2 * modes)
        ref[pl.ds(start, modes), :] = first
        ref[pl.ds(start + modes, modes), :] = second

    def outer(block, carry):
        late = reader(x_ref, block, lambda t: positions - 1.0 - t)
        (up,), (down,) = moments(par_ref[block, :modes, :], [late], [reader(b_ref, block, lambda t: t)])
        keep(suma_ref, block, down, up)
        return carry

    def inner(block, carry):
        pair = [reader(gk_ref, block), reader(gk_ref, block, lambda t: t)]
        _, (plain, slope) = moments(par_ref[block, :modes, :], [], pair)
        keep(sumb_ref, block, plain, slope)
        return carry

    copies = []
    for kind, (step, ref) in enumerate(((outer, suma_ref), (inner, sumb_ref))):
        if kind == 1:
            fetch.wait()
        for group in range(groups):
            lax.fori_loop(group * blocks // groups, (group + 1) * blocks // groups, step, 0)
            slot = kind * groups + group
            turn_ref[slot] = turned(ref, group, owners)
            copies += start_all([pltpu.make_async_copy(turn_ref.at[slot], out_ref.at[:, groups + slot], sem.at[slot])])
    wait_all(copies)


def tree(values):
    while len(values) > 1:
        values = [a + b for a, b in zip(values[::2], values[1::2])]
    return values[0]


def local_body(
    par_ref, x_ref, b_ref, skip_hbm, xs_ref, bs_ref, fwd_ref, inv_ref,
    pre_ref, gp_ref,
    skip_ref, k_ref, fwd_v, inv_v, spec_ref, turn_ref, table_sem, in_sem, out_sem,
):
    modes = par_ref.shape[1] // 2
    width = 2 * LANES
    tiles = x_ref.shape[0] // ROWS
    count = x_ref.shape[1] // width
    tables = start_all([
        pltpu.make_async_copy(fwd_ref, fwd_v, table_sem.at[0]),
        pltpu.make_async_copy(inv_ref, inv_v, table_sem.at[1]),
        pltpu.make_async_copy(skip_hbm, skip_ref, table_sem.at[2]),
    ])
    fetch, stores = [], []
    for pair in range(count):
        lanes = pl.ds(pair * width, width)
        fetch.append(
            start_all([
                pltpu.make_async_copy(ref.at[:, lanes], spec_ref.at[k, :, lanes], in_sem.at[pair, k])
                for k, ref in enumerate((xs_ref, bs_ref))
            ])
        )

    def impulse(block, carry):
        phase = row_iota((ROWS, LANES)).astype(jnp.float32)
        lanes = pl.ds(pl.multiple_of(block * LANES, LANES), LANES)
        decay, residue = par_ref[block, :modes, :], par_ref[block, modes:, :]
        weight = residue * jnp.sqrt(decay)
        rates = [jnp.broadcast_to(decay[m : m + 1], (ROWS, LANES)) for m in range(modes)]
        step8 = [jnp.exp(-float(ROWS) * rate) for rate in rates]
        terms = [weight[m : m + 1] * jnp.exp(-rates[m] * phase) for m in range(modes)]
        for tile in range(tiles):
            k_ref[pl.ds(tile * ROWS, ROWS), lanes] = tree(terms)
            if tile < tiles - 1:
                terms = [t * s for t, s in zip(terms, step8)]
        return carry

    lax.fori_loop(0, 2 * count, impulse, 0)
    for pair in range(count):
        lanes = pl.ds(pair * width, width)
        if pair == 0:
            wait_all(tables)
        skip = jnp.concatenate([skip_ref[pl.ds(2 * pair, 1), :], skip_ref[pl.ds(2 * pair + 1, 1), :]], axis=1)
        ks = split_dot(fwd_v[...], k_ref[:, lanes])
        wait_all(fetch[pair])
        conv = split_dot(inv_v[...], spectral_product(ks, spec_ref[0, :, lanes], False))
        turn_ref[0, :, lanes] = conv + skip * x_ref[:, lanes]
        corr = split_dot(inv_v[...], spectral_product(ks, spec_ref[1, :, lanes], True))
        turn_ref[1, :, lanes] = corr + skip * b_ref[:, lanes]
        stores += start_all([
            pltpu.make_async_copy(turn_ref.at[k, :, lanes], ref.at[:, lanes], out_sem.at[pair, k])
            for k, ref in enumerate((pre_ref, gp_ref))
        ])
    wait_all(stores)


def lane_is_first(shape, modes):
    return lax.broadcasted_iota(jnp.int32, shape, 1) % (2 * modes) < modes


def scan_body(s_ref, rate_ref, slopes_ref, out_ref, heads_ref, acc_ref, skip_ref, sem, *, modes, length):
    chunks, groups, rows = s_ref.shape[0], rate_ref.shape[0], s_ref.shape[2]
    first = lane_is_first((rows, LANES), modes)
    zero = jnp.zeros((rows, LANES), jnp.float32)
    copies = []
    for group in range(groups):
        alpha = jnp.exp(-float(length) * rate_ref[group])
        before, lead, total0, total1 = zero, zero, zero, zero
        heads = []
        for k in range(chunks):
            value = s_ref[k, group]
            later = pltpu.roll(value, LANES - modes, 1)
            heads.append(before)
            total0 += before * later
            total1 += (lead + before) * later
            lead = alpha * (lead + float(length) * before)
            before = alpha * before + value
        after = zero
        for k in reversed(range(chunks)):
            heads_ref[group, k] = jnp.where(first, heads[k], after)
            after = alpha * after + s_ref[k, group]
        copies += start_all([pltpu.make_async_copy(heads_ref.at[group], out_ref.at[:, group], sem.at[group])])
        acc_ref[group] = jnp.where(first, total0, pltpu.roll(total1, modes, 1))
    skip_ref[...] = tree([s_ref[k, groups, : skip_ref.shape[0]] for k in range(chunks)])
    wait_all(copies)


def slope_sum_body(r_ref, own_ref, acc_ref, rate_ref, done_ref, out_ref, pack_ref, sem, *, modes):
    chunks, groups, rows = r_ref.shape[0], rate_ref.shape[0], r_ref.shape[2]
    first = lane_is_first((rows, LANES), modes)
    span = 2 * modes
    fold = LANES // span
    row = row_iota((rows, LANES)) % fold
    column = lax.broadcasted_iota(jnp.int32, (rows, LANES), 1) // span
    for group in range(groups):
        cross = tree([own_ref[group, k] * r_ref[k, groups + group] for k in range(chunks)])
        inner = tree([r_ref[k, 2 * groups + group] for k in range(chunks)])
        cross = jnp.where(first, 0.0, cross + pltpu.roll(cross, modes, 1))
        total = inner + jnp.exp(-rate_ref[group]) * (acc_ref[group] + cross)
        packed = total
        for shift in range(1, fold):
            moved = pltpu.roll(total, LANES - shift * span, 1)
            moved = jnp.where(row >= shift, pltpu.roll(moved, shift, 0), pltpu.roll(moved, rows - fold + shift, 0))
            packed = jnp.where((row - column + fold) % fold == shift, moved, packed)
        for block in range(fold):
            for r in range(rows // fold):
                pack_ref[group * fold + block, pl.ds(r, 1), :] = packed[r * fold + block : r * fold + block + 1]
    wait_all(start_all([pltpu.make_async_copy(pack_ref, out_ref.at[k], sem.at[k]) for k in range(out_ref.shape[0])]))


def final_body(g_ref, residue_ref, decay_ref, gres_ref, gdec_ref, spread_ref):
    modes = residue_ref.shape[0]
    owners, blocks, rows = g_ref.shape[0], g_ref.shape[1], g_ref.shape[2]
    span = 2 * modes
    fold = LANES // span
    total = tree([g_ref[:, block] for block in range(blocks)]).reshape(owners * rows, LANES)
    for k in range(fold):
        moved = total if k == 0 else pltpu.roll(total, LANES - k * span, 1)
        spread_ref[pl.ds(k, owners * rows, stride=fold), :] = moved
    sums = spread_ref[...].T
    plain, slope = sums[:modes], sums[modes:span]
    decay = decay_ref[...]
    root = jnp.sqrt(decay)
    gres_ref[...] = root * plain
    gdec_ref[...] = residue_ref[...] * root * (0.5 * plain - decay * slope)


def out_body(
    par_ref, r_ref, pre_hbm, gp_hbm, gate_hbm, key_hbm, value_hbm, cot_hbm,
    mixed_hbm, ggate_hbm, gkey_hbm, gvalue_hbm,
    hb_ref, wide_ref, in_ref, out_ref, wide_sem, in_sem, out_sem,
):
    blocks, modes = par_ref.shape[0], par_ref.shape[1] // 2
    groups = hb_ref.shape[0] // LANES
    pack = 2 * ROWS
    width = 2 * LANES
    fetch = []
    for pair in range(blocks // 2):
        lanes = pl.ds(pair * width, width)
        fetch.append(
            start_all(
                [
                    pltpu.make_async_copy(ref.at[:, lanes], wide_ref.at[k, :, lanes], wide_sem.at[pair, k])
                    for k, ref in enumerate((pre_hbm, gp_hbm))
                ]
                + [
                    pltpu.make_async_copy(ref.at[:, lanes], in_ref.at[k, :, lanes], in_sem.at[pair, k])
                    for k, ref in enumerate((gate_hbm, cot_hbm, value_hbm, key_hbm))
                ]
            )
        )
    for group in range(groups):
        hb_ref[pl.ds(group * LANES, LANES), :] = r_ref[:, group].reshape(LANES, LANES).T

    def step(block, carry):
        lanes = pl.ds(pl.multiple_of(block * LANES, LANES), LANES)
        phase = row_iota((ROWS, LANES)).astype(jnp.float32)
        decay, residue = par_ref[block, :modes, :], par_ref[block, modes:, :]
        start = pl.multiple_of(block * 2 * modes, 2 * modes)
        weight = residue * jnp.sqrt(decay)
        first = weight * hb_ref[pl.ds(start, modes), :]
        last = weight * hb_ref[pl.ds(start + modes, modes), :]
        rates = [jnp.broadcast_to(decay[m : m + 1], (ROWS, LANES)) for m in range(modes)]
        step8 = [jnp.exp(-float(ROWS) * rate) for rate in rates]
        count = in_ref.shape[1] // pack

        def finish(kind, place, extra):
            rows = pl.ds(place * pack, pack)
            total = wide_ref[kind, rows, lanes] + extra
            for k in (2 * kind, 2 * kind + 1):
                out_ref[k, rows, lanes] = (in_ref[k, rows, lanes].astype(jnp.float32) * total).astype(jnp.bfloat16)

        terms = [first[m : m + 1] * jnp.exp(-rates[m] * (phase + 1.0)) for m in range(modes)]
        for place in range(count):
            lower = tree(terms)
            terms = [t * s for t, s in zip(terms, step8)]
            upper = tree(terms)
            terms = [t * s for t, s in zip(terms, step8)]
            finish(0, place, jnp.concatenate([lower, upper], axis=0))
        terms = [last[m : m + 1] * jnp.exp(-rates[m] * (ROWS - phase)) for m in range(modes)]
        for place in reversed(range(count)):
            upper = tree(terms)
            terms = [t * s for t, s in zip(terms, step8)]
            lower = tree(terms)
            terms = [t * s for t, s in zip(terms, step8)]
            finish(1, place, jnp.concatenate([lower, upper], axis=0))
        return carry

    stores = []
    for pair in range(blocks // 2):
        lanes = pl.ds(pair * width, width)
        wait_all(fetch[pair])
        lax.fori_loop(2 * pair, 2 * pair + 2, step, 0)
        stores += start_all([
            pltpu.make_async_copy(out_ref.at[k, :, lanes], ref.at[:, lanes], out_sem.at[pair, k])
            for k, ref in enumerate((mixed_hbm, ggate_hbm, gkey_hbm, gvalue_hbm))
        ])
    wait_all(stores)


def on_device(gate_in, key_in, value_in, cotangent, skip, residue, decay):
    f32, bf16 = jnp.float32, jnp.bfloat16
    owners = lax.axis_size("ctx")
    blocks = lax.axis_size("ch")
    length, channels = gate_in.shape
    filters, modes = residue.shape
    share = filters // owners
    groups = blocks * 2 * modes // LANES
    place = lax.axis_index("ctx").astype(jnp.int32).reshape(1)
    forward, inverse = (jnp.asarray(t) for t in transform_tables(length))
    whole = (length, channels)
    size = length * channels
    wide = pltpu.VMEM(whole, f32)
    tables = [pltpu.VMEM(forward.shape, bf16), pltpu.VMEM(inverse.shape, bf16)]
    spectra = pltpu.VMEM((2, 2 * length, channels), f32)
    pairs = channels // (2 * LANES)
    sums = pltpu.VMEM((groups * LANES, LANES), f32)
    tile = (share, LANES)

    (sent,) = call(spread_body, [((blocks, 2 * modes, LANES), f32, HBM)], 4, (0, 10**5), [pltpu.VMEM((2 * modes, LANES), f32), DMA((2,)), DMA((blocks,))])(
        [HBM] * 2, decay.T, residue.T
    )
    params = lax.all_to_all(sent, "ch", 0, 0, tiled=True)

    x, b, xs, bs, gk, sk = call(
        product_body,
        [(whole, f32, VMEM)] * 2
        + [((2 * length, channels), f32, HBM)] * 2
        + [(whole, f32, HBM), ((blocks, LANES), f32, VMEM)],
        24,
        (18 * length * size, 36 * size),
        [pltpu.VMEM((4, *whole), bf16), *tables, spectra, wide, DMA((pairs, 4)), DMA((2,)), DMA((pairs, 3))],
    )([HBM] * 6, gate_in, key_in, value_in, cotangent, forward, inverse)

    states, rates = call(
        state_body,
        [((owners, groups + 1, *tile), f32, HBM), ((groups, *tile), f32, VMEM)],
        8,
        (64 * size, 8 * size),
        [sums, sums, pltpu.VMEM((groups + 1, owners, *tile), f32), DMA((groups + 1,))],
    )([SMEM] + [VMEM] * 4, place, params, x, b, sk)
    states = lax.all_to_all(states, "ctx", 0, 0, tiled=True)

    (slopes,) = call(
        slope_body,
        [((owners, 3 * groups, *tile), f32, HBM)],
        8,
        (128 * size, 12 * size),
        [wide, sums, sums, pltpu.VMEM((2 * groups, owners, *tile), f32), DMA((2 * groups,)), DMA],
    )([VMEM] * 3 + [HBM], params, x, b, gk)

    bundle, heads, acc, grad_skip = call(
        functools.partial(scan_body, modes=modes, length=length),
        [
            ((owners, 3 * groups, *tile), f32, HBM),
            ((groups, owners, *tile), f32, VMEM),
            ((groups, *tile), f32, VMEM),
            ((blocks, LANES), f32, VMEM),
        ],
        8,
        (10**5, 10**6),
        [DMA((groups,))],
        {2: 0},
    )([VMEM, VMEM, HBM], states, rates, slopes)
    arrived = lax.all_to_all(bundle, "ctx", 0, 0, tiled=True)

    pre, gp = call(
        local_body,
        [(whole, f32, HBM)] * 2,
        24,
        (18 * length * size, 36 * size),
        [pltpu.VMEM((blocks, LANES), f32), wide, *tables, spectra]
        + [pltpu.VMEM((2, *whole), f32), DMA((3,)), DMA((pairs, 2)), DMA((pairs, 2))],
    )([VMEM] * 3 + [HBM] * 5, params, x, b, skip.reshape(blocks, LANES), xs, bs, forward, inverse)

    packed = (owners, blocks, share * 2 * modes // LANES, LANES)
    (grads,) = call(
        functools.partial(slope_sum_body, modes=modes),
        [(packed, f32, HBM)],
        8,
        (10**5, 10**6),
        [pltpu.VMEM(packed[1:], f32), DMA((owners,))],
    )([VMEM] * 4 + [HBM], arrived, heads, acc, rates, pre)
    grads = lax.all_to_all(grads.reshape(owners * blocks, *packed[2:]), ("ctx", "ch"), 0, 0, tiled=True)

    mixed, grad_gate, grad_key, grad_value = call(
        out_body,
        [(whole, bf16, HBM)] * 4,
        16,
        (64 * size, 20 * size),
        [sums, pltpu.VMEM((2, *whole), f32), pltpu.VMEM((4, *whole), bf16), pltpu.VMEM((4, *whole), bf16)]
        + [DMA((pairs, 2)), DMA((pairs, 4)), DMA((pairs, 4))],
    )([VMEM] * 2 + [HBM] * 6, params, arrived, pre, gp, gate_in, key_in, value_in, cotangent)

    grad_residue, grad_log_decay = call(
        final_body, [((modes, filters), f32, VMEM)] * 2, 8, (10**5, 10**6), [pltpu.VMEM((LANES, LANES), f32)]
    )([VMEM] * 3, grads.reshape(packed), residue.T, decay.T)
    return (mixed, grad_gate, grad_key, grad_value, grad_skip.reshape(channels), grad_residue.T, grad_log_decay.T)


def solution(mesh):
    rows = P("ctx", "ch")
    return jax.shard_map(
        on_device,
        mesh=mesh,
        in_specs=(rows, rows, rows, rows, P("ch"), P("ch", None), P("ch", None)),
        out_specs=(rows, rows, rows, rows, P("ch"), P("ch", None), P("ch", None)),
        check_vma=False,
    )
```

```python
import functools

import jax
import jax.numpy as jnp
from jax import lax
from jax.experimental import pallas as pl
from jax.experimental.pallas import tpu as pltpu
from jax.sharding import PartitionSpec as P

LANES = 128
ROWS = 8
SPAN = 16
VMEM = pl.BlockSpec(memory_space=pltpu.VMEM)
SMEM = pl.BlockSpec(memory_space=pltpu.SMEM)
HBM = pl.BlockSpec(memory_space=pltpu.HBM)
DMA = pltpu.SemaphoreType.DMA


def call(body, outs, limit_mib, cost, scratch=(), aliases=None):
    flops, moved = cost
    return lambda specs, *args: pl.pallas_call(
        body,
        out_shape=[pltpu.HBM(s, t) if w is HBM else jax.ShapeDtypeStruct(s, t) for s, t, w in outs],
        in_specs=list(specs),
        out_specs=[w for _, _, w in outs],
        scratch_shapes=list(scratch),
        input_output_aliases=aliases or {},
        compiler_params=pltpu.CompilerParams(vmem_limit_bytes=limit_mib * 2**20),
        cost_estimate=pl.CostEstimate(flops=flops, bytes_accessed=moved, transcendentals=0),
    )(*(pltpu.with_memory_space_constraint(a, pltpu.HBM) if w is HBM else a for w, a in zip(specs, args)))


def start_all(copies):
    for copy in copies:
        copy.start()
    return copies


def wait_all(copies):
    for copy in copies:
        copy.wait()


def spread_body(decay_ref, residue_ref, out_ref, held_ref, in_sem, out_sem):
    modes, blocks = decay_ref.shape[0], out_ref.shape[0]
    wait_all(
        start_all([
            pltpu.make_async_copy(ref, held_ref.at[pl.ds(k * modes, modes)], in_sem.at[k])
            for k, ref in enumerate((decay_ref, residue_ref))
        ])
    )
    wait_all(start_all([pltpu.make_async_copy(held_ref, out_ref.at[k], out_sem.at[k]) for k in range(blocks)]))


def tree(values):
    while len(values) > 1:
        odd = values[-1:] if len(values) % 2 else []
        values = [a + b for a, b in zip(values[::2], values[1::2])] + odd
    return values[0]


def turned(scratch_ref, group, owners):
    return scratch_ref[pl.ds(group * LANES, LANES), :].T.reshape(owners, LANES // owners, LANES)


def by_mode(ref, row, blocks):
    return ref[pl.ds(row, blocks, stride=ref.shape[0] // blocks), :]


def product_body(
    gate_hbm, key_hbm, value_hbm, cot_hbm,
    x_ref, b_ref, sk_ref,
    in_ref, sem,
):
    length, channels = gate_hbm.shape
    blocks = channels // LANES
    pieces = sem.shape[0]
    depth = length // pieces
    fetch = [
        start_all([
            pltpu.make_async_copy(ref.at[pl.ds(p * depth, depth)], in_ref.at[k, pl.ds(p * depth, depth)], sem.at[p, k])
            for k, ref in enumerate((gate_hbm, key_hbm, value_hbm, cot_hbm))
        ])
        for p in range(pieces)
    ]

    def step(place, sums):
        rows = pl.ds(pl.multiple_of(place * SPAN, SPAN), SPAN)
        after = []
        for block in range(blocks):
            lanes = pl.ds(block * LANES, LANES)
            gate, key, value, cot = (in_ref[k, rows, lanes].astype(jnp.float32) for k in range(4))
            x, b = key * value, cot * gate
            for part in range(SPAN // ROWS):
                target = pl.ds((place * SPAN + part * ROWS) * blocks + block, ROWS, stride=blocks)
                x_ref[target, :] = x[part * ROWS : (part + 1) * ROWS]
                b_ref[target, :] = b[part * ROWS : (part + 1) * ROWS]
            both = x * b
            after.append(sums[block] + tree([both[k * ROWS : (k + 1) * ROWS] for k in range(SPAN // ROWS)]))
        return tuple(after)

    sums = tuple(jnp.zeros((ROWS, LANES), jnp.float32) for _ in range(blocks))
    for p in range(pieces):
        wait_all(fetch[p])
        sums = lax.fori_loop(p * depth // SPAN, (p + 1) * depth // SPAN, step, sums)
    for block in range(blocks):
        sk_ref[pl.ds(block, 1), :] = jnp.sum(sums[block], axis=0, keepdims=True)


def state_body(
    index_ref, par_ref, x_ref, b_ref, sk_ref,
    out_ref, hs_hbm, bs_hbm, rate_ref,
    sums_ref, rates_ref, turn_ref, hs_ref, bs_ref, sem, snap_sem,
):
    owners, share = out_ref.shape[0], out_ref.shape[2]
    groups = sums_ref.shape[0] // LANES
    blocks = sk_ref.shape[0]
    modes = par_ref.shape[0] // blocks // 2
    spans = hs_ref.shape[0]
    pieces = snap_sem.shape[1]
    part = spans // pieces
    for owner in range(owners):
        turn_ref[groups, owner, :blocks] = sk_ref[...]
    copies = start_all([pltpu.make_async_copy(turn_ref.at[groups], out_ref.at[:, groups], sem.at[groups])])
    for group in range(groups):
        for block in range(group * blocks // groups, (group + 1) * blocks // groups):
            decay = par_ref[pl.ds(block * 2 * modes, modes), :]
            rates_ref[pl.ds(block * 2 * modes, 2 * modes), :] = jnp.concatenate([decay, decay], axis=0)
        rates_ref[pl.ds(group * LANES, LANES), :] = rates_ref[pl.ds(group * LANES, LANES), :].T
        rate_ref[group] = rates_ref[pl.ds(pl.multiple_of(group * LANES + index_ref[0] * share, share), share), :]
    factor = [jnp.exp(-by_mode(par_ref, m, blocks)) for m in range(modes)]

    def step(span, carry):
        ups, downs = carry
        mirror = spans - 1 - span
        for m in range(modes):
            hs_ref[span, pl.ds(m * blocks, blocks), :] = ups[m]
            bs_ref[mirror + 1, pl.ds(m * blocks, blocks), :] = downs[m]
        for r in range(SPAN):
            x = x_ref[pl.ds(pl.multiple_of((span * SPAN + r) * blocks, blocks), blocks), :]
            b = b_ref[pl.ds(pl.multiple_of((mirror * SPAN + SPAN - 1 - r) * blocks, blocks), blocks), :]
            ups = tuple(f * u + x for f, u in zip(factor, ups))
            downs = tuple(f * d + b for f, d in zip(factor, downs))
        return ups, downs

    zero = tuple(jnp.zeros((blocks, LANES), jnp.float32) for _ in range(modes))
    ups, downs = zero, zero
    for p in range(pieces):
        ups, downs = lax.fori_loop(p * part, (p + 1) * part, step, (ups, downs))
        here, there = pl.ds(p * part, part), pl.ds((pieces - 1 - p) * part + 1, part)
        copies += start_all([
            pltpu.make_async_copy(hs_ref.at[here], hs_hbm.at[here], snap_sem.at[0, p]),
            pltpu.make_async_copy(bs_ref.at[there], bs_hbm.at[there], snap_sem.at[1, p]),
        ])
    for m in range(modes):
        bs_ref[0, pl.ds(m * blocks, blocks), :] = downs[m]
        sums_ref[pl.ds(m, blocks, stride=2 * modes), :] = ups[m]
        sums_ref[pl.ds(modes + m, blocks, stride=2 * modes), :] = downs[m]
    copies += start_all([pltpu.make_async_copy(bs_ref.at[0], bs_hbm.at[0], sem.at[groups + 1])])
    for group in range(groups):
        turn_ref[group] = turned(sums_ref, group, owners)
        copies += start_all([pltpu.make_async_copy(turn_ref.at[group], out_ref.at[:, group], sem.at[group])])
    wait_all(copies)


def slope_body(
    par_ref, x_ref, b_ref, hs_hbm, bs_hbm,
    out_ref,
    hs_ref, bs_ref, lag_ref, run_ref, suma_ref, sumb_ref, turn_ref, sem, snap_sem,
):
    owners = out_ref.shape[0]
    groups = suma_ref.shape[0] // LANES
    spans = hs_ref.shape[0]
    blocks = x_ref.shape[0] // (spans * SPAN)
    modes = par_ref.shape[0] // blocks // 2
    pieces = snap_sem.shape[1]
    part = spans // pieces
    fetch = []
    for p in range(pieces):
        here = pl.ds(p * part, part)
        there = pl.ds(p * part + (1 if p else 0), part + (0 if p else 1))
        fetch.append(
            start_all([
                pltpu.make_async_copy(hs_hbm.at[here], hs_ref.at[here], snap_sem.at[0, p]),
                pltpu.make_async_copy(bs_hbm.at[there], bs_ref.at[there], snap_sem.at[1, p]),
            ])
        )
    zero = jnp.zeros((blocks, LANES), jnp.float32)
    SLOPE, SUM0, SUM1, DOWN, POWER, FACTOR, FAR = range(7)
    for m in range(modes):
        rate = by_mode(par_ref, m, blocks)
        rows = pl.ds(m * blocks, blocks)
        for kind in (SLOPE, SUM0, SUM1, DOWN):
            run_ref[kind, rows, :] = zero
        run_ref[POWER, rows, :] = zero + 1.0
        run_ref[FACTOR, rows, :] = jnp.exp(-rate)
        run_ref[FAR, rows, :] = jnp.exp(-float(SPAN) * rate)
    for u in range(SPAN):
        lag_ref[pl.ds(u * blocks, blocks), :] = zero

    def step(span, carry):
        def at(ref, r):
            return ref[pl.ds(pl.multiple_of((span * SPAN + r) * blocks, blocks), blocks), :]

        x = [at(x_ref, r) for r in range(SPAN)]
        b = [at(b_ref, r) for r in range(SPAN)]
        for u in range(SPAN):
            rows = pl.ds(u * blocks, blocks)
            total = lag_ref[rows, :]
            for r in range(SPAN - u):
                total = total + b[r + u] * x[r]
            lag_ref[rows, :] = total
        late = [x[r] * (SPAN - 1.0 - r) for r in range(SPAN - 1)]
        early = [b[r] * float(r) for r in range(SPAN - 1, 0, -1)]
        begin = (span * SPAN).astype(jnp.float32)
        for m in range(modes):
            rows = pl.ds(m * blocks, blocks)
            factor, far = run_ref[FACTOR, rows, :], run_ref[FAR, rows, :]
            up, down = late[0], early[0]
            for k in range(1, SPAN - 1):
                up = factor * up + late[k]
                down = factor * down + early[k]
            up, down = factor * up, factor * down
            head = hs_ref[span, rows, :]
            own = bs_ref[span, rows, :] - far * bs_ref[span + 1, rows, :]
            slope, power = run_ref[SLOPE, rows, :], run_ref[POWER, rows, :]
            run_ref[SUM0, rows, :] = run_ref[SUM0, rows, :] + head * own
            run_ref[SUM1, rows, :] = run_ref[SUM1, rows, :] + (slope * own + head * (own + down))
            run_ref[DOWN, rows, :] = run_ref[DOWN, rows, :] + power * (begin * own + down)
            run_ref[POWER, rows, :] = power * far
            run_ref[SLOPE, rows, :] = far * (slope + float(SPAN) * head) + up
        return carry

    for p in range(pieces):
        wait_all(fetch[p])
        lax.fori_loop(p * part, (p + 1) * part, step, 0)
    lags = [lag_ref[pl.ds(u * blocks, blocks), :] for u in range(SPAN)]
    for m in range(modes):
        rows = pl.ds(m * blocks, blocks)
        factor = run_ref[FACTOR, rows, :]
        plain, slope = lags[SPAN - 1], lags[SPAN - 1] * (SPAN - 1.0)
        for u in range(SPAN - 2, -1, -1):
            plain = factor * plain + lags[u]
            slope = factor * slope + lags[u] * float(u)
        low, high = pl.ds(m, blocks, stride=2 * modes), pl.ds(modes + m, blocks, stride=2 * modes)
        suma_ref[low, :] = run_ref[DOWN, rows, :]
        suma_ref[high, :] = run_ref[SLOPE, rows, :]
        sumb_ref[low, :] = factor * run_ref[SUM0, rows, :] + plain
        sumb_ref[high, :] = factor * run_ref[SUM1, rows, :] + slope
    copies = []
    for kind, ref in enumerate((suma_ref, sumb_ref)):
        for group in range(groups):
            slot = kind * groups + group
            turn_ref[slot] = turned(ref, group, owners)
            copies += start_all([pltpu.make_async_copy(turn_ref.at[slot], out_ref.at[:, groups + slot], sem.at[slot])])
    wait_all(copies)


def local_body(par_ref, x_ref, b_ref, skip_hbm, y_hbm, z_hbm, skip_ref, out_ref, skip_sem, sem):
    fetch = pltpu.make_async_copy(skip_hbm, skip_ref, skip_sem)
    fetch.start()
    blocks = skip_ref.shape[0]
    modes = par_ref.shape[0] // blocks // 2
    spans = x_ref.shape[0] // blocks // SPAN
    pieces = sem.shape[1]
    part = spans // pieces
    factors, terms = [], []
    for m in range(modes):
        rate = by_mode(par_ref, m, blocks)
        factors.append(jnp.exp(-rate))
        terms.append(by_mode(par_ref, modes + m, blocks) * jnp.sqrt(rate))
    kernel = []
    for u in range(SPAN):
        kernel.append(tree(terms))
        terms = [t * f for t, f in zip(terms, factors)]
    fetch.wait()
    kernel[0] = kernel[0] + skip_ref[...]

    def step(span, carry):
        def at(r):
            return pl.ds(pl.multiple_of((span * SPAN + r) * blocks, blocks), blocks)

        x = [x_ref[at(r), :] for r in range(SPAN)]
        for r in range(SPAN):
            out_ref[0, at(r), :] = tree([kernel[u] * x[r - u] for u in range(r + 1)])
        b = [b_ref[at(r), :] for r in range(SPAN)]
        for r in range(SPAN):
            out_ref[1, at(r), :] = tree([kernel[u] * b[r + u] for u in range(SPAN - r)])
        return carry

    copies = []
    for p in range(pieces):
        lax.fori_loop(p * part, (p + 1) * part, step, 0)
        rows = pl.ds(p * part * SPAN * blocks, part * SPAN * blocks)
        copies += start_all([
            pltpu.make_async_copy(out_ref.at[k, rows], ref.at[rows], sem.at[k, p]) for k, ref in enumerate((y_hbm, z_hbm))
        ])
    wait_all(copies)


def lane_is_first(shape, modes):
    return lax.broadcasted_iota(jnp.int32, shape, 1) % (2 * modes) < modes


def scan_body(s_ref, rate_ref, slopes_ref, out_ref, heads_ref, acc_ref, skip_ref, sem, *, modes, length):
    chunks, groups, rows = s_ref.shape[0], rate_ref.shape[0], s_ref.shape[2]
    first = lane_is_first((rows, LANES), modes)
    zero = jnp.zeros((rows, LANES), jnp.float32)
    copies = []
    for group in range(groups):
        alpha = jnp.exp(-float(length) * rate_ref[group])
        before, lead, total0, total1 = zero, zero, zero, zero
        heads = []
        for k in range(chunks):
            value = s_ref[k, group]
            later = pltpu.roll(value, LANES - modes, 1)
            heads.append(before)
            total0 += before * later
            total1 += (lead + before) * later
            lead = alpha * (lead + float(length) * before)
            before = alpha * before + value
        after = zero
        for k in reversed(range(chunks)):
            heads_ref[group, k] = jnp.where(first, heads[k], after)
            after = alpha * after + s_ref[k, group]
        copies += start_all([pltpu.make_async_copy(heads_ref.at[group], out_ref.at[:, group], sem.at[group])])
        acc_ref[group] = jnp.where(first, total0, pltpu.roll(total1, modes, 1))
    skip_ref[...] = tree([s_ref[k, groups, : skip_ref.shape[0]] for k in range(chunks)])
    wait_all(copies)


def slope_sum_body(r_ref, own_ref, acc_ref, rate_ref, done_ref, out_ref, pack_ref, sem, *, modes):
    chunks, groups, rows = r_ref.shape[0], rate_ref.shape[0], r_ref.shape[2]
    first = lane_is_first((rows, LANES), modes)
    span = 2 * modes
    fold = LANES // span
    row = lax.broadcasted_iota(jnp.int32, (rows, LANES), 0) % fold
    column = lax.broadcasted_iota(jnp.int32, (rows, LANES), 1) // span
    for group in range(groups):
        cross = tree([own_ref[group, k] * r_ref[k, groups + group] for k in range(chunks)])
        inner = tree([r_ref[k, 2 * groups + group] for k in range(chunks)])
        cross = jnp.where(first, 0.0, cross + pltpu.roll(cross, modes, 1))
        total = inner + jnp.exp(-rate_ref[group]) * (acc_ref[group] + cross)
        packed = total
        for shift in range(1, fold):
            moved = pltpu.roll(total, LANES - shift * span, 1)
            moved = jnp.where(row >= shift, pltpu.roll(moved, shift, 0), pltpu.roll(moved, rows - fold + shift, 0))
            packed = jnp.where((row - column + fold) % fold == shift, moved, packed)
        for block in range(fold):
            for r in range(rows // fold):
                pack_ref[group * fold + block, pl.ds(r, 1), :] = packed[r * fold + block : r * fold + block + 1]
    wait_all(start_all([pltpu.make_async_copy(pack_ref, out_ref.at[k], sem.at[k]) for k in range(out_ref.shape[0])]))


def final_body(g_ref, residue_ref, decay_ref, gres_ref, gdec_ref, spread_ref):
    modes = residue_ref.shape[0]
    owners, blocks, rows = g_ref.shape[0], g_ref.shape[1], g_ref.shape[2]
    span = 2 * modes
    fold = LANES // span
    total = tree([g_ref[:, block] for block in range(blocks)]).reshape(owners * rows, LANES)
    for k in range(fold):
        moved = total if k == 0 else pltpu.roll(total, LANES - k * span, 1)
        spread_ref[pl.ds(k, owners * rows, stride=fold), :] = moved
    sums = spread_ref[...].T
    plain, slope = sums[:modes], sums[modes:span]
    decay = decay_ref[...]
    root = jnp.sqrt(decay)
    gres_ref[...] = root * plain
    gdec_ref[...] = residue_ref[...] * root * (0.5 * plain - decay * slope)


def out_body(
    par_ref, r_ref, y_hbm, z_hbm, hs_hbm, bs_hbm, gate_hbm, key_hbm, value_hbm, cot_hbm,
    mixed_hbm, ggate_hbm, gkey_hbm, gvalue_hbm,
    hb_ref, run_ref, loc_ref, snap_ref, in_ref, out_ref, loc_sem, in_sem, out_sem,
):
    length, channels = gate_hbm.shape
    blocks = channels // LANES
    modes = par_ref.shape[0] // blocks // 2
    groups = hb_ref.shape[0] // LANES
    spans = length // SPAN
    pieces = loc_sem.shape[0]
    part = spans // pieces
    depth = part * SPAN
    fetch = []
    for p in range(pieces):
        mirror = pieces - 1 - p
        copies = []
        for kind, (place, local, snaps, shift, near) in enumerate((
            (p, y_hbm, hs_hbm, 0, (gate_hbm, cot_hbm)),
            (mirror, z_hbm, bs_hbm, 1, (value_hbm, key_hbm)),
        )):
            rows = pl.ds(place * depth * blocks, depth * blocks)
            copies.append(pltpu.make_async_copy(local.at[rows], loc_ref.at[kind, rows], loc_sem.at[p, 2 * kind]))
            source, target = pl.ds(place * part + shift, part), pl.ds(place * part, part)
            copies.append(
                pltpu.make_async_copy(snaps.at[source], snap_ref.at[kind, target], loc_sem.at[p, 2 * kind + 1])
            )
            rows = pl.ds(place * depth, depth)
            for k, ref in enumerate(near):
                slot = 2 * kind + k
                copies.append(pltpu.make_async_copy(ref.at[rows], in_ref.at[slot, rows], in_sem.at[p, slot]))
        fetch.append(start_all(copies))
    for group in range(groups):
        hb_ref[pl.ds(group * LANES, LANES), :] = r_ref[:, group].reshape(LANES, LANES).T
    FACTOR, FAR, WEIGHT, HEAD, TAIL = range(5)
    for m in range(modes):
        rows = pl.ds(m * blocks, blocks)
        rate = by_mode(par_ref, m, blocks)
        factor = jnp.exp(-rate)
        run_ref[FACTOR, rows, :] = factor
        run_ref[FAR, rows, :] = jnp.exp(-float(SPAN) * rate)
        run_ref[WEIGHT, rows, :] = by_mode(par_ref, modes + m, blocks) * jnp.sqrt(rate) * factor
        run_ref[HEAD, rows, :] = by_mode(hb_ref, m, blocks)
        run_ref[TAIL, rows, :] = by_mode(hb_ref, modes + m, blocks)

    def finish(kind, span, run):
        terms, factors = [], []
        for m in range(modes):
            rows = pl.ds(m * blocks, blocks)
            state = run_ref[run, rows, :]
            terms.append(run_ref[WEIGHT, rows, :] * (snap_ref[kind, span, rows, :] + state))
            run_ref[run, rows, :] = state * run_ref[FAR, rows, :]
            factors.append(run_ref[FACTOR, rows, :])
        for k in range(SPAN):
            r = k if kind == 0 else SPAN - 1 - k
            rows = pl.ds(pl.multiple_of((span * SPAN + r) * blocks, blocks), blocks)
            loc_ref[kind, rows, :] = loc_ref[kind, rows, :] + tree(terms)
            if k < SPAN - 1:
                terms = [t * f for t, f in zip(terms, factors)]
        rows = pl.ds(pl.multiple_of(span * SPAN, SPAN), SPAN)
        for block in range(blocks):
            lanes = pl.ds(block * LANES, LANES)
            total = jnp.concatenate(
                [
                    loc_ref[kind, pl.ds((span * SPAN + half * ROWS) * blocks + block, ROWS, stride=blocks), :]
                    for half in range(SPAN // ROWS)
                ],
                axis=0,
            )
            for slot in (2 * kind, 2 * kind + 1):
                value = in_ref[slot, rows, lanes].astype(jnp.float32) * total
                out_ref[slot, rows, lanes] = value.astype(jnp.bfloat16)

    def step(span, carry):
        finish(0, span, HEAD)
        finish(1, spans - 1 - span, TAIL)
        return carry

    stores = []
    for p in range(pieces):
        wait_all(fetch[p])
        lax.fori_loop(p * part, (p + 1) * part, step, 0)
        for slot, ref in enumerate((mixed_hbm, ggate_hbm, gkey_hbm, gvalue_hbm)):
            rows = pl.ds((p if slot < 2 else pieces - 1 - p) * depth, depth)
            stores += start_all([pltpu.make_async_copy(out_ref.at[slot, rows], ref.at[rows], out_sem.at[p, slot])])
    wait_all(stores)


def on_device(gate_in, key_in, value_in, cotangent, skip, residue, decay):
    f32, bf16 = jnp.float32, jnp.bfloat16
    owners = lax.axis_size("ctx")
    blocks = lax.axis_size("ch")
    length, channels = gate_in.shape
    filters, modes = residue.shape
    share = filters // owners
    groups = blocks * 2 * modes // LANES
    spans = length // SPAN
    pieces = 4
    place = lax.axis_index("ctx").astype(jnp.int32).reshape(1)
    whole = (length, channels)
    signal = (length * blocks, LANES)
    heads_at, tails_at = (spans, modes * blocks, LANES), (spans + 1, modes * blocks, LANES)
    size = length * channels
    sums = pltpu.VMEM((groups * LANES, LANES), f32)
    dense = pltpu.VMEM((4, *whole), bf16)
    tile = (share, LANES)

    (sent,) = call(
        spread_body,
        [((blocks, 2 * modes, LANES), f32, HBM)],
        4,
        (0, 10**5),
        [pltpu.VMEM((2 * modes, LANES), f32), DMA((2,)), DMA((blocks,))],
    )([HBM] * 2, decay.T, residue.T)
    params = lax.all_to_all(sent, "ch", 0, 0, tiled=True).reshape(blocks * 2 * modes, LANES)

    x, b, sk = call(
        product_body,
        [(signal, f32, VMEM)] * 2 + [((blocks, LANES), f32, VMEM)],
        16,
        (4 * size, 16 * size),
        [dense, DMA((pieces, 4))],
    )([HBM] * 4, gate_in, key_in, value_in, cotangent)

    states, head_states, tail_states, rates = call(
        state_body,
        [
            ((owners, groups + 1, *tile), f32, HBM),
            (heads_at, f32, HBM),
            (tails_at, f32, HBM),
            ((groups, *tile), f32, VMEM),
        ],
        16,
        (64 * size, 16 * size),
        [sums, sums, pltpu.VMEM((groups + 1, owners, *tile), f32), pltpu.VMEM(heads_at, f32), pltpu.VMEM(tails_at, f32)]
        + [DMA((groups + 2,)), DMA((2, pieces))],
    )([SMEM] + [VMEM] * 4, place, params, x, b, sk)
    states = lax.all_to_all(states, "ctx", 0, 0, tiled=True)

    (slopes,) = call(
        slope_body,
        [((owners, 3 * groups, *tile), f32, HBM)],
        16,
        (100 * size, 16 * size),
        [pltpu.VMEM(heads_at, f32), pltpu.VMEM(tails_at, f32), pltpu.VMEM((SPAN * blocks, LANES), f32)]
        + [pltpu.VMEM((7, modes * blocks, LANES), f32), sums, sums, pltpu.VMEM((2 * groups, owners, *tile), f32)]
        + [DMA((2 * groups,)), DMA((2, pieces))],
    )([VMEM] * 3 + [HBM] * 2, params, x, b, head_states, tail_states)

    bundle, heads, acc, grad_skip = call(
        functools.partial(scan_body, modes=modes, length=length),
        [
            ((owners, 3 * groups, *tile), f32, HBM),
            ((groups, owners, *tile), f32, VMEM),
            ((groups, *tile), f32, VMEM),
            ((blocks, LANES), f32, VMEM),
        ],
        8,
        (10**5, 10**6),
        [DMA((groups,))],
        {2: 0},
    )([VMEM, VMEM, HBM], states, rates, slopes)
    arrived = lax.all_to_all(bundle, "ctx", 0, 0, tiled=True)

    y, z = call(
        local_body,
        [(signal, f32, HBM)] * 2,
        16,
        (40 * size, 16 * size),
        [pltpu.VMEM((blocks, LANES), f32), pltpu.VMEM((2, *signal), f32), DMA, DMA((2, pieces))],
    )([VMEM] * 3 + [HBM], params, x, b, skip.reshape(blocks, LANES))

    packed = (owners, blocks, share * 2 * modes // LANES, LANES)
    (grads,) = call(
        functools.partial(slope_sum_body, modes=modes),
        [(packed, f32, HBM)],
        8,
        (10**5, 10**6),
        [pltpu.VMEM(packed[1:], f32), DMA((owners,))],
    )([VMEM] * 4 + [HBM], arrived, heads, acc, rates, y)
    grads = lax.all_to_all(grads.reshape(owners * blocks, *packed[2:]), ("ctx", "ch"), 0, 0, tiled=True)

    mixed, grad_gate, grad_key, grad_value = call(
        out_body,
        [(whole, bf16, HBM)] * 4,
        24,
        (64 * size, 32 * size),
        [sums, pltpu.VMEM((5, modes * blocks, LANES), f32), pltpu.VMEM((2, *signal), f32)]
        + [pltpu.VMEM((2, *heads_at), f32), dense, dense, DMA((pieces, 4)), DMA((pieces, 4)), DMA((pieces, 4))],
    )([VMEM] * 2 + [HBM] * 8, params, arrived, y, z, head_states, tail_states, gate_in, key_in, value_in, cotangent)

    grad_residue, grad_log_decay = call(
        final_body, [((modes, filters), f32, VMEM)] * 2, 8, (10**5, 10**6), [pltpu.VMEM((LANES, LANES), f32)]
    )([VMEM] * 3, grads.reshape(packed), residue.T, decay.T)
    return (mixed, grad_gate, grad_key, grad_value, grad_skip.reshape(channels), grad_residue.T, grad_log_decay.T)


def solution(mesh):
    rows = P("ctx", "ch")
    return jax.shard_map(
        on_device,
        mesh=mesh,
        in_specs=(rows, rows, rows, rows, P("ch"), P("ch", None), P("ch", None)),
        out_specs=(rows, rows, rows, rows, P("ch"), P("ch", None), P("ch", None)),
        check_vma=False,
    )
```

```python
import functools

import jax
import jax.numpy as jnp
from jax import lax
from jax.experimental import pallas as pl
from jax.experimental.pallas import tpu as pltpu
from jax.sharding import PartitionSpec as P

LANES = 128
ROWS = 8
SPAN = 16
VMEM = pl.BlockSpec(memory_space=pltpu.VMEM)
SMEM = pl.BlockSpec(memory_space=pltpu.SMEM)
HBM = pl.BlockSpec(memory_space=pltpu.HBM)
DMA = pltpu.SemaphoreType.DMA


def call(body, outs, limit_mib, cost, scratch=(), aliases=None):
    flops, moved = cost
    return lambda specs, *args: pl.pallas_call(
        body,
        out_shape=[pltpu.HBM(s, t) if w is HBM else jax.ShapeDtypeStruct(s, t) for s, t, w in outs],
        in_specs=list(specs),
        out_specs=[w for _, _, w in outs],
        scratch_shapes=list(scratch),
        input_output_aliases=aliases or {},
        compiler_params=pltpu.CompilerParams(vmem_limit_bytes=limit_mib * 2**20),
        cost_estimate=pl.CostEstimate(flops=flops, bytes_accessed=moved, transcendentals=0),
    )(*(pltpu.with_memory_space_constraint(a, pltpu.HBM) if w is HBM else a for w, a in zip(specs, args)))


def start_all(copies):
    for copy in copies:
        copy.start()
    return copies


def wait_all(copies):
    for copy in copies:
        copy.wait()


def spread_body(decay_ref, residue_ref, out_ref, held_ref, in_sem, out_sem):
    modes, blocks = decay_ref.shape[0], out_ref.shape[0]
    wait_all(
        start_all([
            pltpu.make_async_copy(ref, held_ref.at[pl.ds(k * modes, modes)], in_sem.at[k])
            for k, ref in enumerate((decay_ref, residue_ref))
        ])
    )
    wait_all(start_all([pltpu.make_async_copy(held_ref, out_ref.at[k], out_sem.at[k]) for k in range(blocks)]))


def tree(values):
    while len(values) > 1:
        odd = values[-1:] if len(values) % 2 else []
        values = [a + b for a, b in zip(values[::2], values[1::2])] + odd
    return values[0]


def turned(scratch_ref, group, owners):
    return scratch_ref[pl.ds(group * LANES, LANES), :].T.reshape(owners, LANES // owners, LANES)


def by_mode(ref, row, blocks):
    return ref[pl.ds(row, blocks, stride=ref.shape[0] // blocks), :]


def position(span, offset, blocks):
    return pl.ds(pl.multiple_of((span * SPAN + offset) * blocks, blocks), blocks)


def product_body(
    gate_hbm, key_hbm, value_hbm, cot_hbm,
    x_ref, b_ref, sk_ref, lag_ref,
    in_ref, sem,
):
    length, channels = gate_hbm.shape
    blocks = channels // LANES
    pieces = sem.shape[0]
    depth = length // pieces
    fetch = [
        start_all([
            pltpu.make_async_copy(ref.at[pl.ds(p * depth, depth)], in_ref.at[k, pl.ds(p * depth, depth)], sem.at[p, k])
            for k, ref in enumerate((gate_hbm, key_hbm, value_hbm, cot_hbm))
        ])
        for p in range(pieces)
    ]
    lag_ref[...] = jnp.zeros(lag_ref.shape, jnp.float32)

    def step(place, sums):
        rows = pl.ds(pl.multiple_of(place * SPAN, SPAN), SPAN)
        after = []
        for block in range(blocks):
            lanes = pl.ds(block * LANES, LANES)
            gate, key, value, cot = (in_ref[k, rows, lanes].astype(jnp.float32) for k in range(4))
            x, b = key * value, cot * gate
            for part in range(SPAN // ROWS):
                target = pl.ds((place * SPAN + part * ROWS) * blocks + block, ROWS, stride=blocks)
                x_ref[target, :] = x[part * ROWS : (part + 1) * ROWS]
                b_ref[target, :] = b[part * ROWS : (part + 1) * ROWS]
            both = x * b
            after.append(sums[block] + tree([both[k * ROWS : (k + 1) * ROWS] for k in range(SPAN // ROWS)]))
        return tuple(after)

    def lags(span, carry):
        x = [x_ref[position(span, r, blocks), :] for r in range(SPAN)]
        b = [b_ref[position(span, r, blocks), :] for r in range(SPAN)]
        for u in range(SPAN):
            rows = pl.ds(u * blocks, blocks)
            lag_ref[rows, :] = lag_ref[rows, :] + tree([b[r + u] * x[r] for r in range(SPAN - u)])
        return carry

    sums = tuple(jnp.zeros((ROWS, LANES), jnp.float32) for _ in range(blocks))
    for p in range(pieces):
        wait_all(fetch[p])
        sums = lax.fori_loop(p * depth // SPAN, (p + 1) * depth // SPAN, step, sums)
        lax.fori_loop(p * depth // SPAN, (p + 1) * depth // SPAN, lags, 0)
    for block in range(blocks):
        sk_ref[pl.ds(block, 1), :] = jnp.sum(sums[block], axis=0, keepdims=True)


def state_body(
    par_ref, x_ref, b_ref, sk_ref,
    out_ref, hs_hbm, bs_hbm,
    sums_ref, turn_ref, hs_ref, bs_ref, sem, snap_sem,
):
    owners = out_ref.shape[0]
    groups = sums_ref.shape[0] // LANES
    blocks = sk_ref.shape[0]
    modes = par_ref.shape[0] // blocks // 2
    spans = hs_ref.shape[0]
    pieces = snap_sem.shape[1]
    part = spans // pieces
    for owner in range(owners):
        turn_ref[groups, owner, :blocks] = sk_ref[...]
    copies = start_all([pltpu.make_async_copy(turn_ref.at[groups], out_ref.at[:, groups], sem.at[groups])])
    factor = [jnp.exp(-by_mode(par_ref, m, blocks)) for m in range(modes)]

    def step(span, carry):
        ups, downs = carry
        mirror = spans - 1 - span
        for m in range(modes):
            hs_ref[span, pl.ds(m * blocks, blocks), :] = ups[m]
            bs_ref[mirror + 1, pl.ds(m * blocks, blocks), :] = downs[m]
        for r in range(SPAN):
            x = x_ref[pl.ds(pl.multiple_of((span * SPAN + r) * blocks, blocks), blocks), :]
            b = b_ref[pl.ds(pl.multiple_of((mirror * SPAN + SPAN - 1 - r) * blocks, blocks), blocks), :]
            ups = tuple(f * u + x for f, u in zip(factor, ups))
            downs = tuple(f * d + b for f, d in zip(factor, downs))
        return ups, downs

    zero = tuple(jnp.zeros((blocks, LANES), jnp.float32) for _ in range(modes))
    ups, downs = zero, zero
    for p in range(pieces):
        ups, downs = lax.fori_loop(p * part, (p + 1) * part, step, (ups, downs))
        here, there = pl.ds(p * part, part), pl.ds((pieces - 1 - p) * part + 1, part)
        copies += start_all([
            pltpu.make_async_copy(hs_ref.at[here], hs_hbm.at[here], snap_sem.at[0, p]),
            pltpu.make_async_copy(bs_ref.at[there], bs_hbm.at[there], snap_sem.at[1, p]),
        ])
    for m in range(modes):
        bs_ref[0, pl.ds(m * blocks, blocks), :] = downs[m]
        sums_ref[pl.ds(m, blocks, stride=2 * modes), :] = ups[m]
        sums_ref[pl.ds(modes + m, blocks, stride=2 * modes), :] = downs[m]
    copies += start_all([pltpu.make_async_copy(bs_ref.at[0], bs_hbm.at[0], sem.at[groups + 1])])
    for group in range(groups):
        turn_ref[group] = turned(sums_ref, group, owners)
        copies += start_all([pltpu.make_async_copy(turn_ref.at[group], out_ref.at[:, group], sem.at[group])])
    wait_all(copies)


def slope_body(
    index_ref, par_ref, x_ref, b_ref, lag_ref, hs_hbm, bs_hbm,
    out_ref, rate_ref,
    hs_ref, bs_ref, up_ref, down_ref, run_ref, sums_ref, turn_ref, rates_ref, sem, snap_sem,
):
    owners = out_ref.shape[0]
    kinds = sums_ref.shape[0]
    groups = sums_ref.shape[1] // LANES
    spans = hs_ref.shape[0]
    blocks = lag_ref.shape[0] // SPAN
    modes = par_ref.shape[0] // blocks // 2
    fetch = start_all([
        pltpu.make_async_copy(hs_hbm, hs_ref, snap_sem.at[0]),
        pltpu.make_async_copy(bs_hbm, bs_ref, snap_sem.at[1]),
    ])
    share = rate_ref.shape[1]
    zero = jnp.zeros((blocks, LANES), jnp.float32)
    SLOPE, SUM0, SUM1, DOWN, POWER, FACTOR, FAR = range(7)
    for m in range(modes):
        rate = by_mode(par_ref, m, blocks)
        rows = pl.ds(m * blocks, blocks)
        for kind in (SLOPE, SUM0, SUM1, DOWN):
            run_ref[kind, rows, :] = zero
        run_ref[POWER, rows, :] = zero + 1.0
        run_ref[FACTOR, rows, :] = jnp.exp(-rate)
        run_ref[FAR, rows, :] = jnp.exp(-float(SPAN) * rate)

    def send(kind, first, second):
        for m in range(modes):
            sums_ref[kind, pl.ds(m, blocks, stride=2 * modes), :] = first(m)
            sums_ref[kind, pl.ds(modes + m, blocks, stride=2 * modes), :] = second(m)
        sent = []
        for group in range(groups):
            slot = kind * groups + group
            turned = sums_ref[kind, pl.ds(group * LANES, LANES), :].T
            turn_ref[slot] = turned.reshape(owners, LANES // owners, LANES)
            sent += start_all([pltpu.make_async_copy(turn_ref.at[slot], out_ref.at[:, groups + slot], sem.at[slot])])
        return sent

    def at(m):
        return pl.ds(m * blocks, blocks)

    for group in range(groups):
        for block in range(group * blocks // groups, (group + 1) * blocks // groups):
            decay = par_ref[pl.ds(block * 2 * modes, modes), :]
            rates_ref[pl.ds(block * 2 * modes, 2 * modes), :] = jnp.concatenate([decay, decay], axis=0)
        rates_ref[pl.ds(group * LANES, LANES), :] = rates_ref[pl.ds(group * LANES, LANES), :].T
        rate_ref[group] = rates_ref[pl.ds(pl.multiple_of(group * LANES + index_ref[0] * share, share), share), :]

    def near(span, carry):
        late = [x_ref[position(span, r, blocks), :] * (SPAN - 1.0 - r) for r in range(SPAN - 1)]
        early = [b_ref[position(span, r, blocks), :] * float(r) for r in range(SPAN - 1, 0, -1)]
        factors = [run_ref[FACTOR, at(m), :] for m in range(modes)]
        for ref, terms in ((up_ref, late), (down_ref, early)):
            sums = [terms[0]] * modes
            for term in terms[1:]:
                sums = [f * s + term for f, s in zip(factors, sums)]
            for m in range(modes):
                ref[span, at(m), :] = factors[m] * sums[m]
        return carry

    def across(span, carry):
        begin = (span * SPAN).astype(jnp.float32)
        for m in range(modes):
            rows = at(m)
            far = run_ref[FAR, rows, :]
            up, down = up_ref[span, rows, :], down_ref[span, rows, :]
            head = hs_ref[span, rows, :]
            own = bs_ref[span, rows, :] - far * bs_ref[span + 1, rows, :]
            slope, power = run_ref[SLOPE, rows, :], run_ref[POWER, rows, :]
            run_ref[SUM0, rows, :] = run_ref[SUM0, rows, :] + head * own
            run_ref[SUM1, rows, :] = run_ref[SUM1, rows, :] + (slope * own + head * (own + down))
            run_ref[DOWN, rows, :] = run_ref[DOWN, rows, :] + power * (begin * own + down)
            run_ref[POWER, rows, :] = power * far
            run_ref[SLOPE, rows, :] = far * (slope + float(SPAN) * head) + up
        return carry

    lax.fori_loop(0, spans, near, 0)
    wait_all(fetch)
    lax.fori_loop(0, spans, across, 0)
    copies = send(0, lambda m: run_ref[DOWN, at(m), :], lambda m: run_ref[SLOPE, at(m), :])
    lags = [lag_ref[pl.ds(u * blocks, blocks), :] for u in range(SPAN)]
    factors = [run_ref[FACTOR, at(m), :] for m in range(modes)]
    plain = [lags[SPAN - 1]] * modes
    slope = [lags[SPAN - 1] * (SPAN - 1.0)] * modes
    for u in range(SPAN - 2, -1, -1):
        sloped = lags[u] * float(u)
        plain = [f * p + lags[u] for f, p in zip(factors, plain)]
        slope = [f * p + sloped for f, p in zip(factors, slope)]
    copies += send(
        1,
        lambda m: factors[m] * run_ref[SUM0, at(m), :] + plain[m],
        lambda m: factors[m] * run_ref[SUM1, at(m), :] + slope[m],
    )
    wait_all(copies)


def local_body(par_ref, x_ref, b_ref, skip_hbm, y_hbm, z_hbm, skip_ref, out_ref, skip_sem, sem):
    fetch = pltpu.make_async_copy(skip_hbm, skip_ref, skip_sem)
    fetch.start()
    blocks = skip_ref.shape[0]
    modes = par_ref.shape[0] // blocks // 2
    spans = x_ref.shape[0] // blocks // SPAN
    pieces = sem.shape[1]
    part = spans // pieces
    factors, terms = [], []
    for m in range(modes):
        rate = by_mode(par_ref, m, blocks)
        factors.append(jnp.exp(-rate))
        terms.append(by_mode(par_ref, modes + m, blocks) * jnp.sqrt(rate))
    kernel = []
    for u in range(SPAN):
        kernel.append(tree(terms))
        terms = [t * f for t, f in zip(terms, factors)]
    fetch.wait()
    kernel[0] = kernel[0] + skip_ref[...]

    def step(span, carry):
        def at(r):
            return pl.ds(pl.multiple_of((span * SPAN + r) * blocks, blocks), blocks)

        x = [x_ref[at(r), :] for r in range(SPAN)]
        for r in range(SPAN):
            out_ref[0, at(r), :] = tree([kernel[u] * x[r - u] for u in range(r + 1)])
        b = [b_ref[at(r), :] for r in range(SPAN)]
        for r in range(SPAN):
            out_ref[1, at(r), :] = tree([kernel[u] * b[r + u] for u in range(SPAN - r)])
        return carry

    copies = []
    for p in range(pieces):
        lax.fori_loop(p * part, (p + 1) * part, step, 0)
        rows = pl.ds(p * part * SPAN * blocks, part * SPAN * blocks)
        copies += start_all([
            pltpu.make_async_copy(out_ref.at[k, rows], ref.at[rows], sem.at[k, p]) for k, ref in enumerate((y_hbm, z_hbm))
        ])
    wait_all(copies)


def lane_is_first(shape, modes):
    return lax.broadcasted_iota(jnp.int32, shape, 1) % (2 * modes) < modes


def scan_body(s_ref, rate_ref, slopes_ref, out_ref, heads_ref, acc_ref, skip_ref, sem, *, modes, length):
    chunks, groups, rows = s_ref.shape[0], rate_ref.shape[0], s_ref.shape[2]
    first = lane_is_first((rows, LANES), modes)
    zero = jnp.zeros((rows, LANES), jnp.float32)
    copies = []
    for group in range(groups):
        alpha = jnp.exp(-float(length) * rate_ref[group])
        before, lead, total0, total1 = zero, zero, zero, zero
        heads = []
        for k in range(chunks):
            value = s_ref[k, group]
            later = pltpu.roll(value, LANES - modes, 1)
            heads.append(before)
            total0 += before * later
            total1 += (lead + before) * later
            lead = alpha * (lead + float(length) * before)
            before = alpha * before + value
        after = zero
        for k in reversed(range(chunks)):
            heads_ref[group, k] = jnp.where(first, heads[k], after)
            after = alpha * after + s_ref[k, group]
        copies += start_all([pltpu.make_async_copy(heads_ref.at[group], out_ref.at[:, group], sem.at[group])])
        acc_ref[group] = jnp.where(first, total0, pltpu.roll(total1, modes, 1))
    skip_ref[...] = tree([s_ref[k, groups, : skip_ref.shape[0]] for k in range(chunks)])
    wait_all(copies)


def slope_sum_body(r_ref, own_ref, acc_ref, rate_ref, done_ref, out_ref, pack_ref, sem, *, modes):
    chunks, groups, rows = r_ref.shape[0], rate_ref.shape[0], r_ref.shape[2]
    first = lane_is_first((rows, LANES), modes)
    span = 2 * modes
    fold = LANES // span
    row = lax.broadcasted_iota(jnp.int32, (rows, LANES), 0) % fold
    column = lax.broadcasted_iota(jnp.int32, (rows, LANES), 1) // span
    for group in range(groups):
        cross = tree([own_ref[group, k] * r_ref[k, groups + group] for k in range(chunks)])
        inner = tree([r_ref[k, 2 * groups + group] for k in range(chunks)])
        cross = jnp.where(first, 0.0, cross + pltpu.roll(cross, modes, 1))
        total = inner + jnp.exp(-rate_ref[group]) * (acc_ref[group] + cross)
        packed = total
        for shift in range(1, fold):
            moved = pltpu.roll(total, LANES - shift * span, 1)
            moved = jnp.where(row >= shift, pltpu.roll(moved, shift, 0), pltpu.roll(moved, rows - fold + shift, 0))
            packed = jnp.where((row - column + fold) % fold == shift, moved, packed)
        for block in range(fold):
            for r in range(rows // fold):
                pack_ref[group * fold + block, pl.ds(r, 1), :] = packed[r * fold + block : r * fold + block + 1]
    wait_all(start_all([pltpu.make_async_copy(pack_ref, out_ref.at[k], sem.at[k]) for k in range(out_ref.shape[0])]))


def final_body(g_ref, residue_ref, decay_ref, gres_ref, gdec_ref, spread_ref):
    modes = residue_ref.shape[0]
    owners, blocks, rows = g_ref.shape[0], g_ref.shape[1], g_ref.shape[2]
    span = 2 * modes
    fold = LANES // span
    total = tree([g_ref[:, block] for block in range(blocks)]).reshape(owners * rows, LANES)
    for k in range(fold):
        moved = total if k == 0 else pltpu.roll(total, LANES - k * span, 1)
        spread_ref[pl.ds(k, owners * rows, stride=fold), :] = moved
    sums = spread_ref[...].T
    plain, slope = sums[:modes], sums[modes:span]
    decay = decay_ref[...]
    root = jnp.sqrt(decay)
    gres_ref[...] = root * plain
    gdec_ref[...] = residue_ref[...] * root * (0.5 * plain - decay * slope)


def out_body(
    par_ref, r_ref, y_hbm, z_hbm, hs_hbm, bs_hbm, gate_hbm, key_hbm, value_hbm, cot_hbm,
    mixed_hbm, ggate_hbm, gkey_hbm, gvalue_hbm,
    hb_ref, run_ref, loc_ref, snap_ref, in_ref, out_ref, loc_sem, in_sem, out_sem,
):
    length, channels = gate_hbm.shape
    blocks = channels // LANES
    modes = par_ref.shape[0] // blocks // 2
    groups = hb_ref.shape[0] // LANES
    spans = length // SPAN
    pieces = loc_sem.shape[0]
    part = spans // pieces
    depth = part * SPAN
    fetch = []
    for p in range(pieces):
        mirror = pieces - 1 - p
        copies = []
        for kind, (place, local, snaps, shift, near) in enumerate((
            (p, y_hbm, hs_hbm, 0, (gate_hbm, cot_hbm)),
            (mirror, z_hbm, bs_hbm, 1, (value_hbm, key_hbm)),
        )):
            rows = pl.ds(place * depth * blocks, depth * blocks)
            copies.append(pltpu.make_async_copy(local.at[rows], loc_ref.at[kind, rows], loc_sem.at[p, 2 * kind]))
            source, target = pl.ds(place * part + shift, part), pl.ds(place * part, part)
            copies.append(
                pltpu.make_async_copy(snaps.at[source], snap_ref.at[kind, target], loc_sem.at[p, 2 * kind + 1])
            )
            rows = pl.ds(place * depth, depth)
            for k, ref in enumerate(near):
                slot = 2 * kind + k
                copies.append(pltpu.make_async_copy(ref.at[rows], in_ref.at[slot, rows], in_sem.at[p, slot]))
        fetch.append(start_all(copies))
    for group in range(groups):
        hb_ref[pl.ds(group * LANES, LANES), :] = r_ref[:, group].reshape(LANES, LANES).T
    FACTOR, FAR, WEIGHT, HEAD, TAIL = range(5)
    for m in range(modes):
        rows = pl.ds(m * blocks, blocks)
        rate = by_mode(par_ref, m, blocks)
        factor = jnp.exp(-rate)
        run_ref[FACTOR, rows, :] = factor
        run_ref[FAR, rows, :] = jnp.exp(-float(SPAN) * rate)
        run_ref[WEIGHT, rows, :] = by_mode(par_ref, modes + m, blocks) * jnp.sqrt(rate) * factor
        run_ref[HEAD, rows, :] = by_mode(hb_ref, m, blocks)
        run_ref[TAIL, rows, :] = by_mode(hb_ref, modes + m, blocks)

    def finish(kind, span, run):
        terms, factors = [], []
        for m in range(modes):
            rows = pl.ds(m * blocks, blocks)
            state = run_ref[run, rows, :]
            terms.append(run_ref[WEIGHT, rows, :] * (snap_ref[kind, span, rows, :] + state))
            run_ref[run, rows, :] = state * run_ref[FAR, rows, :]
            factors.append(run_ref[FACTOR, rows, :])
        for k in range(SPAN):
            r = k if kind == 0 else SPAN - 1 - k
            rows = pl.ds(pl.multiple_of((span * SPAN + r) * blocks, blocks), blocks)
            loc_ref[kind, rows, :] = loc_ref[kind, rows, :] + tree(terms)
            if k < SPAN - 1:
                terms = [t * f for t, f in zip(terms, factors)]
        rows = pl.ds(pl.multiple_of(span * SPAN, SPAN), SPAN)
        for block in range(blocks):
            lanes = pl.ds(block * LANES, LANES)
            total = jnp.concatenate(
                [
                    loc_ref[kind, pl.ds((span * SPAN + half * ROWS) * blocks + block, ROWS, stride=blocks), :]
                    for half in range(SPAN // ROWS)
                ],
                axis=0,
            )
            for slot in (2 * kind, 2 * kind + 1):
                value = in_ref[slot, rows, lanes].astype(jnp.float32) * total
                out_ref[slot, rows, lanes] = value.astype(jnp.bfloat16)

    def step(span, carry):
        finish(0, span, HEAD)
        finish(1, spans - 1 - span, TAIL)
        return carry

    stores = []
    for p in range(pieces):
        wait_all(fetch[p])
        lax.fori_loop(p * part, (p + 1) * part, step, 0)
        for slot, ref in enumerate((mixed_hbm, ggate_hbm, gkey_hbm, gvalue_hbm)):
            rows = pl.ds((p if slot < 2 else pieces - 1 - p) * depth, depth)
            stores += start_all([pltpu.make_async_copy(out_ref.at[slot, rows], ref.at[rows], out_sem.at[p, slot])])
    wait_all(stores)


def on_device(gate_in, key_in, value_in, cotangent, skip, residue, decay):
    f32, bf16 = jnp.float32, jnp.bfloat16
    owners = lax.axis_size("ctx")
    blocks = lax.axis_size("ch")
    length, channels = gate_in.shape
    filters, modes = residue.shape
    share = filters // owners
    groups = blocks * 2 * modes // LANES
    spans = length // SPAN
    pieces = 4
    place = lax.axis_index("ctx").astype(jnp.int32).reshape(1)
    whole = (length, channels)
    signal = (length * blocks, LANES)
    heads_at, tails_at = (spans, modes * blocks, LANES), (spans + 1, modes * blocks, LANES)
    size = length * channels
    sums = pltpu.VMEM((groups * LANES, LANES), f32)
    dense = pltpu.VMEM((4, *whole), bf16)
    tile = (share, LANES)

    (sent,) = call(
        spread_body,
        [((blocks, 2 * modes, LANES), f32, HBM)],
        4,
        (0, 10**5),
        [pltpu.VMEM((2 * modes, LANES), f32), DMA((2,)), DMA((blocks,))],
    )([HBM] * 2, decay.T, residue.T)
    params = lax.all_to_all(sent, "ch", 0, 0, tiled=True).reshape(blocks * 2 * modes, LANES)

    x, b, sk, lag = call(
        product_body,
        [(signal, f32, VMEM)] * 2 + [((blocks, LANES), f32, VMEM), ((SPAN * blocks, LANES), f32, VMEM)],
        16,
        (8 * size, 16 * size),
        [dense, DMA((pieces, 4))],
    )([HBM] * 4, gate_in, key_in, value_in, cotangent)

    states, head_states, tail_states = call(
        state_body,
        [((owners, groups + 1, *tile), f32, HBM), (heads_at, f32, HBM), (tails_at, f32, HBM)],
        16,
        (64 * size, 16 * size),
        [sums, pltpu.VMEM((groups + 1, owners, *tile), f32), pltpu.VMEM(heads_at, f32), pltpu.VMEM(tails_at, f32)]
        + [DMA((groups + 2,)), DMA((2, pieces))],
    )([VMEM] * 4, params, x, b, sk)
    states = lax.all_to_all(states, "ctx", 0, 0, tiled=True)

    slopes, rates = call(
        slope_body,
        [((owners, 3 * groups, *tile), f32, HBM), ((groups, *tile), f32, VMEM)],
        16,
        (100 * size, 16 * size),
        [pltpu.VMEM(heads_at, f32), pltpu.VMEM(tails_at, f32), pltpu.VMEM(heads_at, f32), pltpu.VMEM(heads_at, f32)]
        + [pltpu.VMEM((7, modes * blocks, LANES), f32), pltpu.VMEM((2, groups * LANES, LANES), f32)]
        + [pltpu.VMEM((2 * groups, owners, *tile), f32), sums, DMA((2 * groups,)), DMA((2,))],
    )([SMEM] + [VMEM] * 4 + [HBM] * 2, place, params, x, b, lag, head_states, tail_states)

    bundle, heads, acc, grad_skip = call(
        functools.partial(scan_body, modes=modes, length=length),
        [
            ((owners, 3 * groups, *tile), f32, HBM),
            ((groups, owners, *tile), f32, VMEM),
            ((groups, *tile), f32, VMEM),
            ((blocks, LANES), f32, VMEM),
        ],
        8,
        (10**5, 10**6),
        [DMA((groups,))],
        {2: 0},
    )([VMEM, VMEM, HBM], states, rates, slopes)
    arrived = lax.all_to_all(bundle, "ctx", 0, 0, tiled=True)

    y, z = call(
        local_body,
        [(signal, f32, HBM)] * 2,
        16,
        (40 * size, 16 * size),
        [pltpu.VMEM((blocks, LANES), f32), pltpu.VMEM((2, *signal), f32), DMA, DMA((2, pieces))],
    )([VMEM] * 3 + [HBM], params, x, b, skip.reshape(blocks, LANES))

    packed = (owners, blocks, share * 2 * modes // LANES, LANES)
    (grads,) = call(
        functools.partial(slope_sum_body, modes=modes),
        [(packed, f32, HBM)],
        8,
        (10**5, 10**6),
        [pltpu.VMEM(packed[1:], f32), DMA((owners,))],
    )([VMEM] * 4 + [HBM], arrived, heads, acc, rates, y)
    grads = lax.all_to_all(grads.reshape(owners * blocks, *packed[2:]), ("ctx", "ch"), 0, 0, tiled=True)

    mixed, grad_gate, grad_key, grad_value = call(
        out_body,
        [(whole, bf16, HBM)] * 4,
        24,
        (64 * size, 32 * size),
        [sums, pltpu.VMEM((5, modes * blocks, LANES), f32), pltpu.VMEM((2, *signal), f32)]
        + [pltpu.VMEM((2, *heads_at), f32), dense, dense, DMA((pieces, 4)), DMA((pieces, 4)), DMA((pieces, 4))],
    )([VMEM] * 2 + [HBM] * 8, params, arrived, y, z, head_states, tail_states, gate_in, key_in, value_in, cotangent)

    grad_residue, grad_log_decay = call(
        final_body, [((modes, filters), f32, VMEM)] * 2, 8, (10**5, 10**6), [pltpu.VMEM((LANES, LANES), f32)]
    )([VMEM] * 3, grads.reshape(packed), residue.T, decay.T)
    return (mixed, grad_gate, grad_key, grad_value, grad_skip.reshape(channels), grad_residue.T, grad_log_decay.T)


def solution(mesh):
    rows = P("ctx", "ch")
    return jax.shard_map(
        on_device,
        mesh=mesh,
        in_specs=(rows, rows, rows, rows, P("ch"), P("ch", None), P("ch", None)),
        out_specs=(rows, rows, rows, rows, P("ch"), P("ch", None), P("ch", None)),
        check_vma=False,
    )
```

```python
import functools

import jax
import jax.numpy as jnp
from jax import lax
from jax.experimental import pallas as pl
from jax.experimental.pallas import tpu as pltpu
from jax.sharding import PartitionSpec as P

LANES = 128
ROWS = 8
SPAN = 16
VMEM = pl.BlockSpec(memory_space=pltpu.VMEM)
SMEM = pl.BlockSpec(memory_space=pltpu.SMEM)
HBM = pl.BlockSpec(memory_space=pltpu.HBM)
DMA = pltpu.SemaphoreType.DMA


def call(body, outs, limit_mib, cost, scratch=(), aliases=None):
    flops, moved = cost
    return lambda specs, *args: pl.pallas_call(
        body,
        out_shape=[pltpu.HBM(s, t) if w is HBM else jax.ShapeDtypeStruct(s, t) for s, t, w in outs],
        in_specs=list(specs),
        out_specs=[w for _, _, w in outs],
        scratch_shapes=list(scratch),
        input_output_aliases=aliases or {},
        compiler_params=pltpu.CompilerParams(vmem_limit_bytes=limit_mib * 2**20),
        cost_estimate=pl.CostEstimate(flops=flops, bytes_accessed=moved, transcendentals=0),
    )(*(pltpu.with_memory_space_constraint(a, pltpu.HBM) if w is HBM else a for w, a in zip(specs, args)))


def start_all(copies):
    for copy in copies:
        copy.start()
    return copies


def wait_all(copies):
    for copy in copies:
        copy.wait()


def spread_body(decay_ref, residue_ref, out_ref, held_ref, in_sem, out_sem):
    modes, blocks = decay_ref.shape[0], out_ref.shape[0]
    wait_all(
        start_all([
            pltpu.make_async_copy(ref, held_ref.at[pl.ds(k * modes, modes)], in_sem.at[k])
            for k, ref in enumerate((decay_ref, residue_ref))
        ])
    )
    wait_all(start_all([pltpu.make_async_copy(held_ref, out_ref.at[k], out_sem.at[k]) for k in range(blocks)]))


def tree(values):
    while len(values) > 1:
        odd = values[-1:] if len(values) % 2 else []
        values = [a + b for a, b in zip(values[::2], values[1::2])] + odd
    return values[0]


def turned(scratch_ref, group, owners):
    return scratch_ref[pl.ds(group * LANES, LANES), :].T.reshape(owners, LANES // owners, LANES)


def by_mode(ref, row, blocks):
    return ref[pl.ds(row, blocks, stride=ref.shape[0] // blocks), :]


def position(span, offset, blocks):
    return pl.ds(pl.multiple_of((span * SPAN + offset) * blocks, blocks), blocks)


def product_body(
    gate_hbm, key_hbm, value_hbm, cot_hbm,
    x_ref, b_ref, sk_ref, lag_ref,
    in_ref, sem,
):
    length, channels = gate_hbm.shape
    blocks = channels // LANES
    pieces = sem.shape[0]
    depth = length // pieces
    fetch = [
        start_all([
            pltpu.make_async_copy(ref.at[pl.ds(p * depth, depth)], in_ref.at[k, pl.ds(p * depth, depth)], sem.at[p, k])
            for k, ref in enumerate((gate_hbm, key_hbm, value_hbm, cot_hbm))
        ])
        for p in range(pieces)
    ]
    lag_ref[...] = jnp.zeros(lag_ref.shape, jnp.float32)

    def step(place, sums):
        rows = pl.ds(pl.multiple_of(place * SPAN, SPAN), SPAN)
        after = []
        for block in range(blocks):
            lanes = pl.ds(block * LANES, LANES)
            gate, key, value, cot = (in_ref[k, rows, lanes].astype(jnp.float32) for k in range(4))
            x, b = key * value, cot * gate
            for part in range(SPAN // ROWS):
                target = pl.ds((place * SPAN + part * ROWS) * blocks + block, ROWS, stride=blocks)
                x_ref[target, :] = x[part * ROWS : (part + 1) * ROWS]
                b_ref[target, :] = b[part * ROWS : (part + 1) * ROWS]
            both = x * b
            after.append(sums[block] + tree([both[k * ROWS : (k + 1) * ROWS] for k in range(SPAN // ROWS)]))
        return tuple(after)

    def lags(span, carry):
        x = [x_ref[position(span, r, blocks), :] for r in range(SPAN)]
        b = [b_ref[position(span, r, blocks), :] for r in range(SPAN)]
        for u in range(SPAN):
            rows = pl.ds(u * blocks, blocks)
            lag_ref[rows, :] = lag_ref[rows, :] + tree([b[r + u] * x[r] for r in range(SPAN - u)])
        return carry

    sums = tuple(jnp.zeros((ROWS, LANES), jnp.float32) for _ in range(blocks))
    for p in range(pieces):
        wait_all(fetch[p])
        sums = lax.fori_loop(p * depth // SPAN, (p + 1) * depth // SPAN, step, sums)
        lax.fori_loop(p * depth // SPAN, (p + 1) * depth // SPAN, lags, 0)
    for block in range(blocks):
        sk_ref[pl.ds(block, 1), :] = jnp.sum(sums[block], axis=0, keepdims=True)


def part_slices(core, turned_ref, keep_ref, send_ref):
    for chip in range(keep_ref.shape[0]):
        keep_ref[chip] = turned_ref[2 * chip + core]
        send_ref[chip] = turned_ref[2 * chip + 1 - core]


def state_body(
    core_ref, par_ref, x_ref, b_ref, sk_ref,
    out_ref, hs_hbm, bs_hbm, keep_ref, send_ref, edge_ref,
    sums_ref, turn_ref, hs_ref, bs_ref, sem, snap_sem,
):
    owners = out_ref.shape[0]
    groups = sums_ref.shape[0] // LANES
    blocks = sk_ref.shape[0]
    modes = par_ref.shape[0] // blocks // 2
    spans = hs_ref.shape[0]
    pieces = snap_sem.shape[1]
    part = spans // pieces
    for owner in range(owners):
        turn_ref[groups, owner, :blocks] = sk_ref[...]
    copies = start_all([pltpu.make_async_copy(turn_ref.at[groups], out_ref.at[:, groups], sem.at[groups])])
    factor = [jnp.exp(-by_mode(par_ref, m, blocks)) for m in range(modes)]

    def step(span, carry):
        ups, downs = carry
        mirror = spans - 1 - span
        for m in range(modes):
            hs_ref[span, pl.ds(m * blocks, blocks), :] = ups[m]
            bs_ref[mirror + 1, pl.ds(m * blocks, blocks), :] = downs[m]
        for r in range(SPAN):
            x = x_ref[pl.ds(pl.multiple_of((span * SPAN + r) * blocks, blocks), blocks), :]
            b = b_ref[pl.ds(pl.multiple_of((mirror * SPAN + SPAN - 1 - r) * blocks, blocks), blocks), :]
            ups = tuple(f * u + x for f, u in zip(factor, ups))
            downs = tuple(f * d + b for f, d in zip(factor, downs))
        return ups, downs

    zero = tuple(jnp.zeros((blocks, LANES), jnp.float32) for _ in range(modes))
    ups, downs = zero, zero
    for p in range(pieces):
        ups, downs = lax.fori_loop(p * part, (p + 1) * part, step, (ups, downs))
        here, there = pl.ds(p * part, part), pl.ds((pieces - 1 - p) * part + 1, part)
        copies += start_all([
            pltpu.make_async_copy(hs_ref.at[here], hs_hbm.at[here], snap_sem.at[0, p]),
            pltpu.make_async_copy(bs_ref.at[there], bs_hbm.at[there], snap_sem.at[1, p]),
        ])
    for m in range(modes):
        bs_ref[0, pl.ds(m * blocks, blocks), :] = downs[m]
        edge_ref[pl.ds(m * blocks, blocks), :] = jnp.where(core_ref[0] == 0, ups[m], downs[m])
        sums_ref[pl.ds(m, blocks, stride=2 * modes), :] = ups[m]
        sums_ref[pl.ds(modes + m, blocks, stride=2 * modes), :] = downs[m]
    copies += start_all([pltpu.make_async_copy(bs_ref.at[0], bs_hbm.at[0], sem.at[groups + 1])])
    for group in range(groups):
        turn_ref[group] = turned(sums_ref, group, owners)
        copies += start_all([pltpu.make_async_copy(turn_ref.at[group], out_ref.at[:, group], sem.at[group])])
    for group in range(groups):
        part_slices(core_ref[0], turn_ref.at[group], keep_ref.at[group], send_ref.at[group])
    wait_all(copies)


def slope_body(
    index_ref, core_ref, par_ref, x_ref, b_ref, lag_ref, hs_hbm, bs_hbm,
    rate_ref, side_rate_ref, keep_a_ref, send_a_ref, keep_b_ref, send_b_ref,
    hs_ref, bs_ref, up_ref, down_ref, run_ref, sums_ref, turn_ref, rates_ref, snap_sem,
):
    owners = turn_ref.shape[0]
    groups = sums_ref.shape[0] // LANES
    spans = hs_ref.shape[0]
    blocks = lag_ref.shape[0] // SPAN
    modes = par_ref.shape[0] // blocks // 2
    fetch = start_all([
        pltpu.make_async_copy(hs_hbm, hs_ref, snap_sem.at[0]),
        pltpu.make_async_copy(bs_hbm, bs_ref, snap_sem.at[1]),
    ])
    share = rate_ref.shape[1]
    zero = jnp.zeros((blocks, LANES), jnp.float32)
    SLOPE, SUM0, SUM1, DOWN, POWER, FACTOR, FAR = range(7)
    for m in range(modes):
        rate = by_mode(par_ref, m, blocks)
        rows = pl.ds(m * blocks, blocks)
        for kind in (SLOPE, SUM0, SUM1, DOWN):
            run_ref[kind, rows, :] = zero
        run_ref[POWER, rows, :] = zero + 1.0
        run_ref[FACTOR, rows, :] = jnp.exp(-rate)
        run_ref[FAR, rows, :] = jnp.exp(-float(SPAN) * rate)

    def part(first, second, keep_ref, send_ref):
        for m in range(modes):
            sums_ref[pl.ds(m, blocks, stride=2 * modes), :] = first(m)
            sums_ref[pl.ds(modes + m, blocks, stride=2 * modes), :] = second(m)
        for group in range(groups):
            turn_ref[...] = turned(sums_ref, group, owners)
            part_slices(core_ref[0], turn_ref, keep_ref.at[group], send_ref.at[group])

    def at(m):
        return pl.ds(m * blocks, blocks)

    for group in range(groups):
        for block in range(group * blocks // groups, (group + 1) * blocks // groups):
            decay = par_ref[pl.ds(block * 2 * modes, modes), :]
            rates_ref[pl.ds(block * 2 * modes, 2 * modes), :] = jnp.concatenate([decay, decay], axis=0)
        rates_ref[pl.ds(group * LANES, LANES), :] = rates_ref[pl.ds(group * LANES, LANES), :].T
        rate_ref[group] = rates_ref[pl.ds(pl.multiple_of(group * LANES + index_ref[0] * share, share), share), :]
        for chip in range(side_rate_ref.shape[1]):
            start = group * LANES + (2 * chip + core_ref[0]) * share
            side_rate_ref[group, chip] = rates_ref[pl.ds(pl.multiple_of(start, share), share), :]

    def near(span, carry):
        late = [x_ref[position(span, r, blocks), :] * (SPAN - 1.0 - r) for r in range(SPAN - 1)]
        early = [b_ref[position(span, r, blocks), :] * float(r) for r in range(SPAN - 1, 0, -1)]
        factors = [run_ref[FACTOR, at(m), :] for m in range(modes)]
        for ref, terms in ((up_ref, late), (down_ref, early)):
            sums = [terms[0]] * modes
            for term in terms[1:]:
                sums = [f * s + term for f, s in zip(factors, sums)]
            for m in range(modes):
                ref[span, at(m), :] = factors[m] * sums[m]
        return carry

    def across(span, carry):
        begin = (span * SPAN).astype(jnp.float32)
        for m in range(modes):
            rows = at(m)
            far = run_ref[FAR, rows, :]
            up, down = up_ref[span, rows, :], down_ref[span, rows, :]
            head = hs_ref[span, rows, :]
            own = bs_ref[span, rows, :] - far * bs_ref[span + 1, rows, :]
            slope, power = run_ref[SLOPE, rows, :], run_ref[POWER, rows, :]
            run_ref[SUM0, rows, :] = run_ref[SUM0, rows, :] + head * own
            run_ref[SUM1, rows, :] = run_ref[SUM1, rows, :] + (slope * own + head * (own + down))
            run_ref[DOWN, rows, :] = run_ref[DOWN, rows, :] + power * (begin * own + down)
            run_ref[POWER, rows, :] = power * far
            run_ref[SLOPE, rows, :] = far * (slope + float(SPAN) * head) + up
        return carry

    lax.fori_loop(0, spans, near, 0)
    wait_all(fetch)
    lax.fori_loop(0, spans, across, 0)
    part(lambda m: run_ref[DOWN, at(m), :], lambda m: run_ref[SLOPE, at(m), :], keep_a_ref, send_a_ref)
    lags = [lag_ref[pl.ds(u * blocks, blocks), :] for u in range(SPAN)]
    factors = [run_ref[FACTOR, at(m), :] for m in range(modes)]
    plain = [lags[SPAN - 1]] * modes
    slope = [lags[SPAN - 1] * (SPAN - 1.0)] * modes
    for u in range(SPAN - 2, -1, -1):
        sloped = lags[u] * float(u)
        plain = [f * p + lags[u] for f, p in zip(factors, plain)]
        slope = [f * p + sloped for f, p in zip(factors, slope)]
    part(
        lambda m: factors[m] * run_ref[SUM0, at(m), :] + plain[m],
        lambda m: factors[m] * run_ref[SUM1, at(m), :] + slope[m],
        keep_b_ref,
        send_b_ref,
    )


def pair_body(
    core_ref, a_ref, a_other_ref, b_ref, b_other_ref, s_ref, s_other_ref, rate_ref,
    out_hbm, held_ref, sem,
    *, modes, length,
):
    groups, chips, rows = s_ref.shape[0], s_ref.shape[1], s_ref.shape[2]
    first = lane_is_first((rows, LANES), modes)
    low = core_ref[0] == 0

    def turn(value):
        return jnp.where(first, pltpu.roll(value, LANES - modes, 1), pltpu.roll(value, modes, 1))

    copies = []
    for group in range(groups):
        for chip in range(chips):
            def both(own_ref, other_ref):
                own, other = own_ref[group, chip], other_ref[group, chip]
                return jnp.where(low, own, other), jnp.where(low, other, own)

            (a0, a1), (b0, b1), (s0, s1) = both(a_ref, a_other_ref), both(b_ref, b_other_ref), both(s_ref, s_other_ref)
            rate = rate_ref[group, chip]
            far, factor = jnp.exp(-float(length) * rate), jnp.exp(-rate)
            later = turn(s1)
            held_ref[0, group, chip] = jnp.where(
                first, a0 + far * (a1 + float(length) * later), far * (a0 + float(length) * turn(s0)) + a1
            )
            cross = s0 * later
            slope = pltpu.roll(cross + s0 * a1, modes, 1) + a0 * s1
            held_ref[1, group, chip] = b0 + b1 + factor * jnp.where(first, cross, slope)
        copies += start_all([
            pltpu.make_async_copy(held_ref.at[k, group], out_hbm.at[:, (k + 1) * groups + group], sem.at[k, group])
            for k in range(2)
        ])
    wait_all(copies)


def local_body(par_ref, x_ref, b_ref, skip_hbm, y_hbm, z_hbm, skip_ref, out_ref, skip_sem, sem):
    fetch = pltpu.make_async_copy(skip_hbm, skip_ref, skip_sem)
    fetch.start()
    blocks = skip_ref.shape[0]
    modes = par_ref.shape[0] // blocks // 2
    spans = x_ref.shape[0] // blocks // SPAN
    pieces = sem.shape[1]
    part = spans // pieces
    factors, terms = [], []
    for m in range(modes):
        rate = by_mode(par_ref, m, blocks)
        factors.append(jnp.exp(-rate))
        terms.append(by_mode(par_ref, modes + m, blocks) * jnp.sqrt(rate))
    kernel = []
    for u in range(SPAN):
        kernel.append(tree(terms))
        terms = [t * f for t, f in zip(terms, factors)]
    fetch.wait()
    kernel[0] = kernel[0] + skip_ref[...]

    def step(span, carry):
        def at(r):
            return pl.ds(pl.multiple_of((span * SPAN + r) * blocks, blocks), blocks)

        x = [x_ref[at(r), :] for r in range(SPAN)]
        for r in range(SPAN):
            out_ref[0, at(r), :] = tree([kernel[u] * x[r - u] for u in range(r + 1)])
        b = [b_ref[at(r), :] for r in range(SPAN)]
        for r in range(SPAN):
            out_ref[1, at(r), :] = tree([kernel[u] * b[r + u] for u in range(SPAN - r)])
        return carry

    copies = []
    for p in range(pieces):
        lax.fori_loop(p * part, (p + 1) * part, step, 0)
        rows = pl.ds(p * part * SPAN * blocks, part * SPAN * blocks)
        copies += start_all([
            pltpu.make_async_copy(out_ref.at[k, rows], ref.at[rows], sem.at[k, p]) for k, ref in enumerate((y_hbm, z_hbm))
        ])
    wait_all(copies)


def lane_is_first(shape, modes):
    return lax.broadcasted_iota(jnp.int32, shape, 1) % (2 * modes) < modes


def scan_body(s_ref, rate_ref, slopes_ref, out_ref, heads_ref, acc_ref, skip_ref, sem, *, modes, length):
    chunks, groups, rows = s_ref.shape[0], rate_ref.shape[0], s_ref.shape[2]
    first = lane_is_first((rows, LANES), modes)
    zero = jnp.zeros((rows, LANES), jnp.float32)
    copies = []
    for group in range(groups):
        near = jnp.exp(-float(length) * rate_ref[group])
        alpha = near * near
        pairs = [(s_ref[k, group], s_ref[k + 1, group]) for k in range(0, chunks, 2)]
        pairs = [jnp.where(first, near * early + late, early + near * late) for early, late in pairs]
        before, lead, total0, total1 = zero, zero, zero, zero
        heads = []
        for value in pairs:
            later = pltpu.roll(value, LANES - modes, 1)
            heads.append(before)
            total0 += before * later
            total1 += (lead + before) * later
            lead = alpha * (lead + 2.0 * length * before)
            before = alpha * before + value
        after = zero
        for k in reversed(range(len(pairs))):
            heads_ref[group, k] = jnp.where(first, heads[k], after)
            after = alpha * after + pairs[k]
        copies += start_all([pltpu.make_async_copy(heads_ref.at[group], out_ref.at[:, group], sem.at[group])])
        acc_ref[group] = jnp.where(first, total0, pltpu.roll(total1, modes, 1))
    skip_ref[...] = tree([s_ref[k, groups, : skip_ref.shape[0]] for k in range(chunks)])
    wait_all(copies)


def slope_sum_body(r_ref, own_ref, acc_ref, rate_ref, done_ref, out_ref, ends_ref, pack_ref, sem, *, modes):
    chunks, groups, rows = r_ref.shape[0], rate_ref.shape[0], r_ref.shape[2]
    first = lane_is_first((rows, LANES), modes)
    span = 2 * modes
    fold = LANES // span
    row = lax.broadcasted_iota(jnp.int32, (rows, LANES), 0) % fold
    column = lax.broadcasted_iota(jnp.int32, (rows, LANES), 1) // span
    for group in range(groups):
        cross = tree([own_ref[group, k] * r_ref[k, groups + group] for k in range(chunks)])
        inner = tree([r_ref[k, 2 * groups + group] for k in range(chunks)])
        cross = jnp.where(first, 0.0, cross + pltpu.roll(cross, modes, 1))
        total = inner + jnp.exp(-rate_ref[group]) * (acc_ref[group] + cross)
        packed = total
        for shift in range(1, fold):
            moved = pltpu.roll(total, LANES - shift * span, 1)
            moved = jnp.where(row >= shift, pltpu.roll(moved, shift, 0), pltpu.roll(moved, rows - fold + shift, 0))
            packed = jnp.where((row - column + fold) % fold == shift, moved, packed)
        for block in range(fold):
            for r in range(rows // fold):
                pack_ref[group * fold + block, pl.ds(r, 1), :] = packed[r * fold + block : r * fold + block + 1]
    copies = start_all([pltpu.make_async_copy(pack_ref, out_ref.at[k], sem.at[k]) for k in range(out_ref.shape[0])])
    for group in range(groups):
        ends_ref[group] = r_ref[:, group]
    wait_all(copies)


def final_body(g_ref, residue_ref, decay_ref, gres_ref, gdec_ref, spread_ref):
    modes = residue_ref.shape[0]
    owners, blocks, rows = g_ref.shape[0], g_ref.shape[1], g_ref.shape[2]
    span = 2 * modes
    fold = LANES // span
    total = tree([g_ref[:, block] for block in range(blocks)]).reshape(owners * rows, LANES)
    for k in range(fold):
        moved = total if k == 0 else pltpu.roll(total, LANES - k * span, 1)
        spread_ref[pl.ds(k, owners * rows, stride=fold), :] = moved
    sums = spread_ref[...].T
    plain, slope = sums[:modes], sums[modes:span]
    decay = decay_ref[...]
    root = jnp.sqrt(decay)
    gres_ref[...] = root * plain
    gdec_ref[...] = residue_ref[...] * root * (0.5 * plain - decay * slope)


def out_body(
    core_ref, par_ref, ends_ref, other_ref, edge_ref, skip_ref, y_hbm, z_hbm, hs_hbm, bs_hbm, gate_hbm, key_hbm, value_hbm, cot_hbm,
    mixed_hbm, ggate_hbm, gkey_hbm, gvalue_hbm, gskip_ref,
    hb_ref, run_ref, loc_ref, snap_ref, in_ref, out_ref, mix_ref, loc_sem, in_sem, out_sem,
):
    length, channels = gate_hbm.shape
    blocks = channels // LANES
    modes = par_ref.shape[0] // blocks // 2
    groups = hb_ref.shape[0] // LANES
    spans = length // SPAN
    pieces = loc_sem.shape[0]
    part = spans // pieces
    depth = part * SPAN
    fetch = []
    for p in range(pieces):
        mirror = pieces - 1 - p
        copies = []
        for kind, (place, local, snaps, shift, near) in enumerate((
            (p, y_hbm, hs_hbm, 0, (gate_hbm, cot_hbm)),
            (mirror, z_hbm, bs_hbm, 1, (value_hbm, key_hbm)),
        )):
            rows = pl.ds(place * depth * blocks, depth * blocks)
            copies.append(pltpu.make_async_copy(local.at[rows], loc_ref.at[kind, rows], loc_sem.at[p, 2 * kind]))
            source, target = pl.ds(place * part + shift, part), pl.ds(place * part, part)
            copies.append(
                pltpu.make_async_copy(snaps.at[source], snap_ref.at[kind, target], loc_sem.at[p, 2 * kind + 1])
            )
            rows = pl.ds(place * depth, depth)
            for k, ref in enumerate(near):
                slot = 2 * kind + k
                copies.append(pltpu.make_async_copy(ref.at[rows], in_ref.at[slot, rows], in_sem.at[p, slot]))
        fetch.append(start_all(copies))
    gskip_ref[...] = skip_ref[...]
    low = core_ref[0] == 0
    for group in range(groups):
        for chip in range(ends_ref.shape[1]):
            own, other = ends_ref[group, chip], other_ref[group, chip]
            mix_ref[2 * chip] = jnp.where(low, own, other)
            mix_ref[2 * chip + 1] = jnp.where(low, other, own)
        hb_ref[pl.ds(group * LANES, LANES), :] = mix_ref[...].reshape(LANES, LANES).T
    FACTOR, FAR, WEIGHT, HEAD, TAIL = range(5)
    for m in range(modes):
        rows = pl.ds(m * blocks, blocks)
        rate = by_mode(par_ref, m, blocks)
        factor = jnp.exp(-rate)
        run_ref[FACTOR, rows, :] = factor
        run_ref[FAR, rows, :] = jnp.exp(-float(SPAN) * rate)
        run_ref[WEIGHT, rows, :] = by_mode(par_ref, modes + m, blocks) * jnp.sqrt(rate) * factor
        head, tail, edge = by_mode(hb_ref, m, blocks), by_mode(hb_ref, modes + m, blocks), edge_ref[rows, :]
        chunk = jnp.exp(-float(length) * rate)
        run_ref[HEAD, rows, :] = jnp.where(low, head, chunk * head + edge)
        run_ref[TAIL, rows, :] = jnp.where(low, chunk * tail + edge, tail)

    def finish(kind, span, run):
        terms, factors = [], []
        for m in range(modes):
            rows = pl.ds(m * blocks, blocks)
            state = run_ref[run, rows, :]
            terms.append(run_ref[WEIGHT, rows, :] * (snap_ref[kind, span, rows, :] + state))
            run_ref[run, rows, :] = state * run_ref[FAR, rows, :]
            factors.append(run_ref[FACTOR, rows, :])
        for k in range(SPAN):
            r = k if kind == 0 else SPAN - 1 - k
            rows = pl.ds(pl.multiple_of((span * SPAN + r) * blocks, blocks), blocks)
            loc_ref[kind, rows, :] = loc_ref[kind, rows, :] + tree(terms)
            if k < SPAN - 1:
                terms = [t * f for t, f in zip(terms, factors)]
        rows = pl.ds(pl.multiple_of(span * SPAN, SPAN), SPAN)
        for block in range(blocks):
            lanes = pl.ds(block * LANES, LANES)
            total = jnp.concatenate(
                [
                    loc_ref[kind, pl.ds((span * SPAN + half * ROWS) * blocks + block, ROWS, stride=blocks), :]
                    for half in range(SPAN // ROWS)
                ],
                axis=0,
            )
            for slot in (2 * kind, 2 * kind + 1):
                value = in_ref[slot, rows, lanes].astype(jnp.float32) * total
                out_ref[slot, rows, lanes] = value.astype(jnp.bfloat16)

    def step(span, carry):
        finish(0, span, HEAD)
        finish(1, spans - 1 - span, TAIL)
        return carry

    stores = []
    for p in range(pieces):
        wait_all(fetch[p])
        lax.fori_loop(p * part, (p + 1) * part, step, 0)
        for slot, ref in enumerate((mixed_hbm, ggate_hbm, gkey_hbm, gvalue_hbm)):
            rows = pl.ds((p if slot < 2 else pieces - 1 - p) * depth, depth)
            stores += start_all([pltpu.make_async_copy(out_ref.at[slot, rows], ref.at[rows], out_sem.at[p, slot])])
    wait_all(stores)


def on_device(gate_in, key_in, value_in, cotangent, skip, residue, decay):
    f32, bf16 = jnp.float32, jnp.bfloat16
    chips, cores = lax.axis_size("chip"), lax.axis_size("core")
    ctx = ("chip", "core")
    owners = chips * cores
    blocks = lax.axis_size("ch")
    length, channels = gate_in.shape
    filters, modes = residue.shape
    share = filters // owners
    groups = blocks * 2 * modes // LANES
    spans = length // SPAN
    pieces = 4
    place = lax.axis_index(ctx).astype(jnp.int32).reshape(1)
    core = lax.axis_index("core").astype(jnp.int32).reshape(1)

    def change(value):
        return lax.ppermute(value, "core", [(i, cores - 1 - i) for i in range(cores)])

    whole = (length, channels)
    signal = (length * blocks, LANES)
    heads_at, tails_at = (spans, modes * blocks, LANES), (spans + 1, modes * blocks, LANES)
    size = length * channels
    sums = pltpu.VMEM((groups * LANES, LANES), f32)
    dense = pltpu.VMEM((4, *whole), bf16)
    tile = (share, LANES)

    (sent,) = call(
        spread_body,
        [((blocks, 2 * modes, LANES), f32, HBM)],
        4,
        (0, 10**5),
        [pltpu.VMEM((2 * modes, LANES), f32), DMA((2,)), DMA((blocks,))],
    )([HBM] * 2, decay.T, residue.T)
    params = lax.all_to_all(sent, "ch", 0, 0, tiled=True).reshape(blocks * 2 * modes, LANES)

    x, b, sk, lag = call(
        product_body,
        [(signal, f32, VMEM)] * 2 + [((blocks, LANES), f32, VMEM), ((SPAN * blocks, LANES), f32, VMEM)],
        16,
        (8 * size, 16 * size),
        [dense, DMA((pieces, 4))],
    )([HBM] * 4, gate_in, key_in, value_in, cotangent)

    side = (groups, chips, *tile)
    states, head_states, tail_states, own_s, send_s, edge = call(
        state_body,
        [((owners, groups + 1, *tile), f32, HBM), (heads_at, f32, HBM), (tails_at, f32, HBM)]
        + [(side, f32, VMEM)] * 2
        + [((modes * blocks, LANES), f32, VMEM)],
        16,
        (64 * size, 16 * size),
        [sums, pltpu.VMEM((groups + 1, owners, *tile), f32), pltpu.VMEM(heads_at, f32), pltpu.VMEM(tails_at, f32)]
        + [DMA((groups + 2,)), DMA((2, pieces))],
    )([SMEM] + [VMEM] * 4, core, params, x, b, sk)
    states = lax.all_to_all(states, ctx, 0, 0, tiled=True)

    rates, side_rates, own_a, send_a, own_b, send_b = call(
        slope_body,
        [((groups, *tile), f32, VMEM)] + [(side, f32, VMEM)] * 5,
        16,
        (100 * size, 16 * size),
        [pltpu.VMEM(heads_at, f32), pltpu.VMEM(tails_at, f32), pltpu.VMEM(heads_at, f32), pltpu.VMEM(heads_at, f32)]
        + [pltpu.VMEM((7, modes * blocks, LANES), f32), sums, pltpu.VMEM((owners, *tile), f32), sums, DMA((2,))],
    )([SMEM] * 2 + [VMEM] * 4 + [HBM] * 2, place, core, params, x, b, lag, head_states, tail_states)

    (slopes,) = call(
        functools.partial(pair_body, modes=modes, length=length),
        [((chips, 3 * groups, *tile), f32, HBM)],
        8,
        (size, size),
        [pltpu.VMEM((2, *side), f32), DMA((2, groups))],
    )([SMEM] + [VMEM] * 7, core, own_a, change(send_a), own_b, change(send_b), own_s, change(send_s), side_rates)

    bundle, heads, acc, sum_skip = call(
        functools.partial(scan_body, modes=modes, length=length),
        [
            ((chips, 3 * groups, *tile), f32, HBM),
            (side, f32, VMEM),
            ((groups, *tile), f32, VMEM),
            ((blocks, LANES), f32, VMEM),
        ],
        8,
        (10**5, 10**6),
        [DMA((groups,))],
        {2: 0},
    )([VMEM, VMEM, HBM], states, rates, slopes)
    arrived = lax.all_to_all(bundle, "chip", 0, 0, tiled=True)

    y, z = call(
        local_body,
        [(signal, f32, HBM)] * 2,
        16,
        (40 * size, 16 * size),
        [pltpu.VMEM((blocks, LANES), f32), pltpu.VMEM((2, *signal), f32), DMA, DMA((2, pieces))],
    )([VMEM] * 3 + [HBM], params, x, b, skip.reshape(blocks, LANES))

    packed = (owners, blocks, share * 2 * modes // LANES, LANES)
    grads, ends = call(
        functools.partial(slope_sum_body, modes=modes),
        [(packed, f32, HBM), (side, f32, VMEM)],
        8,
        (10**5, 10**6),
        [pltpu.VMEM(packed[1:], f32), DMA((owners,))],
    )([VMEM] * 4 + [HBM], arrived, heads, acc, rates, y)
    grads = lax.all_to_all(grads.reshape(owners * blocks, *packed[2:]), ("chip", "core", "ch"), 0, 0, tiled=True)

    mixed, grad_gate, grad_key, grad_value, grad_skip = call(
        out_body,
        [(whole, bf16, HBM)] * 4 + [((blocks, LANES), f32, VMEM)],
        24,
        (64 * size, 32 * size),
        [sums, pltpu.VMEM((5, modes * blocks, LANES), f32), pltpu.VMEM((2, *signal), f32)]
        + [pltpu.VMEM((2, *heads_at), f32), dense, dense, pltpu.VMEM((owners, *tile), f32)]
        + [DMA((pieces, 4)), DMA((pieces, 4)), DMA((pieces, 4))],
    )(
        [SMEM] + [VMEM] * 5 + [HBM] * 8,
        core, params, ends, change(ends), change(edge), sum_skip, y, z, head_states, tail_states, gate_in, key_in, value_in, cotangent,
    )

    grad_residue, grad_log_decay = call(
        final_body, [((modes, filters), f32, VMEM)] * 2, 8, (10**5, 10**6), [pltpu.VMEM((LANES, LANES), f32)]
    )([VMEM] * 3, grads.reshape(packed), residue.T, decay.T)
    return (mixed, grad_gate, grad_key, grad_value, grad_skip.reshape(channels), grad_residue.T, grad_log_decay.T)


def solution(mesh):
    cores = 2
    shape = (mesh.shape["ctx"] // cores, cores, mesh.shape["ch"])
    split = jax.sharding.Mesh(mesh.devices.reshape(shape), ("chip", "core", "ch"))
    rows = P(("chip", "core"), "ch")
    specs = (rows, rows, rows, rows, P("ch"), P("ch", None), P("ch", None))
    return jax.shard_map(on_device, mesh=split, in_specs=specs, out_specs=specs, check_vma=False)
```

```python
import functools

import jax
import jax.numpy as jnp
from jax import lax
from jax.experimental import pallas as pl
from jax.experimental.pallas import tpu as pltpu
from jax.sharding import PartitionSpec as P

LANES = 128
ROWS = 8
SPAN = 16
VMEM = pl.BlockSpec(memory_space=pltpu.VMEM)
SMEM = pl.BlockSpec(memory_space=pltpu.SMEM)
HBM = pl.BlockSpec(memory_space=pltpu.HBM)
DMA = pltpu.SemaphoreType.DMA


def call(body, outs, limit_mib, cost, scratch=(), aliases=None):
    flops, moved = cost
    return lambda specs, *args: pl.pallas_call(
        body,
        out_shape=[pltpu.HBM(s, t) if w is HBM else jax.ShapeDtypeStruct(s, t) for s, t, w in outs],
        in_specs=list(specs),
        out_specs=[w for _, _, w in outs],
        scratch_shapes=list(scratch),
        input_output_aliases=aliases or {},
        compiler_params=pltpu.CompilerParams(vmem_limit_bytes=limit_mib * 2**20),
        cost_estimate=pl.CostEstimate(flops=flops, bytes_accessed=moved, transcendentals=0),
    )(*(pltpu.with_memory_space_constraint(a, pltpu.HBM) if w is HBM else a for w, a in zip(specs, args)))


def start_all(copies):
    for copy in copies:
        copy.start()
    return copies


def wait_all(copies):
    for copy in copies:
        copy.wait()


def spread_body(decay_ref, residue_ref, out_ref, held_ref, in_sem, out_sem):
    modes, blocks = decay_ref.shape[0], out_ref.shape[0]
    wait_all(
        start_all([
            pltpu.make_async_copy(ref, held_ref.at[pl.ds(k * modes, modes)], in_sem.at[k])
            for k, ref in enumerate((decay_ref, residue_ref))
        ])
    )
    wait_all(start_all([pltpu.make_async_copy(held_ref, out_ref.at[k], out_sem.at[k]) for k in range(blocks)]))


def tree(values):
    while len(values) > 1:
        odd = values[-1:] if len(values) % 2 else []
        values = [a + b for a, b in zip(values[::2], values[1::2])] + odd
    return values[0]


def turned(scratch_ref, group, owners):
    return scratch_ref[pl.ds(group * LANES, LANES), :].T.reshape(owners, LANES // owners, LANES)


def by_mode(ref, row, blocks):
    return ref[pl.ds(row, blocks, stride=ref.shape[0] // blocks), :]


def position(span, offset, blocks):
    return pl.ds(pl.multiple_of((span * SPAN + offset) * blocks, blocks), blocks)


def product_body(
    gate_hbm, key_hbm, value_hbm, cot_hbm,
    x_ref, b_ref, sk_ref, lag_ref,
    in_ref, sem,
):
    length, channels = gate_hbm.shape
    blocks = channels // LANES
    pieces = sem.shape[0]
    depth = length // pieces
    fetch = [
        start_all([
            pltpu.make_async_copy(ref.at[pl.ds(p * depth, depth)], in_ref.at[k, pl.ds(p * depth, depth)], sem.at[p, k])
            for k, ref in enumerate((gate_hbm, key_hbm, value_hbm, cot_hbm))
        ])
        for p in range(pieces)
    ]
    lag_ref[...] = jnp.zeros(lag_ref.shape, jnp.float32)

    def step(place, sums):
        rows = pl.ds(pl.multiple_of(place * SPAN, SPAN), SPAN)
        after = []
        for block in range(blocks):
            lanes = pl.ds(block * LANES, LANES)
            gate, key, value, cot = (in_ref[k, rows, lanes].astype(jnp.float32) for k in range(4))
            x, b = key * value, cot * gate
            for part in range(SPAN // ROWS):
                target = pl.ds((place * SPAN + part * ROWS) * blocks + block, ROWS, stride=blocks)
                x_ref[target, :] = x[part * ROWS : (part + 1) * ROWS]
                b_ref[target, :] = b[part * ROWS : (part + 1) * ROWS]
            both = x * b
            after.append(sums[block] + tree([both[k * ROWS : (k + 1) * ROWS] for k in range(SPAN // ROWS)]))
        return tuple(after)

    def lags(span, carry):
        x = [x_ref[position(span, r, blocks), :] for r in range(SPAN)]
        b = [b_ref[position(span, r, blocks), :] for r in range(SPAN)]
        for u in range(SPAN):
            rows = pl.ds(u * blocks, blocks)
            lag_ref[rows, :] = lag_ref[rows, :] + tree([b[r + u] * x[r] for r in range(SPAN - u)])
        return carry

    sums = tuple(jnp.zeros((ROWS, LANES), jnp.float32) for _ in range(blocks))
    for p in range(pieces):
        wait_all(fetch[p])
        sums = lax.fori_loop(p * depth // SPAN, (p + 1) * depth // SPAN, step, sums)
        lax.fori_loop(p * depth // SPAN, (p + 1) * depth // SPAN, lags, 0)
    for block in range(blocks):
        sk_ref[pl.ds(block, 1), :] = jnp.sum(sums[block], axis=0, keepdims=True)


def part_slices(core, turned_ref, keep_ref, send_ref):
    for chip in range(keep_ref.shape[0]):
        keep_ref[chip] = turned_ref[2 * chip + core]
        send_ref[chip] = turned_ref[2 * chip + 1 - core]


def state_body(par_ref, x_ref, b_ref, sk_ref, total_ref, hs_hbm, bs_hbm, hs_ref, bs_ref, sem, last_sem):
    spans = hs_ref.shape[0]
    blocks = sk_ref.shape[0]
    modes = par_ref.shape[0] // blocks // 2
    pieces = sem.shape[1]
    part = spans // pieces
    factor = [jnp.exp(-by_mode(par_ref, m, blocks)) for m in range(modes)]

    def step(span, carry):
        ups, downs = carry
        mirror = spans - 1 - span
        for m in range(modes):
            hs_ref[span, pl.ds(m * blocks, blocks), :] = ups[m]
            bs_ref[mirror + 1, pl.ds(m * blocks, blocks), :] = downs[m]
        for r in range(SPAN):
            x = x_ref[position(span, r, blocks), :]
            b = b_ref[position(mirror, SPAN - 1 - r, blocks), :]
            ups = tuple(f * u + x for f, u in zip(factor, ups))
            downs = tuple(f * d + b for f, d in zip(factor, downs))
        return ups, downs

    zero = tuple(jnp.zeros((blocks, LANES), jnp.float32) for _ in range(modes))
    ups, downs = zero, zero
    copies = []
    for p in range(pieces):
        ups, downs = lax.fori_loop(p * part, (p + 1) * part, step, (ups, downs))
        here, there = pl.ds(p * part, part), pl.ds((pieces - 1 - p) * part + 1, part)
        copies += start_all([
            pltpu.make_async_copy(hs_ref.at[here], hs_hbm.at[here], sem.at[0, p]),
            pltpu.make_async_copy(bs_ref.at[there], bs_hbm.at[there], sem.at[1, p]),
        ])
    for m in range(modes):
        bs_ref[0, pl.ds(m * blocks, blocks), :] = downs[m]
        total_ref[pl.ds(m * blocks, blocks), :] = ups[m]
        total_ref[pl.ds((modes + m) * blocks, blocks), :] = downs[m]
    total_ref[pl.ds(2 * modes * blocks, blocks), :] = sk_ref[...]
    copies += start_all([pltpu.make_async_copy(bs_ref.at[0], bs_hbm.at[0], last_sem)])
    wait_all(copies)


def slope_body(
    index_ref, core_ref, par_ref, x_ref, b_ref, lag_ref, total_ref, joined_ref, hs_hbm, bs_hbm,
    rate_ref, side_rate_ref, keep_s_ref, send_s_ref, keep_a_ref, send_a_ref, keep_b_ref, send_b_ref,
    hs_ref, bs_ref, up_ref, down_ref, run_ref, sums_ref, turn_ref, rates_ref, snap_sem,
):
    owners = turn_ref.shape[0]
    groups = sums_ref.shape[0] // LANES
    spans = hs_ref.shape[0]
    blocks = lag_ref.shape[0] // SPAN
    modes = par_ref.shape[0] // blocks // 2
    fetch = start_all([
        pltpu.make_async_copy(hs_hbm, hs_ref, snap_sem.at[0]),
        pltpu.make_async_copy(bs_hbm, bs_ref, snap_sem.at[1]),
    ])
    share = rate_ref.shape[1]
    zero = jnp.zeros((blocks, LANES), jnp.float32)
    SLOPE, SUM0, SUM1, DOWN, POWER, FACTOR, FAR = range(7)
    for m in range(modes):
        rate = by_mode(par_ref, m, blocks)
        rows = pl.ds(m * blocks, blocks)
        for kind in (SLOPE, SUM0, SUM1, DOWN):
            run_ref[kind, rows, :] = zero
        run_ref[POWER, rows, :] = zero + 1.0
        run_ref[FACTOR, rows, :] = jnp.exp(-rate)
        run_ref[FAR, rows, :] = jnp.exp(-float(SPAN) * rate)

    def part(first, second, keep_ref, send_ref):
        for m in range(modes):
            sums_ref[pl.ds(m, blocks, stride=2 * modes), :] = first(m)
            sums_ref[pl.ds(modes + m, blocks, stride=2 * modes), :] = second(m)
        for group in range(groups):
            turn_ref[...] = turned(sums_ref, group, owners)
            part_slices(core_ref[0], turn_ref, keep_ref.at[group], send_ref.at[group])

    def at(m):
        return pl.ds(m * blocks, blocks)

    def totals(kind):
        return lambda m: total_ref[pl.ds((kind * modes + m) * blocks, blocks), :]

    part(totals(0), totals(1), keep_s_ref, send_s_ref)
    for group in range(groups):
        for block in range(group * blocks // groups, (group + 1) * blocks // groups):
            decay = par_ref[pl.ds(block * 2 * modes, modes), :]
            rates_ref[pl.ds(block * 2 * modes, 2 * modes), :] = jnp.concatenate([decay, decay], axis=0)
        rates_ref[pl.ds(group * LANES, LANES), :] = rates_ref[pl.ds(group * LANES, LANES), :].T
        rate_ref[group] = rates_ref[pl.ds(pl.multiple_of(group * LANES + index_ref[0] * share, share), share), :]
        for chip in range(side_rate_ref.shape[1]):
            start = group * LANES + (2 * chip + core_ref[0]) * share
            side_rate_ref[group, chip] = rates_ref[pl.ds(pl.multiple_of(start, share), share), :]

    def near(span, carry):
        late = [x_ref[position(span, r, blocks), :] * (SPAN - 1.0 - r) for r in range(SPAN - 1)]
        early = [b_ref[position(span, r, blocks), :] * float(r) for r in range(SPAN - 1, 0, -1)]
        factors = [run_ref[FACTOR, at(m), :] for m in range(modes)]
        for ref, terms in ((up_ref, late), (down_ref, early)):
            sums = [terms[0]] * modes
            for term in terms[1:]:
                sums = [f * s + term for f, s in zip(factors, sums)]
            for m in range(modes):
                ref[span, at(m), :] = factors[m] * sums[m]
        return carry

    def across(span, carry):
        begin = (span * SPAN).astype(jnp.float32)
        for m in range(modes):
            rows = at(m)
            far = run_ref[FAR, rows, :]
            up, down = up_ref[span, rows, :], down_ref[span, rows, :]
            head = hs_ref[span, rows, :]
            own = bs_ref[span, rows, :] - far * bs_ref[span + 1, rows, :]
            slope, power = run_ref[SLOPE, rows, :], run_ref[POWER, rows, :]
            run_ref[SUM0, rows, :] = run_ref[SUM0, rows, :] + head * own
            run_ref[SUM1, rows, :] = run_ref[SUM1, rows, :] + (slope * own + head * (own + down))
            run_ref[DOWN, rows, :] = run_ref[DOWN, rows, :] + power * (begin * own + down)
            run_ref[POWER, rows, :] = power * far
            run_ref[SLOPE, rows, :] = far * (slope + float(SPAN) * head) + up
        return carry

    lax.fori_loop(0, spans, near, 0)
    wait_all(fetch)
    lax.fori_loop(0, spans, across, 0)
    part(lambda m: run_ref[DOWN, at(m), :], lambda m: run_ref[SLOPE, at(m), :], keep_a_ref, send_a_ref)
    lags = [lag_ref[pl.ds(u * blocks, blocks), :] for u in range(SPAN)]
    factors = [run_ref[FACTOR, at(m), :] for m in range(modes)]
    plain = [lags[SPAN - 1]] * modes
    slope = [lags[SPAN - 1] * (SPAN - 1.0)] * modes
    for u in range(SPAN - 2, -1, -1):
        sloped = lags[u] * float(u)
        plain = [f * p + lags[u] for f, p in zip(factors, plain)]
        slope = [f * p + sloped for f, p in zip(factors, slope)]
    part(
        lambda m: factors[m] * run_ref[SUM0, at(m), :] + plain[m],
        lambda m: factors[m] * run_ref[SUM1, at(m), :] + slope[m],
        keep_b_ref,
        send_b_ref,
    )


def pair_body(
    core_ref, a_ref, a_other_ref, b_ref, b_other_ref, s_ref, s_other_ref, rate_ref, joined_ref,
    out_hbm, held_ref, sem,
    *, modes, length,
):
    groups, chips, rows = s_ref.shape[0], s_ref.shape[1], s_ref.shape[2]
    first = lane_is_first((rows, LANES), modes)
    low = core_ref[0] == 0

    def turn(value):
        return jnp.where(first, pltpu.roll(value, LANES - modes, 1), pltpu.roll(value, modes, 1))

    copies = []
    for group in range(groups):
        for chip in range(chips):
            def both(own_ref, other_ref):
                own, other = own_ref[group, chip], other_ref[group, chip]
                return jnp.where(low, own, other), jnp.where(low, other, own)

            (a0, a1), (b0, b1), (s0, s1) = both(a_ref, a_other_ref), both(b_ref, b_other_ref), both(s_ref, s_other_ref)
            rate = rate_ref[group, chip]
            far, factor = jnp.exp(-float(length) * rate), jnp.exp(-rate)
            later = turn(s1)
            held_ref[0, group, chip] = jnp.where(first, far * s0 + s1, s0 + far * s1)
            held_ref[1, group, chip] = jnp.where(
                first, a0 + far * (a1 + float(length) * later), far * (a0 + float(length) * turn(s0)) + a1
            )
            cross = s0 * later
            slope = pltpu.roll(cross + s0 * a1, modes, 1) + a0 * s1
            held_ref[2, group, chip] = b0 + b1 + factor * jnp.where(first, cross, slope)
        copies += start_all([
            pltpu.make_async_copy(held_ref.at[k, group], out_hbm.at[:, k * groups + group], sem.at[k, group])
            for k in range(3)
        ])
    wait_all(copies)


def join_weights(index, step, rate, length):
    run = 2**step
    upper = lax.rem(lax.div(index, run), 2) == 1
    offset = lax.rem(index, run)
    chunk = float(length) * rate
    ahead = jnp.where(upper, offset, run - 1 - offset).astype(jnp.float32)
    return upper, jnp.exp(-float(run) * chunk), jnp.exp(-ahead * chunk)


def join_body(index_ref, par_ref, total_ref, other_ref, *refs, step, length, modes, last):
    sends_later = lax.rem(lax.div(index_ref[0], 2 ** (step + 1)), 2) == 1
    held_ref = refs[0] if step else None
    next_ref, out_ref = refs[-2:]
    blocks = par_ref.shape[0] // modes // 2
    for m in range(modes):
        low, high = pl.ds(m * blocks, blocks), pl.ds((modes + m) * blocks, blocks)
        upper, far, near = join_weights(index_ref[0], step, by_mode(par_ref, m, blocks), length)
        x, y, ox, oy = total_ref[low, :], total_ref[high, :], other_ref[low, :], other_ref[high, :]
        head, tail = jnp.where(upper, near * ox, 0.0), jnp.where(upper, 0.0, near * oy)
        if held_ref is not None:
            head, tail = head + held_ref[low, :], tail + held_ref[high, :]
        out_ref[low, :] = head
        out_ref[high, :] = tail
        new_x, new_y = jnp.where(upper, far * ox + x, far * x + ox), jnp.where(upper, far * y + oy, far * oy + y)
        if last:
            next_ref[low, :] = jnp.where(sends_later, new_y, new_x)
        else:
            next_ref[low, :] = new_x
            next_ref[high, :] = new_y
    rest = pl.ds(2 * modes * blocks, blocks)
    next_ref[pl.ds(next_ref.shape[0] - blocks, blocks), :] = total_ref[rest, :] + other_ref[rest, :]


def local_body(par_ref, x_ref, b_ref, joined_ref, skip_hbm, y_hbm, z_hbm, skip_ref, out_ref, skip_sem, sem):
    fetch = pltpu.make_async_copy(skip_hbm, skip_ref, skip_sem)
    fetch.start()
    blocks = skip_ref.shape[0]
    modes = par_ref.shape[0] // blocks // 2
    spans = x_ref.shape[0] // blocks // SPAN
    pieces = sem.shape[1]
    part = spans // pieces
    factors, terms = [], []
    for m in range(modes):
        rate = by_mode(par_ref, m, blocks)
        factors.append(jnp.exp(-rate))
        terms.append(by_mode(par_ref, modes + m, blocks) * jnp.sqrt(rate))
    kernel = []
    for u in range(SPAN):
        kernel.append(tree(terms))
        terms = [t * f for t, f in zip(terms, factors)]
    fetch.wait()
    kernel[0] = kernel[0] + skip_ref[...]

    def step(span, carry):
        def at(r):
            return pl.ds(pl.multiple_of((span * SPAN + r) * blocks, blocks), blocks)

        x = [x_ref[at(r), :] for r in range(SPAN)]
        for r in range(SPAN):
            out_ref[0, at(r), :] = tree([kernel[u] * x[r - u] for u in range(r + 1)])
        b = [b_ref[at(r), :] for r in range(SPAN)]
        for r in range(SPAN):
            out_ref[1, at(r), :] = tree([kernel[u] * b[r + u] for u in range(SPAN - r)])
        return carry

    copies = []
    for p in range(pieces):
        lax.fori_loop(p * part, (p + 1) * part, step, 0)
        rows = pl.ds(p * part * SPAN * blocks, part * SPAN * blocks)
        copies += start_all([
            pltpu.make_async_copy(out_ref.at[k, rows], ref.at[rows], sem.at[k, p]) for k, ref in enumerate((y_hbm, z_hbm))
        ])
    wait_all(copies)


def lane_is_first(shape, modes):
    return lax.broadcasted_iota(jnp.int32, shape, 1) % (2 * modes) < modes


def scan_body(s_ref, rate_ref, done_hbm, out_ref, pack_ref, sem, *, modes, length):
    chunks, groups, rows = s_ref.shape[0], rate_ref.shape[0], rate_ref.shape[1]
    first = lane_is_first((rows, LANES), modes)
    zero = jnp.zeros((rows, LANES), jnp.float32)
    span = 2 * modes
    fold = LANES // span
    row = lax.broadcasted_iota(jnp.int32, (rows, LANES), 0) % fold
    column = lax.broadcasted_iota(jnp.int32, (rows, LANES), 1) // span
    for group in range(groups):
        alpha = jnp.exp(-float(length) * rate_ref[group])
        before, lead, total0, total1 = zero, zero, zero, zero
        heads = []
        for k in range(chunks):
            value = s_ref[k, group]
            later = pltpu.roll(value, LANES - modes, 1)
            heads.append(before)
            total0 += before * later
            total1 += (lead + before) * later
            lead = alpha * (lead + float(length) * before)
            before = alpha * before + value
        after, cross = zero, zero
        for k in reversed(range(chunks)):
            cross += jnp.where(first, heads[k], after) * s_ref[k, groups + group]
            after = alpha * after + s_ref[k, group]
        inner = tree([s_ref[k, 2 * groups + group] for k in range(chunks)])
        outer = jnp.where(first, total0, pltpu.roll(total1, modes, 1) + cross + pltpu.roll(cross, modes, 1))
        total = inner + jnp.exp(-rate_ref[group]) * outer
        packed = total
        for shift in range(1, fold):
            moved = pltpu.roll(total, LANES - shift * span, 1)
            moved = jnp.where(row >= shift, pltpu.roll(moved, shift, 0), pltpu.roll(moved, rows - fold + shift, 0))
            packed = jnp.where((row - column + fold) % fold == shift, moved, packed)
        for block in range(fold):
            for r in range(rows // fold):
                pack_ref[group * fold + block, pl.ds(r, 1), :] = packed[r * fold + block : r * fold + block + 1]
    wait_all(start_all([pltpu.make_async_copy(pack_ref, out_ref.at[k], sem.at[k]) for k in range(out_ref.shape[0])]))


def final_body(g_ref, residue_ref, decay_ref, gres_ref, gdec_ref, spread_ref):
    modes = residue_ref.shape[0]
    owners, blocks, rows = g_ref.shape[0], g_ref.shape[1], g_ref.shape[2]
    span = 2 * modes
    fold = LANES // span
    total = tree([g_ref[:, block] for block in range(blocks)]).reshape(owners * rows, LANES)
    for k in range(fold):
        moved = total if k == 0 else pltpu.roll(total, LANES - k * span, 1)
        spread_ref[pl.ds(k, owners * rows, stride=fold), :] = moved
    sums = spread_ref[...].T
    plain, slope = sums[:modes], sums[modes:span]
    decay = decay_ref[...]
    root = jnp.sqrt(decay)
    gres_ref[...] = root * plain
    gdec_ref[...] = residue_ref[...] * root * (0.5 * plain - decay * slope)


def settle_body(
    par_ref, held_ref, y_hbm, z_hbm, hs_hbm, bs_hbm,
    loc_ref,
    run_ref, snap_ref, sem,
):
    spans, blocks = hs_hbm.shape[0], y_hbm.shape[0] // hs_hbm.shape[0] // SPAN
    modes = hs_hbm.shape[1] // blocks
    pieces = sem.shape[0]
    part = spans // pieces
    fetch = []
    for p in range(pieces):
        copies = []
        for kind, (place, local, snaps, shift) in enumerate(((p, y_hbm, hs_hbm, 0), (pieces - 1 - p, z_hbm, bs_hbm, 1))):
            rows = pl.ds(place * part * SPAN * blocks, part * SPAN * blocks)
            copies.append(pltpu.make_async_copy(local.at[rows], loc_ref.at[kind, rows], sem.at[p, 2 * kind]))
            source, target = pl.ds(place * part + shift, part), pl.ds(place * part, part)
            copies.append(pltpu.make_async_copy(snaps.at[source], snap_ref.at[kind, target], sem.at[p, 2 * kind + 1]))
        fetch.append(start_all(copies))
    FACTOR, FAR, WEIGHT, HEAD, TAIL = range(5)
    for m in range(modes):
        rows = pl.ds(m * blocks, blocks)
        rate = by_mode(par_ref, m, blocks)
        factor = jnp.exp(-rate)
        run_ref[FACTOR, rows, :] = factor
        run_ref[FAR, rows, :] = jnp.exp(-float(SPAN) * rate)
        run_ref[WEIGHT, rows, :] = by_mode(par_ref, modes + m, blocks) * jnp.sqrt(rate) * factor
        run_ref[HEAD, rows, :] = held_ref[rows, :]
        run_ref[TAIL, rows, :] = held_ref[pl.ds((modes + m) * blocks, blocks), :]

    def finish(kind, span, run):
        terms, factors = [], []
        for m in range(modes):
            rows = pl.ds(m * blocks, blocks)
            state = run_ref[run, rows, :]
            terms.append(run_ref[WEIGHT, rows, :] * (snap_ref[kind, span, rows, :] + state))
            run_ref[run, rows, :] = state * run_ref[FAR, rows, :]
            factors.append(run_ref[FACTOR, rows, :])
        for k in range(SPAN):
            rows = position(span, k if kind == 0 else SPAN - 1 - k, blocks)
            loc_ref[kind, rows, :] = loc_ref[kind, rows, :] + tree(terms)
            if k < SPAN - 1:
                terms = [t * f for t, f in zip(terms, factors)]

    def both(span, carry):
        finish(0, span, HEAD)
        finish(1, spans - 1 - span, TAIL)
        return carry

    for p in range(pieces):
        wait_all(fetch[p])
        lax.fori_loop(p * part, (p + 1) * part, both, 0)


def out_body(
    index_ref, par_ref, loc_ref, total_ref, other_ref, gate_hbm, key_hbm, value_hbm, cot_hbm,
    mixed_hbm, ggate_hbm, gkey_hbm, gvalue_hbm, gskip_ref,
    run_ref, sum_ref, in_ref, out_ref, in_sem, out_sem,
    *, step,
):
    length, channels = gate_hbm.shape
    blocks = channels // LANES
    modes = par_ref.shape[0] // blocks // 2
    spans = length // SPAN
    pieces = in_sem.shape[0]
    part = spans // pieces
    depth = part * SPAN
    fetch = [
        start_all([
            pltpu.make_async_copy(ref.at[pl.ds(p * depth, depth)], in_ref.at[k, pl.ds(p * depth, depth)], in_sem.at[p, k])
            for k, ref in enumerate((gate_hbm, cot_hbm, value_hbm, key_hbm))
        ])
        for p in range(pieces)
    ]
    rest = pl.ds(modes * blocks, blocks)
    gskip_ref[...] = total_ref[rest, :] + other_ref[rest, :]
    FACTOR, FAR, STATE = range(3)
    for m in range(modes):
        rows = pl.ds(m * blocks, blocks)
        rate = by_mode(par_ref, m, blocks)
        _, _, near = join_weights(index_ref[0], step, rate, length)
        factor = jnp.exp(-rate)
        run_ref[FACTOR, rows, :] = factor
        run_ref[FAR, rows, :] = jnp.exp(-float(SPAN) * rate)
        weight = by_mode(par_ref, modes + m, blocks) * jnp.sqrt(rate) * factor
        run_ref[STATE, rows, :] = weight * (near * other_ref[rows, :])
    later = lax.rem(lax.div(index_ref[0], 2**step), 2) == 1
    kind, other_kind = jnp.where(later, 0, 1), jnp.where(later, 1, 0)

    def carry_in(span, carry):
        place = jnp.where(later, span, spans - 1 - span)
        terms, factors = [], []
        for m in range(modes):
            rows = pl.ds(m * blocks, blocks)
            terms.append(run_ref[STATE, rows, :])
            run_ref[STATE, rows, :] = terms[-1] * run_ref[FAR, rows, :]
            factors.append(run_ref[FACTOR, rows, :])
        for k in range(SPAN):
            rows = position(place, jnp.where(later, k, SPAN - 1 - k), blocks)
            sum_ref[kind, rows, :] = loc_ref[kind, rows, :] + tree(terms)
            sum_ref[other_kind, rows, :] = loc_ref[other_kind, rows, :]
            if k < SPAN - 1:
                terms = [t * f for t, f in zip(terms, factors)]
        return carry

    def finish(span, carry):
        rows = pl.ds(pl.multiple_of(span * SPAN, SPAN), SPAN)
        for block in range(blocks):
            lanes = pl.ds(block * LANES, LANES)
            for side in range(2):
                total = jnp.concatenate(
                    [
                        sum_ref[side, pl.ds((span * SPAN + half * ROWS) * blocks + block, ROWS, stride=blocks), :]
                        for half in range(SPAN // ROWS)
                    ],
                    axis=0,
                )
                for slot in (2 * side, 2 * side + 1):
                    value = in_ref[slot, rows, lanes].astype(jnp.float32) * total
                    out_ref[slot, rows, lanes] = value.astype(jnp.bfloat16)
        return carry

    lax.fori_loop(0, spans, carry_in, 0)
    stores = []
    for p in range(pieces):
        wait_all(fetch[p])
        lax.fori_loop(p * part, (p + 1) * part, finish, 0)
        rows = pl.ds(p * depth, depth)
        for slot, ref in enumerate((mixed_hbm, ggate_hbm, gkey_hbm, gvalue_hbm)):
            stores += start_all([pltpu.make_async_copy(out_ref.at[slot, rows], ref.at[rows], out_sem.at[p, slot])])
    wait_all(stores)


def on_device(gate_in, key_in, value_in, cotangent, skip, residue, decay):
    f32, bf16 = jnp.float32, jnp.bfloat16
    chips, cores = lax.axis_size("chip"), lax.axis_size("core")
    ctx = ("chip", "core")
    owners = chips * cores
    blocks = lax.axis_size("ch")
    length, channels = gate_in.shape
    filters, modes = residue.shape
    share = filters // owners
    groups = blocks * 2 * modes // LANES
    spans = length // SPAN
    pieces = 4
    place = lax.axis_index(ctx).astype(jnp.int32).reshape(1)
    core = lax.axis_index("core").astype(jnp.int32).reshape(1)

    def change(value):
        return lax.ppermute(value, "core", [(i, cores - 1 - i) for i in range(cores)])

    whole = (length, channels)
    signal = (length * blocks, LANES)
    heads_at, tails_at = (spans, modes * blocks, LANES), (spans + 1, modes * blocks, LANES)
    size = length * channels
    sums = pltpu.VMEM((groups * LANES, LANES), f32)
    dense = pltpu.VMEM((4, *whole), bf16)
    tile = (share, LANES)

    (sent,) = call(
        spread_body,
        [((blocks, 2 * modes, LANES), f32, HBM)],
        4,
        (0, 10**5),
        [pltpu.VMEM((2 * modes, LANES), f32), DMA((2,)), DMA((blocks,))],
    )([HBM] * 2, decay.T, residue.T)
    params = lax.all_to_all(sent, "ch", 0, 0, tiled=True).reshape(blocks * 2 * modes, LANES)

    x, b, sk, lag = call(
        product_body,
        [(signal, f32, VMEM)] * 2 + [((blocks, LANES), f32, VMEM), ((SPAN * blocks, LANES), f32, VMEM)],
        16,
        (8 * size, 16 * size),
        [dense, DMA((pieces, 4))],
    )([HBM] * 4, gate_in, key_in, value_in, cotangent)

    side = (groups, chips, *tile)
    total_at = ((2 * modes + 1) * blocks, LANES)
    total, head_states, tail_states = call(
        state_body,
        [(total_at, f32, VMEM), (heads_at, f32, HBM), (tails_at, f32, HBM)],
        16,
        (64 * size, 16 * size),
        [pltpu.VMEM(heads_at, f32), pltpu.VMEM(tails_at, f32), DMA((2, pieces)), DMA],
    )([VMEM] * 4, params, x, b, sk)

    totals, held, others = [total], [], []
    steps = (owners - 1).bit_length()
    for step in range(steps):
        others.append(lax.ppermute(totals[-1], ctx, [(i, i ^ 2**step) for i in range(owners)]))
        if step == steps - 1:
            break
        last = step == steps - 2
        total, *held = call(
            functools.partial(join_body, step=step, length=length, modes=modes, last=last),
            [(((modes + 1) * blocks, LANES) if last else total_at, f32, VMEM), ((2 * modes * blocks, LANES), f32, VMEM)],
            8,
            (size, size),
        )([SMEM] + [VMEM] * (3 + len(held)), place, params, totals[-1], others[-1], *held)
        totals.append(total)

    y, z = call(
        local_body,
        [(signal, f32, HBM)] * 2,
        16,
        (40 * size, 16 * size),
        [pltpu.VMEM((blocks, LANES), f32), pltpu.VMEM((2, *signal), f32), DMA, DMA((2, pieces))],
    )([VMEM] * 4 + [HBM], params, x, b, totals[2], skip.reshape(blocks, LANES))

    rates, side_rates, own_s, send_s, own_a, send_a, own_b, send_b = call(
        slope_body,
        [((groups, *tile), f32, VMEM)] + [(side, f32, VMEM)] * 7,
        16,
        (100 * size, 16 * size),
        [pltpu.VMEM(heads_at, f32), pltpu.VMEM(tails_at, f32), pltpu.VMEM(heads_at, f32), pltpu.VMEM(heads_at, f32)]
        + [pltpu.VMEM((7, modes * blocks, LANES), f32), sums, pltpu.VMEM((owners, *tile), f32), sums, DMA((2,))],
    )(
        [SMEM] * 2 + [VMEM] * 6 + [HBM] * 2,
        place, core, params, x, b, lag, totals[0], totals[1], head_states, tail_states,
    )

    (states,) = call(
        functools.partial(pair_body, modes=modes, length=length),
        [((chips, 3 * groups, *tile), f32, HBM)],
        8,
        (size, size),
        [pltpu.VMEM((3, *side), f32), DMA((3, groups))],
    )(
        [SMEM] + [VMEM] * 8,
        core, own_a, change(send_a), own_b, change(send_b), own_s, change(send_s), side_rates, totals[2],
    )
    states = lax.all_to_all(states, "chip", 0, 0, tiled=True)

    packed = (owners, blocks, share * 2 * modes // LANES, LANES)
    (grads,) = call(
        functools.partial(scan_body, modes=modes, length=cores * length),
        [(packed, f32, HBM)],
        8,
        (10**5, 10**6),
        [pltpu.VMEM(packed[1:], f32), DMA((owners,))],
    )([VMEM] * 2 + [HBM], states, rates, y)
    grads = lax.all_to_all(grads.reshape(owners * blocks, *packed[2:]), ("chip", "core", "ch"), 0, 0, tiled=True)

    (settled,) = call(
        settle_body,
        [((2, *signal), f32, VMEM)],
        16,
        (64 * size, 16 * size),
        [pltpu.VMEM((5, modes * blocks, LANES), f32), pltpu.VMEM((2, *heads_at), f32), DMA((pieces, 4))],
    )([VMEM] * 2 + [HBM] * 4, params, *held, y, z, head_states, tail_states)

    mixed, grad_gate, grad_key, grad_value, grad_skip = call(
        functools.partial(out_body, step=steps - 1),
        [(whole, bf16, HBM)] * 4 + [((blocks, LANES), f32, VMEM)],
        16,
        (32 * size, 16 * size),
        [pltpu.VMEM((3, modes * blocks, LANES), f32), pltpu.VMEM((2, *signal), f32), dense, dense]
        + [DMA((pieces, 4)), DMA((pieces, 4))],
    )(
        [SMEM] + [VMEM] * 4 + [HBM] * 4,
        place, params, settled, totals[3], others[3], gate_in, key_in, value_in, cotangent,
    )

    grad_residue, grad_log_decay = call(
        final_body, [((modes, filters), f32, VMEM)] * 2, 8, (10**5, 10**6), [pltpu.VMEM((LANES, LANES), f32)]
    )([VMEM] * 3, grads.reshape(packed), residue.T, decay.T)
    return (mixed, grad_gate, grad_key, grad_value, grad_skip.reshape(channels), grad_residue.T, grad_log_decay.T)


def solution(mesh):
    cores = 2
    shape = (mesh.shape["ctx"] // cores, cores, mesh.shape["ch"])
    split = jax.sharding.Mesh(mesh.devices.reshape(shape), ("chip", "core", "ch"))
    rows = P(("chip", "core"), "ch")
    specs = (rows, rows, rows, rows, P("ch"), P("ch", None), P("ch", None))
    return jax.shard_map(on_device, mesh=split, in_specs=specs, out_specs=specs, check_vma=False)
```

```python
import functools

import jax
import jax.numpy as jnp
from jax import lax
from jax.experimental import pallas as pl
from jax.experimental.pallas import tpu as pltpu
from jax.sharding import PartitionSpec as P

LANES = 128
ROWS = 8
SPAN = 16
VMEM = pl.BlockSpec(memory_space=pltpu.VMEM)
SMEM = pl.BlockSpec(memory_space=pltpu.SMEM)
HBM = pl.BlockSpec(memory_space=pltpu.HBM)
DMA = pltpu.SemaphoreType.DMA


def call(body, outs, limit_mib, cost, scratch=(), aliases=None):
    flops, moved = cost
    return lambda specs, *args: pl.pallas_call(
        body,
        out_shape=[pltpu.HBM(s, t) if w is HBM else jax.ShapeDtypeStruct(s, t) for s, t, w in outs],
        in_specs=list(specs),
        out_specs=[w for _, _, w in outs],
        scratch_shapes=list(scratch),
        input_output_aliases=aliases or {},
        compiler_params=pltpu.CompilerParams(vmem_limit_bytes=limit_mib * 2**20),
        cost_estimate=pl.CostEstimate(flops=flops, bytes_accessed=moved, transcendentals=0),
    )(*(pltpu.with_memory_space_constraint(a, pltpu.HBM) if w is HBM else a for w, a in zip(specs, args)))


def start_all(copies):
    for copy in copies:
        copy.start()
    return copies


def wait_all(copies):
    for copy in copies:
        copy.wait()


def spread_body(decay_ref, residue_ref, out_ref, held_ref, in_sem, out_sem):
    modes, blocks = decay_ref.shape[0], out_ref.shape[0]
    wait_all(
        start_all([
            pltpu.make_async_copy(ref, held_ref.at[pl.ds(k * modes, modes)], in_sem.at[k])
            for k, ref in enumerate((decay_ref, residue_ref))
        ])
    )
    wait_all(start_all([pltpu.make_async_copy(held_ref, out_ref.at[k], out_sem.at[k]) for k in range(blocks)]))


def tree(values):
    while len(values) > 1:
        odd = values[-1:] if len(values) % 2 else []
        values = [a + b for a, b in zip(values[::2], values[1::2])] + odd
    return values[0]


def turned(scratch_ref, group, owners):
    return scratch_ref[pl.ds(group * LANES, LANES), :].T.reshape(owners, LANES // owners, LANES)


def by_mode(ref, row, blocks):
    return ref[pl.ds(row, blocks, stride=ref.shape[0] // blocks), :]


def position(span, offset, blocks):
    return pl.ds(pl.multiple_of((span * SPAN + offset) * blocks, blocks), blocks)


def product_body(
    gate_hbm, key_hbm, value_hbm, cot_hbm,
    x_ref, b_ref, sk_ref, lag_ref,
    in_ref, sem,
):
    length, channels = gate_hbm.shape
    blocks = channels // LANES
    pieces = sem.shape[0]
    depth = length // pieces
    fetch = [
        start_all([
            pltpu.make_async_copy(ref.at[pl.ds(p * depth, depth)], in_ref.at[k, pl.ds(p * depth, depth)], sem.at[p, k])
            for k, ref in enumerate((gate_hbm, key_hbm, value_hbm, cot_hbm))
        ])
        for p in range(pieces)
    ]
    lag_ref[...] = jnp.zeros(lag_ref.shape, jnp.float32)

    def step(place, sums):
        rows = pl.ds(pl.multiple_of(place * SPAN, SPAN), SPAN)
        after = []
        for block in range(blocks):
            lanes = pl.ds(block * LANES, LANES)
            gate, key, value, cot = (in_ref[k, rows, lanes].astype(jnp.float32) for k in range(4))
            x, b = key * value, cot * gate
            for part in range(SPAN // ROWS):
                target = pl.ds((place * SPAN + part * ROWS) * blocks + block, ROWS, stride=blocks)
                x_ref[target, :] = x[part * ROWS : (part + 1) * ROWS]
                b_ref[target, :] = b[part * ROWS : (part + 1) * ROWS]
            both = x * b
            after.append(sums[block] + tree([both[k * ROWS : (k + 1) * ROWS] for k in range(SPAN // ROWS)]))
        return tuple(after)

    def lags(span, carry):
        x = [x_ref[position(span, r, blocks), :] for r in range(SPAN)]
        b = [b_ref[position(span, r, blocks), :] for r in range(SPAN)]
        for u in range(SPAN):
            rows = pl.ds(u * blocks, blocks)
            lag_ref[rows, :] = lag_ref[rows, :] + tree([b[r + u] * x[r] for r in range(SPAN - u)])
        return carry

    sums = tuple(jnp.zeros((ROWS, LANES), jnp.float32) for _ in range(blocks))
    for p in range(pieces):
        wait_all(fetch[p])
        sums = lax.fori_loop(p * depth // SPAN, (p + 1) * depth // SPAN, step, sums)
        lax.fori_loop(p * depth // SPAN, (p + 1) * depth // SPAN, lags, 0)
    for block in range(blocks):
        sk_ref[pl.ds(block, 1), :] = jnp.sum(sums[block], axis=0, keepdims=True)


def part_slices(core, turned_ref, keep_ref, send_ref):
    for chip in range(keep_ref.shape[0]):
        keep_ref[chip] = turned_ref[2 * chip + core]
        send_ref[chip] = turned_ref[2 * chip + 1 - core]


def state_body(par_ref, x_ref, b_ref, sk_ref, total_ref, hs_hbm, bs_hbm, hs_last_ref, bs_last_ref, hs_ref, bs_ref, sem):
    spans = hs_ref.shape[0]
    blocks = sk_ref.shape[0]
    modes = par_ref.shape[0] // blocks // 2
    part = hs_last_ref.shape[0]
    pieces = spans // part
    factor = [jnp.exp(-by_mode(par_ref, m, blocks)) for m in range(modes)]

    def step(span, carry, last):
        ups, downs = carry
        mirror = spans - 1 - span
        heads, tails, first = (hs_last_ref, bs_last_ref, spans - part) if last else (hs_ref, bs_ref, 0)
        for m in range(modes):
            heads[span - first, pl.ds(m * blocks, blocks), :] = ups[m]
            tails[mirror + 1, pl.ds(m * blocks, blocks), :] = downs[m]
        for r in range(SPAN):
            x = x_ref[position(span, r, blocks), :]
            b = b_ref[position(mirror, SPAN - 1 - r, blocks), :]
            ups = tuple(f * u + x for f, u in zip(factor, ups))
            downs = tuple(f * d + b for f, d in zip(factor, downs))
        return ups, downs

    zero = tuple(jnp.zeros((blocks, LANES), jnp.float32) for _ in range(modes))
    ups, downs = zero, zero
    copies = []
    for p in range(pieces):
        last = p == pieces - 1
        ups, downs = lax.fori_loop(p * part, (p + 1) * part, functools.partial(step, last=last), (ups, downs))
        if last:
            break
        here, there = pl.ds(p * part, part), pl.ds((pieces - 1 - p) * part + 1, part)
        copies += start_all([
            pltpu.make_async_copy(hs_ref.at[here], hs_hbm.at[here], sem.at[0, p]),
            pltpu.make_async_copy(bs_ref.at[there], bs_hbm.at[there], sem.at[1, p]),
        ])
    for m in range(modes):
        bs_last_ref[0, pl.ds(m * blocks, blocks), :] = downs[m]
        total_ref[pl.ds(m * blocks, blocks), :] = ups[m]
        total_ref[pl.ds((modes + m) * blocks, blocks), :] = downs[m]
    total_ref[pl.ds(2 * modes * blocks, blocks), :] = sk_ref[...]
    wait_all(copies)


def slope_body(
    index_ref, core_ref, par_ref, x_ref, b_ref, lag_ref, total_ref, joined_ref, hs_in, bs_in, hs_last_ref, bs_last_ref,
    hs_hbm, bs_hbm, rate_ref, side_rate_ref, keep_s_ref, send_s_ref, keep_a_ref, send_a_ref, keep_b_ref, send_b_ref,
    hs_ref, bs_ref, up_ref, down_ref, run_ref, sums_ref, turn_ref, rates_ref, snap_sem,
):
    owners = turn_ref.shape[0]
    groups = sums_ref.shape[0] // LANES
    spans = hs_ref.shape[0]
    blocks = lag_ref.shape[0] // SPAN
    modes = par_ref.shape[0] // blocks // 2
    part_spans = hs_last_ref.shape[0]
    rest = spans - part_spans
    heads, tails = pl.ds(0, rest), pl.ds(part_spans + 1, rest)
    fetch = start_all([
        pltpu.make_async_copy(hs_in.at[heads], hs_ref.at[heads], snap_sem.at[0]),
        pltpu.make_async_copy(bs_in.at[tails], bs_ref.at[tails], snap_sem.at[1]),
    ])
    stores = start_all([
        pltpu.make_async_copy(hs_last_ref, hs_hbm.at[pl.ds(rest, part_spans)], snap_sem.at[2]),
        pltpu.make_async_copy(bs_last_ref, bs_hbm.at[pl.ds(0, part_spans + 1)], snap_sem.at[3]),
    ])
    hs_ref[rest:] = hs_last_ref[...]
    bs_ref[: part_spans + 1] = bs_last_ref[...]
    share = rate_ref.shape[1]
    zero = jnp.zeros((blocks, LANES), jnp.float32)
    SLOPE, SUM0, SUM1, DOWN, POWER, FACTOR, FAR = range(7)
    for m in range(modes):
        rate = by_mode(par_ref, m, blocks)
        rows = pl.ds(m * blocks, blocks)
        for kind in (SLOPE, SUM0, SUM1, DOWN):
            run_ref[kind, rows, :] = zero
        run_ref[POWER, rows, :] = zero + 1.0
        run_ref[FACTOR, rows, :] = jnp.exp(-rate)
        run_ref[FAR, rows, :] = jnp.exp(-float(SPAN) * rate)

    def part(first, second, keep_ref, send_ref):
        for m in range(modes):
            sums_ref[pl.ds(m, blocks, stride=2 * modes), :] = first(m)
            sums_ref[pl.ds(modes + m, blocks, stride=2 * modes), :] = second(m)
        for group in range(groups):
            turn_ref[...] = turned(sums_ref, group, owners)
            part_slices(core_ref[0], turn_ref, keep_ref.at[group], send_ref.at[group])

    def at(m):
        return pl.ds(m * blocks, blocks)

    def totals(kind):
        return lambda m: total_ref[pl.ds((kind * modes + m) * blocks, blocks), :]

    part(totals(0), totals(1), keep_s_ref, send_s_ref)
    for group in range(groups):
        for block in range(group * blocks // groups, (group + 1) * blocks // groups):
            decay = par_ref[pl.ds(block * 2 * modes, modes), :]
            rates_ref[pl.ds(block * 2 * modes, 2 * modes), :] = jnp.concatenate([decay, decay], axis=0)
        rates_ref[pl.ds(group * LANES, LANES), :] = rates_ref[pl.ds(group * LANES, LANES), :].T
        rate_ref[group] = rates_ref[pl.ds(pl.multiple_of(group * LANES + index_ref[0] * share, share), share), :]
        for chip in range(side_rate_ref.shape[1]):
            start = group * LANES + (2 * chip + core_ref[0]) * share
            side_rate_ref[group, chip] = rates_ref[pl.ds(pl.multiple_of(start, share), share), :]

    def near(span, carry):
        late = [x_ref[position(span, r, blocks), :] * (SPAN - 1.0 - r) for r in range(SPAN - 1)]
        early = [b_ref[position(span, r, blocks), :] * float(r) for r in range(SPAN - 1, 0, -1)]
        factors = [run_ref[FACTOR, at(m), :] for m in range(modes)]
        for ref, terms in ((up_ref, late), (down_ref, early)):
            sums = [terms[0]] * modes
            for term in terms[1:]:
                sums = [f * s + term for f, s in zip(factors, sums)]
            for m in range(modes):
                ref[span, at(m), :] = factors[m] * sums[m]
        return carry

    def across(span, carry):
        begin = (span * SPAN).astype(jnp.float32)
        for m in range(modes):
            rows = at(m)
            far = run_ref[FAR, rows, :]
            up, down = up_ref[span, rows, :], down_ref[span, rows, :]
            head = hs_ref[span, rows, :]
            own = bs_ref[span, rows, :] - far * bs_ref[span + 1, rows, :]
            slope, power = run_ref[SLOPE, rows, :], run_ref[POWER, rows, :]
            run_ref[SUM0, rows, :] = run_ref[SUM0, rows, :] + head * own
            run_ref[SUM1, rows, :] = run_ref[SUM1, rows, :] + (slope * own + head * (own + down))
            run_ref[DOWN, rows, :] = run_ref[DOWN, rows, :] + power * (begin * own + down)
            run_ref[POWER, rows, :] = power * far
            run_ref[SLOPE, rows, :] = far * (slope + float(SPAN) * head) + up
        return carry

    lax.fori_loop(0, spans, near, 0)
    wait_all(fetch)
    lax.fori_loop(0, spans, across, 0)
    part(lambda m: run_ref[DOWN, at(m), :], lambda m: run_ref[SLOPE, at(m), :], keep_a_ref, send_a_ref)
    lags = [lag_ref[pl.ds(u * blocks, blocks), :] for u in range(SPAN)]
    factors = [run_ref[FACTOR, at(m), :] for m in range(modes)]
    plain = [lags[SPAN - 1]] * modes
    slope = [lags[SPAN - 1] * (SPAN - 1.0)] * modes
    for u in range(SPAN - 2, -1, -1):
        sloped = lags[u] * float(u)
        plain = [f * p + lags[u] for f, p in zip(factors, plain)]
        slope = [f * p + sloped for f, p in zip(factors, slope)]
    part(
        lambda m: factors[m] * run_ref[SUM0, at(m), :] + plain[m],
        lambda m: factors[m] * run_ref[SUM1, at(m), :] + slope[m],
        keep_b_ref,
        send_b_ref,
    )
    wait_all(stores)


def pair_body(
    core_ref, a_ref, a_other_ref, b_ref, b_other_ref, s_ref, s_other_ref, rate_ref, joined_ref,
    out_hbm, held_ref, sem,
    *, modes, length,
):
    groups, chips, rows = s_ref.shape[0], s_ref.shape[1], s_ref.shape[2]
    first = lane_is_first((rows, LANES), modes)
    low = core_ref[0] == 0

    def turn(value):
        return jnp.where(first, pltpu.roll(value, LANES - modes, 1), pltpu.roll(value, modes, 1))

    copies = []
    for group in range(groups):
        for chip in range(chips):
            def both(own_ref, other_ref):
                own, other = own_ref[group, chip], other_ref[group, chip]
                return jnp.where(low, own, other), jnp.where(low, other, own)

            (a0, a1), (b0, b1), (s0, s1) = both(a_ref, a_other_ref), both(b_ref, b_other_ref), both(s_ref, s_other_ref)
            rate = rate_ref[group, chip]
            far, factor = jnp.exp(-float(length) * rate), jnp.exp(-rate)
            later = turn(s1)
            held_ref[0, group, chip] = jnp.where(first, far * s0 + s1, s0 + far * s1)
            held_ref[1, group, chip] = jnp.where(
                first, a0 + far * (a1 + float(length) * later), far * (a0 + float(length) * turn(s0)) + a1
            )
            cross = s0 * later
            slope = pltpu.roll(cross + s0 * a1, modes, 1) + a0 * s1
            held_ref[2, group, chip] = b0 + b1 + factor * jnp.where(first, cross, slope)
        copies += start_all([
            pltpu.make_async_copy(held_ref.at[k, group], out_hbm.at[:, k * groups + group], sem.at[k, group])
            for k in range(3)
        ])
    wait_all(copies)


def join_weights(index, step, rate, length):
    run = 2**step
    upper = lax.rem(lax.div(index, run), 2) == 1
    offset = lax.rem(index, run)
    chunk = float(length) * rate
    ahead = jnp.where(upper, offset, run - 1 - offset).astype(jnp.float32)
    return upper, jnp.exp(-float(run) * chunk), jnp.exp(-ahead * chunk)


def join_body(index_ref, par_ref, total_ref, other_ref, *refs, step, length, modes, last):
    sends_later = lax.rem(lax.div(index_ref[0], 2 ** (step + 1)), 2) == 1
    held_ref = refs[0] if step else None
    next_ref, out_ref = refs[-2:]
    blocks = par_ref.shape[0] // modes // 2
    for m in range(modes):
        low, high = pl.ds(m * blocks, blocks), pl.ds((modes + m) * blocks, blocks)
        upper, far, near = join_weights(index_ref[0], step, by_mode(par_ref, m, blocks), length)
        x, y, ox, oy = total_ref[low, :], total_ref[high, :], other_ref[low, :], other_ref[high, :]
        head, tail = jnp.where(upper, near * ox, 0.0), jnp.where(upper, 0.0, near * oy)
        if held_ref is not None:
            head, tail = head + held_ref[low, :], tail + held_ref[high, :]
        out_ref[low, :] = head
        out_ref[high, :] = tail
        new_x, new_y = jnp.where(upper, far * ox + x, far * x + ox), jnp.where(upper, far * y + oy, far * oy + y)
        if last:
            next_ref[low, :] = jnp.where(sends_later, new_y, new_x)
        else:
            next_ref[low, :] = new_x
            next_ref[high, :] = new_y
    rest = pl.ds(2 * modes * blocks, blocks)
    next_ref[pl.ds(next_ref.shape[0] - blocks, blocks), :] = total_ref[rest, :] + other_ref[rest, :]


def local_body(par_ref, x_ref, b_ref, joined_ref, skip_hbm, y_hbm, z_hbm, skip_ref, out_ref, skip_sem, sem):
    fetch = pltpu.make_async_copy(skip_hbm, skip_ref, skip_sem)
    fetch.start()
    blocks = skip_ref.shape[0]
    modes = par_ref.shape[0] // blocks // 2
    spans = x_ref.shape[0] // blocks // SPAN
    pieces = sem.shape[1]
    part = spans // pieces
    factors, terms = [], []
    for m in range(modes):
        rate = by_mode(par_ref, m, blocks)
        factors.append(jnp.exp(-rate))
        terms.append(by_mode(par_ref, modes + m, blocks) * jnp.sqrt(rate))
    kernel = []
    for u in range(SPAN):
        kernel.append(tree(terms))
        terms = [t * f for t, f in zip(terms, factors)]
    fetch.wait()
    kernel[0] = kernel[0] + skip_ref[...]

    def step(span, carry):
        def at(r):
            return pl.ds(pl.multiple_of((span * SPAN + r) * blocks, blocks), blocks)

        x = [x_ref[at(r), :] for r in range(SPAN)]
        for r in range(SPAN):
            out_ref[0, at(r), :] = tree([kernel[u] * x[r - u] for u in range(r + 1)])
        b = [b_ref[at(r), :] for r in range(SPAN)]
        for r in range(SPAN):
            out_ref[1, at(r), :] = tree([kernel[u] * b[r + u] for u in range(SPAN - r)])
        return carry

    copies = []
    for p in range(pieces):
        lax.fori_loop(p * part, (p + 1) * part, step, 0)
        rows = pl.ds(p * part * SPAN * blocks, part * SPAN * blocks)
        copies += start_all([
            pltpu.make_async_copy(out_ref.at[k, rows], ref.at[rows], sem.at[k, p]) for k, ref in enumerate((y_hbm, z_hbm))
        ])
    wait_all(copies)


def lane_is_first(shape, modes):
    return lax.broadcasted_iota(jnp.int32, shape, 1) % (2 * modes) < modes


def scan_body(s_ref, rate_ref, done_hbm, out_ref, pack_ref, sem, *, modes, length):
    chunks, groups, rows = s_ref.shape[0], rate_ref.shape[0], rate_ref.shape[1]
    first = lane_is_first((rows, LANES), modes)
    zero = jnp.zeros((rows, LANES), jnp.float32)
    span = 2 * modes
    fold = LANES // span
    row = lax.broadcasted_iota(jnp.int32, (rows, LANES), 0) % fold
    column = lax.broadcasted_iota(jnp.int32, (rows, LANES), 1) // span
    for group in range(groups):
        alpha = jnp.exp(-float(length) * rate_ref[group])
        before, lead, total0, total1 = zero, zero, zero, zero
        heads = []
        for k in range(chunks):
            value = s_ref[k, group]
            later = pltpu.roll(value, LANES - modes, 1)
            heads.append(before)
            total0 += before * later
            total1 += (lead + before) * later
            lead = alpha * (lead + float(length) * before)
            before = alpha * before + value
        after, cross = zero, zero
        for k in reversed(range(chunks)):
            cross += jnp.where(first, heads[k], after) * s_ref[k, groups + group]
            after = alpha * after + s_ref[k, group]
        inner = tree([s_ref[k, 2 * groups + group] for k in range(chunks)])
        outer = jnp.where(first, total0, pltpu.roll(total1, modes, 1) + cross + pltpu.roll(cross, modes, 1))
        total = inner + jnp.exp(-rate_ref[group]) * outer
        packed = total
        for shift in range(1, fold):
            moved = pltpu.roll(total, LANES - shift * span, 1)
            moved = jnp.where(row >= shift, pltpu.roll(moved, shift, 0), pltpu.roll(moved, rows - fold + shift, 0))
            packed = jnp.where((row - column + fold) % fold == shift, moved, packed)
        for block in range(fold):
            for r in range(rows // fold):
                pack_ref[group * fold + block, pl.ds(r, 1), :] = packed[r * fold + block : r * fold + block + 1]
    wait_all(start_all([pltpu.make_async_copy(pack_ref, out_ref.at[k], sem.at[k]) for k in range(out_ref.shape[0])]))


def final_body(g_ref, residue_ref, decay_ref, gres_ref, gdec_ref, spread_ref):
    modes = residue_ref.shape[0]
    owners, blocks, rows = g_ref.shape[0], g_ref.shape[1], g_ref.shape[2]
    span = 2 * modes
    fold = LANES // span
    total = tree([g_ref[:, block] for block in range(blocks)]).reshape(owners * rows, LANES)
    for k in range(fold):
        moved = total if k == 0 else pltpu.roll(total, LANES - k * span, 1)
        spread_ref[pl.ds(k, owners * rows, stride=fold), :] = moved
    sums = spread_ref[...].T
    plain, slope = sums[:modes], sums[modes:span]
    decay = decay_ref[...]
    root = jnp.sqrt(decay)
    gres_ref[...] = root * plain
    gdec_ref[...] = residue_ref[...] * root * (0.5 * plain - decay * slope)


def settle_body(
    par_ref, held_ref, y_hbm, z_hbm, hs_hbm, bs_hbm,
    loc_ref,
    run_ref, snap_ref, sem,
):
    spans, blocks = hs_hbm.shape[0], y_hbm.shape[0] // hs_hbm.shape[0] // SPAN
    modes = hs_hbm.shape[1] // blocks
    pieces = sem.shape[0]
    part = spans // pieces
    fetch = []
    for p in range(pieces):
        copies = []
        for kind, (place, local, snaps, shift) in enumerate(((p, y_hbm, hs_hbm, 0), (pieces - 1 - p, z_hbm, bs_hbm, 1))):
            rows = pl.ds(place * part * SPAN * blocks, part * SPAN * blocks)
            copies.append(pltpu.make_async_copy(local.at[rows], loc_ref.at[kind, rows], sem.at[p, 2 * kind]))
            source, target = pl.ds(place * part + shift, part), pl.ds(place * part, part)
            copies.append(pltpu.make_async_copy(snaps.at[source], snap_ref.at[kind, target], sem.at[p, 2 * kind + 1]))
        fetch.append(start_all(copies))
    FACTOR, FAR, WEIGHT, HEAD, TAIL = range(5)
    for m in range(modes):
        rows = pl.ds(m * blocks, blocks)
        rate = by_mode(par_ref, m, blocks)
        factor = jnp.exp(-rate)
        run_ref[FACTOR, rows, :] = factor
        run_ref[FAR, rows, :] = jnp.exp(-float(SPAN) * rate)
        run_ref[WEIGHT, rows, :] = by_mode(par_ref, modes + m, blocks) * jnp.sqrt(rate) * factor
        run_ref[HEAD, rows, :] = held_ref[rows, :]
        run_ref[TAIL, rows, :] = held_ref[pl.ds((modes + m) * blocks, blocks), :]

    def finish(kind, span, run):
        terms, factors = [], []
        for m in range(modes):
            rows = pl.ds(m * blocks, blocks)
            state = run_ref[run, rows, :]
            terms.append(run_ref[WEIGHT, rows, :] * (snap_ref[kind, span, rows, :] + state))
            run_ref[run, rows, :] = state * run_ref[FAR, rows, :]
            factors.append(run_ref[FACTOR, rows, :])
        for k in range(SPAN):
            rows = position(span, k if kind == 0 else SPAN - 1 - k, blocks)
            loc_ref[kind, rows, :] = loc_ref[kind, rows, :] + tree(terms)
            if k < SPAN - 1:
                terms = [t * f for t, f in zip(terms, factors)]

    def both(span, carry):
        finish(0, span, HEAD)
        finish(1, spans - 1 - span, TAIL)
        return carry

    for p in range(pieces):
        wait_all(fetch[p])
        lax.fori_loop(p * part, (p + 1) * part, both, 0)


def out_body(
    index_ref, par_ref, loc_ref, total_ref, other_ref, gate_hbm, key_hbm, value_hbm, cot_hbm,
    mixed_hbm, ggate_hbm, gkey_hbm, gvalue_hbm, gskip_ref,
    run_ref, sum_ref, in_ref, out_ref, in_sem, out_sem,
    *, step,
):
    length, channels = gate_hbm.shape
    blocks = channels // LANES
    modes = par_ref.shape[0] // blocks // 2
    spans = length // SPAN
    pieces = in_sem.shape[0]
    part = spans // pieces
    depth = part * SPAN
    fetch = [
        start_all([
            pltpu.make_async_copy(ref.at[pl.ds(p * depth, depth)], in_ref.at[k, pl.ds(p * depth, depth)], in_sem.at[p, k])
            for k, ref in enumerate((gate_hbm, cot_hbm, value_hbm, key_hbm))
        ])
        for p in range(pieces)
    ]
    rest = pl.ds(modes * blocks, blocks)
    gskip_ref[...] = total_ref[rest, :] + other_ref[rest, :]
    FACTOR, FAR, STATE = range(3)
    for m in range(modes):
        rows = pl.ds(m * blocks, blocks)
        rate = by_mode(par_ref, m, blocks)
        _, _, near = join_weights(index_ref[0], step, rate, length)
        factor = jnp.exp(-rate)
        run_ref[FACTOR, rows, :] = factor
        run_ref[FAR, rows, :] = jnp.exp(-float(SPAN) * rate)
        weight = by_mode(par_ref, modes + m, blocks) * jnp.sqrt(rate) * factor
        run_ref[STATE, rows, :] = weight * (near * other_ref[rows, :])
    later = lax.rem(lax.div(index_ref[0], 2**step), 2) == 1
    kind, other_kind = jnp.where(later, 0, 1), jnp.where(later, 1, 0)

    def carry_in(span, carry):
        place = jnp.where(later, span, spans - 1 - span)
        terms, factors = [], []
        for m in range(modes):
            rows = pl.ds(m * blocks, blocks)
            terms.append(run_ref[STATE, rows, :])
            run_ref[STATE, rows, :] = terms[-1] * run_ref[FAR, rows, :]
            factors.append(run_ref[FACTOR, rows, :])
        for k in range(SPAN):
            rows = position(place, jnp.where(later, k, SPAN - 1 - k), blocks)
            sum_ref[kind, rows, :] = loc_ref[kind, rows, :] + tree(terms)
            sum_ref[other_kind, rows, :] = loc_ref[other_kind, rows, :]
            if k < SPAN - 1:
                terms = [t * f for t, f in zip(terms, factors)]
        return carry

    def finish(span, carry):
        rows = pl.ds(pl.multiple_of(span * SPAN, SPAN), SPAN)
        for block in range(blocks):
            lanes = pl.ds(block * LANES, LANES)
            for side in range(2):
                total = jnp.concatenate(
                    [
                        sum_ref[side, pl.ds((span * SPAN + half * ROWS) * blocks + block, ROWS, stride=blocks), :]
                        for half in range(SPAN // ROWS)
                    ],
                    axis=0,
                )
                for slot in (2 * side, 2 * side + 1):
                    value = in_ref[slot, rows, lanes].astype(jnp.float32) * total
                    out_ref[slot, rows, lanes] = value.astype(jnp.bfloat16)
        return carry

    lax.fori_loop(0, spans, carry_in, 0)
    stores = []
    for p in range(pieces):
        wait_all(fetch[p])
        lax.fori_loop(p * part, (p + 1) * part, finish, 0)
        rows = pl.ds(p * depth, depth)
        for slot, ref in enumerate((mixed_hbm, ggate_hbm, gkey_hbm, gvalue_hbm)):
            stores += start_all([pltpu.make_async_copy(out_ref.at[slot, rows], ref.at[rows], out_sem.at[p, slot])])
    wait_all(stores)


def on_device(gate_in, key_in, value_in, cotangent, skip, residue, decay):
    f32, bf16 = jnp.float32, jnp.bfloat16
    chips, cores = lax.axis_size("chip"), lax.axis_size("core")
    ctx = ("chip", "core")
    owners = chips * cores
    blocks = lax.axis_size("ch")
    length, channels = gate_in.shape
    filters, modes = residue.shape
    share = filters // owners
    groups = blocks * 2 * modes // LANES
    spans = length // SPAN
    pieces = 4
    place = lax.axis_index(ctx).astype(jnp.int32).reshape(1)
    core = lax.axis_index("core").astype(jnp.int32).reshape(1)

    def change(value):
        return lax.ppermute(value, "core", [(i, cores - 1 - i) for i in range(cores)])

    whole = (length, channels)
    signal = (length * blocks, LANES)
    heads_at, tails_at = (spans, modes * blocks, LANES), (spans + 1, modes * blocks, LANES)
    size = length * channels
    sums = pltpu.VMEM((groups * LANES, LANES), f32)
    dense = pltpu.VMEM((4, *whole), bf16)
    tile = (share, LANES)

    (sent,) = call(
        spread_body,
        [((blocks, 2 * modes, LANES), f32, HBM)],
        4,
        (0, 10**5),
        [pltpu.VMEM((2 * modes, LANES), f32), DMA((2,)), DMA((blocks,))],
    )([HBM] * 2, decay.T, residue.T)
    params = lax.all_to_all(sent, "ch", 0, 0, tiled=True).reshape(blocks * 2 * modes, LANES)

    x, b, sk, lag = call(
        product_body,
        [(signal, f32, VMEM)] * 2 + [((blocks, LANES), f32, VMEM), ((SPAN * blocks, LANES), f32, VMEM)],
        16,
        (8 * size, 16 * size),
        [dense, DMA((pieces, 4))],
    )([HBM] * 4, gate_in, key_in, value_in, cotangent)

    side = (groups, chips, *tile)
    total_at = ((2 * modes + 1) * blocks, LANES)
    part = spans // pieces
    total, head_states, tail_states, last_heads, last_tails = call(
        state_body,
        [(total_at, f32, VMEM), (heads_at, f32, HBM), (tails_at, f32, HBM)]
        + [((part, *heads_at[1:]), f32, VMEM), ((part + 1, *heads_at[1:]), f32, VMEM)],
        16,
        (64 * size, 16 * size),
        [pltpu.VMEM(heads_at, f32), pltpu.VMEM(tails_at, f32), DMA((2, pieces))],
    )([VMEM] * 4, params, x, b, sk)

    totals, held, others = [total], [], []
    steps = (owners - 1).bit_length()
    for step in range(steps):
        others.append(lax.ppermute(totals[-1], ctx, [(i, i ^ 2**step) for i in range(owners)]))
        if step == steps - 1:
            break
        last = step == steps - 2
        total, *held = call(
            functools.partial(join_body, step=step, length=length, modes=modes, last=last),
            [(((modes + 1) * blocks, LANES) if last else total_at, f32, VMEM), ((2 * modes * blocks, LANES), f32, VMEM)],
            8,
            (size, size),
        )([SMEM] + [VMEM] * (3 + len(held)), place, params, totals[-1], others[-1], *held)
        totals.append(total)

    y, z = call(
        local_body,
        [(signal, f32, HBM)] * 2,
        16,
        (40 * size, 16 * size),
        [pltpu.VMEM((blocks, LANES), f32), pltpu.VMEM((2, *signal), f32), DMA, DMA((2, pieces))],
    )([VMEM] * 4 + [HBM], params, x, b, totals[2], skip.reshape(blocks, LANES))

    head_states, tail_states, rates, side_rates, own_s, send_s, own_a, send_a, own_b, send_b = call(
        slope_body,
        [(heads_at, f32, HBM), (tails_at, f32, HBM), ((groups, *tile), f32, VMEM)] + [(side, f32, VMEM)] * 7,
        16,
        (100 * size, 16 * size),
        [pltpu.VMEM(heads_at, f32), pltpu.VMEM(tails_at, f32), pltpu.VMEM(heads_at, f32), pltpu.VMEM(heads_at, f32)]
        + [pltpu.VMEM((7, modes * blocks, LANES), f32), sums, pltpu.VMEM((owners, *tile), f32), sums, DMA((4,))],
        {8: 0, 9: 1},
    )(
        [SMEM] * 2 + [VMEM] * 6 + [HBM] * 2 + [VMEM] * 2,
        place, core, params, x, b, lag, totals[0], totals[1], head_states, tail_states, last_heads, last_tails,
    )

    (states,) = call(
        functools.partial(pair_body, modes=modes, length=length),
        [((chips, 3 * groups, *tile), f32, HBM)],
        8,
        (size, size),
        [pltpu.VMEM((3, *side), f32), DMA((3, groups))],
    )(
        [SMEM] + [VMEM] * 8,
        core, own_a, change(send_a), own_b, change(send_b), own_s, change(send_s), side_rates, totals[2],
    )
    states = lax.all_to_all(states, "chip", 0, 0, tiled=True)

    packed = (owners, blocks, share * 2 * modes // LANES, LANES)
    (grads,) = call(
        functools.partial(scan_body, modes=modes, length=cores * length),
        [(packed, f32, HBM)],
        8,
        (10**5, 10**6),
        [pltpu.VMEM(packed[1:], f32), DMA((owners,))],
    )([VMEM] * 2 + [HBM], states, rates, y)
    grads = lax.all_to_all(grads.reshape(owners * blocks, *packed[2:]), ("chip", "core", "ch"), 0, 0, tiled=True)

    (settled,) = call(
        settle_body,
        [((2, *signal), f32, VMEM)],
        16,
        (64 * size, 16 * size),
        [pltpu.VMEM((5, modes * blocks, LANES), f32), pltpu.VMEM((2, *heads_at), f32), DMA((pieces, 4))],
    )([VMEM] * 2 + [HBM] * 4, params, *held, y, z, head_states, tail_states)

    mixed, grad_gate, grad_key, grad_value, grad_skip = call(
        functools.partial(out_body, step=steps - 1),
        [(whole, bf16, HBM)] * 4 + [((blocks, LANES), f32, VMEM)],
        16,
        (32 * size, 16 * size),
        [pltpu.VMEM((3, modes * blocks, LANES), f32), pltpu.VMEM((2, *signal), f32), dense, dense]
        + [DMA((pieces, 4)), DMA((pieces, 4))],
    )(
        [SMEM] + [VMEM] * 4 + [HBM] * 4,
        place, params, settled, totals[3], others[3], gate_in, key_in, value_in, cotangent,
    )

    grad_residue, grad_log_decay = call(
        final_body, [((modes, filters), f32, VMEM)] * 2, 8, (10**5, 10**6), [pltpu.VMEM((LANES, LANES), f32)]
    )([VMEM] * 3, grads.reshape(packed), residue.T, decay.T)
    return (mixed, grad_gate, grad_key, grad_value, grad_skip.reshape(channels), grad_residue.T, grad_log_decay.T)


def solution(mesh):
    cores = 2
    shape = (mesh.shape["ctx"] // cores, cores, mesh.shape["ch"])
    split = jax.sharding.Mesh(mesh.devices.reshape(shape), ("chip", "core", "ch"))
    rows = P(("chip", "core"), "ch")
    specs = (rows, rows, rows, rows, P("ch"), P("ch", None), P("ch", None))
    return jax.shard_map(on_device, mesh=split, in_specs=specs, out_specs=specs, check_vma=False)
```

```python
import functools

import jax
import jax.numpy as jnp
from jax import lax
from jax.experimental import pallas as pl
from jax.experimental.pallas import tpu as pltpu
from jax.sharding import PartitionSpec as P

LANES = 128
ROWS = 8
SPAN = 16
VMEM = pl.BlockSpec(memory_space=pltpu.VMEM)
SMEM = pl.BlockSpec(memory_space=pltpu.SMEM)
HBM = pl.BlockSpec(memory_space=pltpu.HBM)
DMA = pltpu.SemaphoreType.DMA


def call(body, outs, limit_mib, cost, scratch=(), aliases=None):
    flops, moved = cost
    return lambda specs, *args: pl.pallas_call(
        body,
        out_shape=[pltpu.HBM(s, t) if w is HBM else jax.ShapeDtypeStruct(s, t) for s, t, w in outs],
        in_specs=list(specs),
        out_specs=[w for _, _, w in outs],
        scratch_shapes=list(scratch),
        input_output_aliases=aliases or {},
        compiler_params=pltpu.CompilerParams(vmem_limit_bytes=limit_mib * 2**20),
        cost_estimate=pl.CostEstimate(flops=flops, bytes_accessed=moved, transcendentals=0),
    )(*(pltpu.with_memory_space_constraint(a, pltpu.HBM) if w is HBM else a for w, a in zip(specs, args)))


def start_all(copies):
    for copy in copies:
        copy.start()
    return copies


def wait_all(copies):
    for copy in copies:
        copy.wait()


def spread_body(decay_ref, residue_ref, out_ref, held_ref, in_sem, out_sem):
    modes, blocks = decay_ref.shape[0], out_ref.shape[0]
    wait_all(
        start_all([
            pltpu.make_async_copy(ref, held_ref.at[pl.ds(k * modes, modes)], in_sem.at[k])
            for k, ref in enumerate((decay_ref, residue_ref))
        ])
    )
    wait_all(start_all([pltpu.make_async_copy(held_ref, out_ref.at[k], out_sem.at[k]) for k in range(blocks)]))


def tree(values):
    while len(values) > 1:
        odd = values[-1:] if len(values) % 2 else []
        values = [a + b for a, b in zip(values[::2], values[1::2])] + odd
    return values[0]


def turned(scratch_ref, group, owners):
    return scratch_ref[pl.ds(group * LANES, LANES), :].T.reshape(owners, LANES // owners, LANES)


def by_mode(ref, row, blocks):
    return ref[pl.ds(row, blocks, stride=ref.shape[0] // blocks), :]


def position(span, offset, blocks):
    return pl.ds(pl.multiple_of((span * SPAN + offset) * blocks, blocks), blocks)


def product_body(
    gate_hbm, key_hbm, value_hbm, cot_hbm,
    x_ref, b_ref, sk_ref, lag_ref,
    in_ref, sem,
):
    length, channels = gate_hbm.shape
    blocks = channels // LANES
    pieces = sem.shape[0]
    depth = length // pieces
    fetch = [
        start_all([
            pltpu.make_async_copy(ref.at[pl.ds(p * depth, depth)], in_ref.at[k, pl.ds(p * depth, depth)], sem.at[p, k])
            for k, ref in enumerate((gate_hbm, key_hbm, value_hbm, cot_hbm))
        ])
        for p in range(pieces)
    ]
    lag_ref[...] = jnp.zeros(lag_ref.shape, jnp.float32)

    def step(place, sums):
        rows = pl.ds(pl.multiple_of(place * SPAN, SPAN), SPAN)
        after = []
        for block in range(blocks):
            lanes = pl.ds(block * LANES, LANES)
            gate, key, value, cot = (in_ref[k, rows, lanes].astype(jnp.float32) for k in range(4))
            x, b = key * value, cot * gate
            for part in range(SPAN // ROWS):
                target = pl.ds((place * SPAN + part * ROWS) * blocks + block, ROWS, stride=blocks)
                x_ref[target, :] = x[part * ROWS : (part + 1) * ROWS]
                b_ref[target, :] = b[part * ROWS : (part + 1) * ROWS]
            both = x * b
            after.append(sums[block] + tree([both[k * ROWS : (k + 1) * ROWS] for k in range(SPAN // ROWS)]))
        return tuple(after)

    def lags(span, carry):
        x = [x_ref[position(span, r, blocks), :] for r in range(SPAN)]
        b = [b_ref[position(span, r, blocks), :] for r in range(SPAN)]
        for u in range(SPAN):
            rows = pl.ds(u * blocks, blocks)
            lag_ref[rows, :] = lag_ref[rows, :] + tree([b[r + u] * x[r] for r in range(SPAN - u)])
        return carry

    sums = tuple(jnp.zeros((ROWS, LANES), jnp.float32) for _ in range(blocks))
    for p in range(pieces):
        wait_all(fetch[p])
        sums = lax.fori_loop(p * depth // SPAN, (p + 1) * depth // SPAN, step, sums)
        lax.fori_loop(p * depth // SPAN, (p + 1) * depth // SPAN, lags, 0)
    for block in range(blocks):
        sk_ref[pl.ds(block, 1), :] = jnp.sum(sums[block], axis=0, keepdims=True)


def part_slices(core, turned_ref, keep_ref, send_ref):
    for chip in range(keep_ref.shape[0]):
        keep_ref[chip] = turned_ref[2 * chip + core]
        send_ref[chip] = turned_ref[2 * chip + 1 - core]


def state_body(par_ref, x_ref, b_ref, sk_ref, total_ref, hs_hbm, bs_hbm, hs_last_ref, bs_last_ref, hs_ref, bs_ref, sem):
    spans = hs_ref.shape[0]
    blocks = sk_ref.shape[0]
    modes = par_ref.shape[0] // blocks // 2
    part = hs_last_ref.shape[0]
    pieces = spans // part
    factor = [jnp.exp(-by_mode(par_ref, m, blocks)) for m in range(modes)]

    def step(span, carry, last):
        ups, downs = carry
        mirror = spans - 1 - span
        heads, tails, first = (hs_last_ref, bs_last_ref, spans - part) if last else (hs_ref, bs_ref, 0)
        for m in range(modes):
            heads[span - first, pl.ds(m * blocks, blocks), :] = ups[m]
            tails[mirror + 1, pl.ds(m * blocks, blocks), :] = downs[m]
        for r in range(SPAN):
            x = x_ref[position(span, r, blocks), :]
            b = b_ref[position(mirror, SPAN - 1 - r, blocks), :]
            ups = tuple(f * u + x for f, u in zip(factor, ups))
            downs = tuple(f * d + b for f, d in zip(factor, downs))
        return ups, downs

    zero = tuple(jnp.zeros((blocks, LANES), jnp.float32) for _ in range(modes))
    ups, downs = zero, zero
    copies = []
    for p in range(pieces):
        last = p == pieces - 1
        ups, downs = lax.fori_loop(p * part, (p + 1) * part, functools.partial(step, last=last), (ups, downs))
        if last:
            break
        here, there = pl.ds(p * part, part), pl.ds((pieces - 1 - p) * part + 1, part)
        copies += start_all([
            pltpu.make_async_copy(hs_ref.at[here], hs_hbm.at[here], sem.at[0, p]),
            pltpu.make_async_copy(bs_ref.at[there], bs_hbm.at[there], sem.at[1, p]),
        ])
    for m in range(modes):
        bs_last_ref[0, pl.ds(m * blocks, blocks), :] = downs[m]
        total_ref[pl.ds(m * blocks, blocks), :] = ups[m]
        total_ref[pl.ds((modes + m) * blocks, blocks), :] = downs[m]
    total_ref[pl.ds(2 * modes * blocks, blocks), :] = sk_ref[...]
    wait_all(copies)


def layout_body(
    index_ref, core_ref, par_ref, total_ref,
    rate_ref, side_rate_ref, keep_ref, send_ref,
    sums_ref, turn_ref, rates_ref,
    *, modes,
):
    owners, share = turn_ref.shape[0], turn_ref.shape[1]
    groups = sums_ref.shape[0] // LANES
    blocks = par_ref.shape[0] // modes // 2
    for m in range(modes):
        for kind in range(2):
            state = total_ref[pl.ds((kind * modes + m) * blocks, blocks), :]
            sums_ref[pl.ds(kind * modes + m, blocks, stride=2 * modes), :] = state
    for group in range(groups):
        turn_ref[...] = turned(sums_ref, group, owners)
        part_slices(core_ref[0], turn_ref, keep_ref.at[group], send_ref.at[group])
    for group in range(groups):
        for block in range(group * blocks // groups, (group + 1) * blocks // groups):
            decay = par_ref[pl.ds(block * 2 * modes, modes), :]
            rates_ref[pl.ds(block * 2 * modes, 2 * modes), :] = jnp.concatenate([decay, decay], axis=0)
        rates_ref[pl.ds(group * LANES, LANES), :] = rates_ref[pl.ds(group * LANES, LANES), :].T
        rate_ref[group] = rates_ref[pl.ds(pl.multiple_of(group * LANES + index_ref[0] * share, share), share), :]
        for chip in range(side_rate_ref.shape[1]):
            start = group * LANES + (2 * chip + core_ref[0]) * share
            side_rate_ref[group, chip] = rates_ref[pl.ds(pl.multiple_of(start, share), share), :]


def slope_body(
    core_ref, par_ref, x_ref, b_ref, lag_ref, done_ref, joined_ref, hs_in, bs_in, hs_last_ref, bs_last_ref,
    hs_hbm, bs_hbm, keep_a_ref, send_a_ref, keep_b_ref, send_b_ref,
    hs_ref, bs_ref, up_ref, down_ref, run_ref, sums_ref, turn_ref, snap_sem,
):
    owners = turn_ref.shape[0]
    groups = sums_ref.shape[0] // LANES
    spans = hs_ref.shape[0]
    blocks = lag_ref.shape[0] // SPAN
    modes = par_ref.shape[0] // blocks // 2
    part_spans = hs_last_ref.shape[0]
    rest = spans - part_spans
    heads, tails = pl.ds(0, rest), pl.ds(part_spans + 1, rest)
    fetch = start_all([
        pltpu.make_async_copy(hs_in.at[heads], hs_ref.at[heads], snap_sem.at[0]),
        pltpu.make_async_copy(bs_in.at[tails], bs_ref.at[tails], snap_sem.at[1]),
    ])
    stores = start_all([
        pltpu.make_async_copy(hs_last_ref, hs_hbm.at[pl.ds(rest, part_spans)], snap_sem.at[2]),
        pltpu.make_async_copy(bs_last_ref, bs_hbm.at[pl.ds(0, part_spans + 1)], snap_sem.at[3]),
    ])
    hs_ref[rest:] = hs_last_ref[...]
    bs_ref[: part_spans + 1] = bs_last_ref[...]
    zero = jnp.zeros((blocks, LANES), jnp.float32)
    SLOPE, SUM0, SUM1, DOWN, POWER, FACTOR, FAR = range(7)
    for m in range(modes):
        rate = by_mode(par_ref, m, blocks)
        rows = pl.ds(m * blocks, blocks)
        for kind in (SLOPE, SUM0, SUM1, DOWN):
            run_ref[kind, rows, :] = zero
        run_ref[POWER, rows, :] = zero + 1.0
        run_ref[FACTOR, rows, :] = jnp.exp(-rate)
        run_ref[FAR, rows, :] = jnp.exp(-float(SPAN) * rate)

    def part(first, second, keep_ref, send_ref):
        for m in range(modes):
            sums_ref[pl.ds(m, blocks, stride=2 * modes), :] = first(m)
            sums_ref[pl.ds(modes + m, blocks, stride=2 * modes), :] = second(m)
        for group in range(groups):
            turn_ref[...] = turned(sums_ref, group, owners)
            part_slices(core_ref[0], turn_ref, keep_ref.at[group], send_ref.at[group])

    def at(m):
        return pl.ds(m * blocks, blocks)

    def near(span, carry):
        late = [x_ref[position(span, r, blocks), :] * (SPAN - 1.0 - r) for r in range(SPAN - 1)]
        early = [b_ref[position(span, r, blocks), :] * float(r) for r in range(SPAN - 1, 0, -1)]
        factors = [run_ref[FACTOR, at(m), :] for m in range(modes)]
        for ref, terms in ((up_ref, late), (down_ref, early)):
            sums = [terms[0]] * modes
            for term in terms[1:]:
                sums = [f * s + term for f, s in zip(factors, sums)]
            for m in range(modes):
                ref[span, at(m), :] = factors[m] * sums[m]
        return carry

    def across(span, carry):
        begin = (span * SPAN).astype(jnp.float32)
        for m in range(modes):
            rows = at(m)
            far = run_ref[FAR, rows, :]
            up, down = up_ref[span, rows, :], down_ref[span, rows, :]
            head = hs_ref[span, rows, :]
            own = bs_ref[span, rows, :] - far * bs_ref[span + 1, rows, :]
            slope, power = run_ref[SLOPE, rows, :], run_ref[POWER, rows, :]
            run_ref[SUM0, rows, :] = run_ref[SUM0, rows, :] + head * own
            run_ref[SUM1, rows, :] = run_ref[SUM1, rows, :] + (slope * own + head * (own + down))
            run_ref[DOWN, rows, :] = run_ref[DOWN, rows, :] + power * (begin * own + down)
            run_ref[POWER, rows, :] = power * far
            run_ref[SLOPE, rows, :] = far * (slope + float(SPAN) * head) + up
        return carry

    lax.fori_loop(0, spans, near, 0)
    wait_all(fetch)
    lax.fori_loop(0, spans, across, 0)
    part(lambda m: run_ref[DOWN, at(m), :], lambda m: run_ref[SLOPE, at(m), :], keep_a_ref, send_a_ref)
    lags = [lag_ref[pl.ds(u * blocks, blocks), :] for u in range(SPAN)]
    factors = [run_ref[FACTOR, at(m), :] for m in range(modes)]
    plain = [lags[SPAN - 1]] * modes
    slope = [lags[SPAN - 1] * (SPAN - 1.0)] * modes
    for u in range(SPAN - 2, -1, -1):
        sloped = lags[u] * float(u)
        plain = [f * p + lags[u] for f, p in zip(factors, plain)]
        slope = [f * p + sloped for f, p in zip(factors, slope)]
    part(
        lambda m: factors[m] * run_ref[SUM0, at(m), :] + plain[m],
        lambda m: factors[m] * run_ref[SUM1, at(m), :] + slope[m],
        keep_b_ref,
        send_b_ref,
    )
    wait_all(stores)


def pair_body(
    core_ref, a_ref, a_other_ref, b_ref, b_other_ref, s_ref, s_other_ref, rate_ref, joined_ref,
    out_hbm, held_ref, sem,
    *, modes, length,
):
    groups, chips, rows = s_ref.shape[0], s_ref.shape[1], s_ref.shape[2]
    first = lane_is_first((rows, LANES), modes)
    low = core_ref[0] == 0

    def turn(value):
        return jnp.where(first, pltpu.roll(value, LANES - modes, 1), pltpu.roll(value, modes, 1))

    copies = []
    for group in range(groups):
        for chip in range(chips):
            def both(own_ref, other_ref):
                own, other = own_ref[group, chip], other_ref[group, chip]
                return jnp.where(low, own, other), jnp.where(low, other, own)

            (a0, a1), (b0, b1), (s0, s1) = both(a_ref, a_other_ref), both(b_ref, b_other_ref), both(s_ref, s_other_ref)
            rate = rate_ref[group, chip]
            far, factor = jnp.exp(-float(length) * rate), jnp.exp(-rate)
            later = turn(s1)
            held_ref[0, group, chip] = jnp.where(first, far * s0 + s1, s0 + far * s1)
            held_ref[1, group, chip] = jnp.where(
                first, a0 + far * (a1 + float(length) * later), far * (a0 + float(length) * turn(s0)) + a1
            )
            cross = s0 * later
            slope = pltpu.roll(cross + s0 * a1, modes, 1) + a0 * s1
            held_ref[2, group, chip] = b0 + b1 + factor * jnp.where(first, cross, slope)
        copies += start_all([
            pltpu.make_async_copy(held_ref.at[k, group], out_hbm.at[:, k * groups + group], sem.at[k, group])
            for k in range(3)
        ])
    wait_all(copies)


def join_weights(index, step, rate, length):
    run = 2**step
    upper = lax.rem(lax.div(index, run), 2) == 1
    offset = lax.rem(index, run)
    chunk = float(length) * rate
    ahead = jnp.where(upper, offset, run - 1 - offset).astype(jnp.float32)
    return upper, jnp.exp(-float(run) * chunk), jnp.exp(-ahead * chunk)


def join_body(index_ref, par_ref, total_ref, other_ref, *refs, step, length, modes, last):
    sends_later = lax.rem(lax.div(index_ref[0], 2 ** (step + 1)), 2) == 1
    held_ref = refs[0] if step else None
    next_ref, out_ref = refs[-2:]
    blocks = par_ref.shape[0] // modes // 2
    for m in range(modes):
        low, high = pl.ds(m * blocks, blocks), pl.ds((modes + m) * blocks, blocks)
        upper, far, near = join_weights(index_ref[0], step, by_mode(par_ref, m, blocks), length)
        x, y, ox, oy = total_ref[low, :], total_ref[high, :], other_ref[low, :], other_ref[high, :]
        head, tail = jnp.where(upper, near * ox, 0.0), jnp.where(upper, 0.0, near * oy)
        if held_ref is not None:
            head, tail = head + held_ref[low, :], tail + held_ref[high, :]
        out_ref[low, :] = head
        out_ref[high, :] = tail
        new_x, new_y = jnp.where(upper, far * ox + x, far * x + ox), jnp.where(upper, far * y + oy, far * oy + y)
        if last:
            next_ref[low, :] = jnp.where(sends_later, new_y, new_x)
        else:
            next_ref[low, :] = new_x
            next_ref[high, :] = new_y
    rest = pl.ds(2 * modes * blocks, blocks)
    next_ref[pl.ds(next_ref.shape[0] - blocks, blocks), :] = total_ref[rest, :] + other_ref[rest, :]


def local_body(par_ref, x_ref, b_ref, joined_ref, skip_hbm, y_hbm, z_hbm, skip_ref, out_ref, skip_sem, sem):
    fetch = pltpu.make_async_copy(skip_hbm, skip_ref, skip_sem)
    fetch.start()
    blocks = skip_ref.shape[0]
    modes = par_ref.shape[0] // blocks // 2
    spans = x_ref.shape[0] // blocks // SPAN
    pieces = sem.shape[1]
    part = spans // pieces
    factors, terms = [], []
    for m in range(modes):
        rate = by_mode(par_ref, m, blocks)
        factors.append(jnp.exp(-rate))
        terms.append(by_mode(par_ref, modes + m, blocks) * jnp.sqrt(rate))
    kernel = []
    for u in range(SPAN):
        kernel.append(tree(terms))
        terms = [t * f for t, f in zip(terms, factors)]
    fetch.wait()
    kernel[0] = kernel[0] + skip_ref[...]

    def step(span, carry):
        def at(r):
            return pl.ds(pl.multiple_of((span * SPAN + r) * blocks, blocks), blocks)

        x = [x_ref[at(r), :] for r in range(SPAN)]
        for r in range(SPAN):
            out_ref[0, at(r), :] = tree([kernel[u] * x[r - u] for u in range(r + 1)])
        b = [b_ref[at(r), :] for r in range(SPAN)]
        for r in range(SPAN):
            out_ref[1, at(r), :] = tree([kernel[u] * b[r + u] for u in range(SPAN - r)])
        return carry

    copies = []
    for p in range(pieces):
        lax.fori_loop(p * part, (p + 1) * part, step, 0)
        rows = pl.ds(p * part * SPAN * blocks, part * SPAN * blocks)
        copies += start_all([
            pltpu.make_async_copy(out_ref.at[k, rows], ref.at[rows], sem.at[k, p]) for k, ref in enumerate((y_hbm, z_hbm))
        ])
    wait_all(copies)


def lane_is_first(shape, modes):
    return lax.broadcasted_iota(jnp.int32, shape, 1) % (2 * modes) < modes


def scan_body(s_ref, rate_ref, done_hbm, out_ref, pack_ref, sem, *, modes, length):
    chunks, groups, rows = s_ref.shape[0], rate_ref.shape[0], rate_ref.shape[1]
    first = lane_is_first((rows, LANES), modes)
    zero = jnp.zeros((rows, LANES), jnp.float32)
    span = 2 * modes
    fold = LANES // span
    row = lax.broadcasted_iota(jnp.int32, (rows, LANES), 0) % fold
    column = lax.broadcasted_iota(jnp.int32, (rows, LANES), 1) // span
    for group in range(groups):
        alpha = jnp.exp(-float(length) * rate_ref[group])
        before, lead, total0, total1 = zero, zero, zero, zero
        heads = []
        for k in range(chunks):
            value = s_ref[k, group]
            later = pltpu.roll(value, LANES - modes, 1)
            heads.append(before)
            total0 += before * later
            total1 += (lead + before) * later
            lead = alpha * (lead + float(length) * before)
            before = alpha * before + value
        after, cross = zero, zero
        for k in reversed(range(chunks)):
            cross += jnp.where(first, heads[k], after) * s_ref[k, groups + group]
            after = alpha * after + s_ref[k, group]
        inner = tree([s_ref[k, 2 * groups + group] for k in range(chunks)])
        outer = jnp.where(first, total0, pltpu.roll(total1, modes, 1) + cross + pltpu.roll(cross, modes, 1))
        total = inner + jnp.exp(-rate_ref[group]) * outer
        packed = total
        for shift in range(1, fold):
            moved = pltpu.roll(total, LANES - shift * span, 1)
            moved = jnp.where(row >= shift, pltpu.roll(moved, shift, 0), pltpu.roll(moved, rows - fold + shift, 0))
            packed = jnp.where((row - column + fold) % fold == shift, moved, packed)
        for block in range(fold):
            for r in range(rows // fold):
                pack_ref[group * fold + block, pl.ds(r, 1), :] = packed[r * fold + block : r * fold + block + 1]
    wait_all(start_all([pltpu.make_async_copy(pack_ref, out_ref.at[k], sem.at[k]) for k in range(out_ref.shape[0])]))


def final_body(g_ref, residue_ref, decay_ref, gres_ref, gdec_ref, spread_ref):
    modes = residue_ref.shape[0]
    owners, blocks, rows = g_ref.shape[0], g_ref.shape[1], g_ref.shape[2]
    span = 2 * modes
    fold = LANES // span
    total = tree([g_ref[:, block] for block in range(blocks)]).reshape(owners * rows, LANES)
    for k in range(fold):
        moved = total if k == 0 else pltpu.roll(total, LANES - k * span, 1)
        spread_ref[pl.ds(k, owners * rows, stride=fold), :] = moved
    sums = spread_ref[...].T
    plain, slope = sums[:modes], sums[modes:span]
    decay = decay_ref[...]
    root = jnp.sqrt(decay)
    gres_ref[...] = root * plain
    gdec_ref[...] = residue_ref[...] * root * (0.5 * plain - decay * slope)


def settle_body(
    par_ref, held_ref, y_hbm, z_hbm, hs_hbm, bs_hbm,
    loc_ref,
    run_ref, snap_ref, sem,
):
    spans, blocks = hs_hbm.shape[0], y_hbm.shape[0] // hs_hbm.shape[0] // SPAN
    modes = hs_hbm.shape[1] // blocks
    pieces = sem.shape[0]
    part = spans // pieces
    fetch = []
    for p in range(pieces):
        copies = []
        for kind, (place, local, snaps, shift) in enumerate(((p, y_hbm, hs_hbm, 0), (pieces - 1 - p, z_hbm, bs_hbm, 1))):
            rows = pl.ds(place * part * SPAN * blocks, part * SPAN * blocks)
            copies.append(pltpu.make_async_copy(local.at[rows], loc_ref.at[kind, rows], sem.at[p, 2 * kind]))
            source, target = pl.ds(place * part + shift, part), pl.ds(place * part, part)
            copies.append(pltpu.make_async_copy(snaps.at[source], snap_ref.at[kind, target], sem.at[p, 2 * kind + 1]))
        fetch.append(start_all(copies))
    FACTOR, FAR, WEIGHT, HEAD, TAIL = range(5)
    for m in range(modes):
        rows = pl.ds(m * blocks, blocks)
        rate = by_mode(par_ref, m, blocks)
        factor = jnp.exp(-rate)
        run_ref[FACTOR, rows, :] = factor
        run_ref[FAR, rows, :] = jnp.exp(-float(SPAN) * rate)
        run_ref[WEIGHT, rows, :] = by_mode(par_ref, modes + m, blocks) * jnp.sqrt(rate) * factor
        run_ref[HEAD, rows, :] = held_ref[rows, :]
        run_ref[TAIL, rows, :] = held_ref[pl.ds((modes + m) * blocks, blocks), :]

    def finish(kind, span, run):
        terms, factors = [], []
        for m in range(modes):
            rows = pl.ds(m * blocks, blocks)
            state = run_ref[run, rows, :]
            terms.append(run_ref[WEIGHT, rows, :] * (snap_ref[kind, span, rows, :] + state))
            run_ref[run, rows, :] = state * run_ref[FAR, rows, :]
            factors.append(run_ref[FACTOR, rows, :])
        for k in range(SPAN):
            rows = position(span, k if kind == 0 else SPAN - 1 - k, blocks)
            loc_ref[kind, rows, :] = loc_ref[kind, rows, :] + tree(terms)
            if k < SPAN - 1:
                terms = [t * f for t, f in zip(terms, factors)]

    def both(span, carry):
        finish(0, span, HEAD)
        finish(1, spans - 1 - span, TAIL)
        return carry

    for p in range(pieces):
        wait_all(fetch[p])
        lax.fori_loop(p * part, (p + 1) * part, both, 0)


def out_body(
    index_ref, par_ref, loc_ref, total_ref, other_ref, gate_hbm, key_hbm, value_hbm, cot_hbm,
    mixed_hbm, ggate_hbm, gkey_hbm, gvalue_hbm, gskip_ref,
    run_ref, sum_ref, in_ref, out_ref, in_sem, out_sem,
    *, step,
):
    length, channels = gate_hbm.shape
    blocks = channels // LANES
    modes = par_ref.shape[0] // blocks // 2
    spans = length // SPAN
    pieces = in_sem.shape[0]
    part = spans // pieces
    depth = part * SPAN
    fetch = [
        start_all([
            pltpu.make_async_copy(ref.at[pl.ds(p * depth, depth)], in_ref.at[k, pl.ds(p * depth, depth)], in_sem.at[p, k])
            for k, ref in enumerate((gate_hbm, cot_hbm, value_hbm, key_hbm))
        ])
        for p in range(pieces)
    ]
    rest = pl.ds(modes * blocks, blocks)
    gskip_ref[...] = total_ref[rest, :] + other_ref[rest, :]
    FACTOR, FAR, STATE = range(3)
    for m in range(modes):
        rows = pl.ds(m * blocks, blocks)
        rate = by_mode(par_ref, m, blocks)
        _, _, near = join_weights(index_ref[0], step, rate, length)
        factor = jnp.exp(-rate)
        run_ref[FACTOR, rows, :] = factor
        run_ref[FAR, rows, :] = jnp.exp(-float(SPAN) * rate)
        weight = by_mode(par_ref, modes + m, blocks) * jnp.sqrt(rate) * factor
        run_ref[STATE, rows, :] = weight * (near * other_ref[rows, :])
    later = lax.rem(lax.div(index_ref[0], 2**step), 2) == 1
    kind, other_kind = jnp.where(later, 0, 1), jnp.where(later, 1, 0)

    def carry_in(span, carry):
        place = jnp.where(later, span, spans - 1 - span)
        terms, factors = [], []
        for m in range(modes):
            rows = pl.ds(m * blocks, blocks)
            terms.append(run_ref[STATE, rows, :])
            run_ref[STATE, rows, :] = terms[-1] * run_ref[FAR, rows, :]
            factors.append(run_ref[FACTOR, rows, :])
        for k in range(SPAN):
            rows = position(place, jnp.where(later, k, SPAN - 1 - k), blocks)
            sum_ref[kind, rows, :] = loc_ref[kind, rows, :] + tree(terms)
            sum_ref[other_kind, rows, :] = loc_ref[other_kind, rows, :]
            if k < SPAN - 1:
                terms = [t * f for t, f in zip(terms, factors)]
        return carry

    def finish(span, carry):
        rows = pl.ds(pl.multiple_of(span * SPAN, SPAN), SPAN)
        for block in range(blocks):
            lanes = pl.ds(block * LANES, LANES)
            for side in range(2):
                total = jnp.concatenate(
                    [
                        sum_ref[side, pl.ds((span * SPAN + half * ROWS) * blocks + block, ROWS, stride=blocks), :]
                        for half in range(SPAN // ROWS)
                    ],
                    axis=0,
                )
                for slot in (2 * side, 2 * side + 1):
                    value = in_ref[slot, rows, lanes].astype(jnp.float32) * total
                    out_ref[slot, rows, lanes] = value.astype(jnp.bfloat16)
        return carry

    lax.fori_loop(0, spans, carry_in, 0)
    stores = []
    for p in range(pieces):
        wait_all(fetch[p])
        lax.fori_loop(p * part, (p + 1) * part, finish, 0)
        rows = pl.ds(p * depth, depth)
        for slot, ref in enumerate((mixed_hbm, ggate_hbm, gkey_hbm, gvalue_hbm)):
            stores += start_all([pltpu.make_async_copy(out_ref.at[slot, rows], ref.at[rows], out_sem.at[p, slot])])
    wait_all(stores)


def on_device(gate_in, key_in, value_in, cotangent, skip, residue, decay):
    f32, bf16 = jnp.float32, jnp.bfloat16
    chips, cores = lax.axis_size("chip"), lax.axis_size("core")
    ctx = ("chip", "core")
    owners = chips * cores
    blocks = lax.axis_size("ch")
    length, channels = gate_in.shape
    filters, modes = residue.shape
    share = filters // owners
    groups = blocks * 2 * modes // LANES
    spans = length // SPAN
    pieces = 4
    place = lax.axis_index(ctx).astype(jnp.int32).reshape(1)
    core = lax.axis_index("core").astype(jnp.int32).reshape(1)

    def change(value):
        return lax.ppermute(value, "core", [(i, cores - 1 - i) for i in range(cores)])

    whole = (length, channels)
    signal = (length * blocks, LANES)
    heads_at, tails_at = (spans, modes * blocks, LANES), (spans + 1, modes * blocks, LANES)
    size = length * channels
    sums = pltpu.VMEM((groups * LANES, LANES), f32)
    dense = pltpu.VMEM((4, *whole), bf16)
    tile = (share, LANES)

    (sent,) = call(
        spread_body,
        [((blocks, 2 * modes, LANES), f32, HBM)],
        4,
        (0, 10**5),
        [pltpu.VMEM((2 * modes, LANES), f32), DMA((2,)), DMA((blocks,))],
    )([HBM] * 2, decay.T, residue.T)
    params = lax.all_to_all(sent, "ch", 0, 0, tiled=True).reshape(blocks * 2 * modes, LANES)

    x, b, sk, lag = call(
        product_body,
        [(signal, f32, VMEM)] * 2 + [((blocks, LANES), f32, VMEM), ((SPAN * blocks, LANES), f32, VMEM)],
        16,
        (8 * size, 16 * size),
        [dense, DMA((pieces, 4))],
    )([HBM] * 4, gate_in, key_in, value_in, cotangent)

    side = (groups, chips, *tile)
    total_at = ((2 * modes + 1) * blocks, LANES)
    part = spans // pieces
    total, head_states, tail_states, last_heads, last_tails = call(
        state_body,
        [(total_at, f32, VMEM), (heads_at, f32, HBM), (tails_at, f32, HBM)]
        + [((part, *heads_at[1:]), f32, VMEM), ((part + 1, *heads_at[1:]), f32, VMEM)],
        16,
        (64 * size, 16 * size),
        [pltpu.VMEM(heads_at, f32), pltpu.VMEM(tails_at, f32), DMA((2, pieces))],
    )([VMEM] * 4, params, x, b, sk)

    rates, side_rates, own_s, send_s = call(
        functools.partial(layout_body, modes=modes),
        [((groups, *tile), f32, VMEM)] + [(side, f32, VMEM)] * 3,
        8,
        (size, size),
        [sums, pltpu.VMEM((owners, *tile), f32), sums],
    )([SMEM] * 2 + [VMEM] * 2, place, core, params, total)

    totals, held, others = [total], [], []
    steps = (owners - 1).bit_length()
    for step in range(steps):
        others.append(lax.ppermute(totals[-1], ctx, [(i, i ^ 2**step) for i in range(owners)]))
        if step == steps - 1:
            break
        last = step == steps - 2
        total, *held = call(
            functools.partial(join_body, step=step, length=length, modes=modes, last=last),
            [(((modes + 1) * blocks, LANES) if last else total_at, f32, VMEM), ((2 * modes * blocks, LANES), f32, VMEM)],
            8,
            (size, size),
        )([SMEM] + [VMEM] * (3 + len(held) + (step == 0)), place, params, totals[-1], others[-1], *held, *[side_rates] * (step == 0))
        totals.append(total)

    y, z = call(
        local_body,
        [(signal, f32, HBM)] * 2,
        16,
        (40 * size, 16 * size),
        [pltpu.VMEM((blocks, LANES), f32), pltpu.VMEM((2, *signal), f32), DMA, DMA((2, pieces))],
    )([VMEM] * 4 + [HBM], params, x, b, totals[2], skip.reshape(blocks, LANES))

    head_states, tail_states, own_a, send_a, own_b, send_b = call(
        slope_body,
        [(heads_at, f32, HBM), (tails_at, f32, HBM)] + [(side, f32, VMEM)] * 4,
        16,
        (100 * size, 16 * size),
        [pltpu.VMEM(heads_at, f32), pltpu.VMEM(tails_at, f32), pltpu.VMEM(heads_at, f32), pltpu.VMEM(heads_at, f32)]
        + [pltpu.VMEM((7, modes * blocks, LANES), f32), sums, pltpu.VMEM((owners, *tile), f32), DMA((4,))],
        {7: 0, 8: 1},
    )(
        [SMEM] + [VMEM] * 6 + [HBM] * 2 + [VMEM] * 2,
        core, params, x, b, lag, side_rates, totals[1], head_states, tail_states, last_heads, last_tails,
    )

    (states,) = call(
        functools.partial(pair_body, modes=modes, length=length),
        [((chips, 3 * groups, *tile), f32, HBM)],
        8,
        (size, size),
        [pltpu.VMEM((3, *side), f32), DMA((3, groups))],
    )(
        [SMEM] + [VMEM] * 8,
        core, own_a, change(send_a), own_b, change(send_b), own_s, change(send_s), side_rates, totals[2],
    )
    states = lax.all_to_all(states, "chip", 0, 0, tiled=True)

    packed = (owners, blocks, share * 2 * modes // LANES, LANES)
    (grads,) = call(
        functools.partial(scan_body, modes=modes, length=cores * length),
        [(packed, f32, HBM)],
        8,
        (10**5, 10**6),
        [pltpu.VMEM(packed[1:], f32), DMA((owners,))],
    )([VMEM] * 2 + [HBM], states, rates, y)
    grads = lax.all_to_all(grads.reshape(owners * blocks, *packed[2:]), ("chip", "core", "ch"), 0, 0, tiled=True)

    (settled,) = call(
        settle_body,
        [((2, *signal), f32, VMEM)],
        16,
        (64 * size, 16 * size),
        [pltpu.VMEM((5, modes * blocks, LANES), f32), pltpu.VMEM((2, *heads_at), f32), DMA((pieces, 4))],
    )([VMEM] * 2 + [HBM] * 4, params, *held, y, z, head_states, tail_states)

    mixed, grad_gate, grad_key, grad_value, grad_skip = call(
        functools.partial(out_body, step=steps - 1),
        [(whole, bf16, HBM)] * 4 + [((blocks, LANES), f32, VMEM)],
        16,
        (32 * size, 16 * size),
        [pltpu.VMEM((3, modes * blocks, LANES), f32), pltpu.VMEM((2, *signal), f32), dense, dense]
        + [DMA((pieces, 4)), DMA((pieces, 4))],
    )(
        [SMEM] + [VMEM] * 4 + [HBM] * 4,
        place, params, settled, totals[3], others[3], gate_in, key_in, value_in, cotangent,
    )

    grad_residue, grad_log_decay = call(
        final_body, [((modes, filters), f32, VMEM)] * 2, 8, (10**5, 10**6), [pltpu.VMEM((LANES, LANES), f32)]
    )([VMEM] * 3, grads.reshape(packed), residue.T, decay.T)
    return (mixed, grad_gate, grad_key, grad_value, grad_skip.reshape(channels), grad_residue.T, grad_log_decay.T)


def solution(mesh):
    cores = 2
    shape = (mesh.shape["ctx"] // cores, cores, mesh.shape["ch"])
    split = jax.sharding.Mesh(mesh.devices.reshape(shape), ("chip", "core", "ch"))
    rows = P(("chip", "core"), "ch")
    specs = (rows, rows, rows, rows, P("ch"), P("ch", None), P("ch", None))
    return jax.shard_map(on_device, mesh=split, in_specs=specs, out_specs=specs, check_vma=False)
```
